128 devices in a mesh: mx: 8 (over z_hi, x), my: 16 (over y, z_lo, core).
Axes of the slice: x: 4, y: 4, z: 4 (z_hi: 2, z_lo: 2; z = z_hi * 2 + z_lo), core: 2. Of those that a mesh axis runs over, the one named last changes fastest.
Arguments:
- slab: float32 [192, 192, 6400], P('mx', 'my'), may hold values from -40 to 40
- basis_x: float32 [192, 60], replicated, may hold values from -0.4375 to 0.4375
- basis_y: float32 [192, 60], replicated, may hold values from -0.4375 to 0.4375
Outputs:
- gram_x: float32 [192, 192], replicated
- gram_y: float32 [192, 192], replicated
- core: float32 [60, 60, 6400], P(None, None, ('mx', 'my'))
The draws below stay inside these ranges and needn't reach their ends.
All inputs are finite; a program needn't handle non-finite values.
Results may differ from the reference program's by a relative error of at most 0.000075.
Values sent between devices are 32-bit elements; how exact they have to be, the bound alone decides.
A program may use at most 192 MiB of HBM per device.

```python
import jax
import jax.numpy as jnp
from jax import lax

MIDX = 192
MIDY = 192
RANK = 60
COLS = 6400


def draw_slab(key, part):
    key = jax.random.fold_in(key, 11)
    keys = jax.random.split(key, 5)
    scale_a = jax.random.truncated_normal(keys[0], -3.0, 3.0, (MIDX, 1, 1), jnp.float32)
    scale_b = jax.random.truncated_normal(keys[1], -3.0, 3.0, (1, MIDY, 1), jnp.float32)
    shared_y = jax.random.truncated_normal(keys[2], -3.0, 3.0, (1, MIDY, COLS), jnp.float32)
    shared_x = jax.random.truncated_normal(keys[3], -3.0, 3.0, (MIDX, 1, COLS), jnp.float32)
    noise = jax.random.truncated_normal(keys[4], -4.0, 4.0, (MIDX, MIDY, COLS), jnp.float32)
    return 0.6 * scale_a * shared_y + 0.6 * scale_b * shared_x + noise


def gaussian(own_key, shape, scale, reach, kind=jnp.bfloat16):
    array = jax.random.normal(own_key, shape, jnp.float32) * scale
    return jnp.minimum(jnp.maximum(array, -reach), reach).astype(kind)


def setup_inputs(seed: int = 0) -> dict:
    arg_keys = jax.random.split(jax.random.key(seed), 4)
    slab = draw_slab(jax.random.fold_in(arg_keys[3], 71), 0)
    basis_x = gaussian(arg_keys[1], (MIDX, RANK), MIDX ** -0.5, 0.4375, jnp.float32)
    basis_y = gaussian(arg_keys[2], (MIDY, RANK), MIDY ** -0.5, 0.4375, jnp.float32)
    return {"slab": slab, "basis_x": basis_x, "basis_y": basis_y}


def reference(slab, basis_x, basis_y):
    high = lax.Precision.HIGHEST
    flat = slab.reshape(MIDX, -1)
    gram_x = lax.dot_general(flat, flat, (((1,), (1,)), ((), ())), precision=high, preferred_element_type=jnp.float32) / (MIDY * COLS)
    first = lax.dot_general(basis_x, flat, (((0,), (0,)), ((), ())), precision=high, preferred_element_type=jnp.float32).reshape(RANK, MIDY, COLS)
    batched = lax.dot_general(first, first, (((2,), (2,)), ((0,), (0,))), precision=high, preferred_element_type=jnp.float32)
    gram_y = jnp.sum(batched, axis=0) / (RANK * COLS)
    core = lax.dot_general(basis_y, first, (((0,), (1,)), ((), ())), precision=high, preferred_element_type=jnp.float32)
    return gram_x, gram_y, core
```

```python
import functools

import jax
import jax.numpy as jnp
from jax import lax
from jax.experimental import pallas as pl
from jax.experimental.pallas import tpu as pltpu
from jax.sharding import PartitionSpec as P

MESH = pl.DeviceIdType.MESH
F32 = jnp.float32
BF16 = jnp.bfloat16

MIDX = 192
MIDY = 192
RANK = 60
COLS = 6400
JB = 12
IB = 24
OWN = 50
PAIR = 2 * OWN
PACK = 1280
HALF = PACK // 2
HP = OWN // 2
CHUNKS = 4

NT = (((1,), (1,)), ((), ()))
NN = (((1,), (0,)), ((), ()))


def split(a):
    hi = a.astype(BF16)
    return hi, (a - hi.astype(F32)).astype(BF16)


def dot(a, b, dims):
    return lax.dot_general(a, b, dims, preferred_element_type=F32)


def kernel(
    slab, bxt, byt, gx_out, gy_out, core_out,
    raw, s1a, s1b, r1a, r1b, g, ft, fs, fr, bb, bq, gxx, gxm, gyy, gym,
    raw_sem, own_sem, s1_send, s1_recv, s2_send, s2_recv, y_send, y_recv,
):
    mx, my = lax.axis_index("mx"), lax.axis_index("my")
    x, zh = lax.rem(mx, 4), mx // 4
    y, zl, core = my // 4, lax.rem(my // 2, 2), lax.rem(my, 2)
    zz = zl * 2 + zh

    def device(px, py, pz, pc):
        return (lax.rem(pz, 2) * 4 + px, py * 4 + (pz // 2) * 2 + pc)

    def step(v, d):
        return lax.rem(v + d, 4)

    loads = []
    for j in range(JB):
        loads.append(pltpu.make_async_copy(slab.at[j], raw.at[j], raw_sem.at[j]))
        loads[-1].start()

    barrier = pltpu.get_barrier_semaphore()
    partners = [device(step(x, d), y, zz, core) for d in (1, 2, 3)]
    partners += [device(x, y, step(zz, d), core) for d in (1, 2, 3)]
    partners += [device(x, step(y, d), zz, c) for d in (1, 2, 3) for c in (0, 1)]
    partners += [device(x, y, zz, 1 - core)]
    for p in partners:
        pl.semaphore_signal(barrier, inc=1, device_id=p, device_id_type=MESH)

    bb[...] = jnp.zeros_like(bb)
    bb[0:RANK, :] = bxt[...]
    bb[64 : 64 + RANK, :] = bxt[...]
    bq[...] = jnp.zeros_like(bq)
    bq[0:RANK, :] = byt[...]
    for acc in (gxx, gxm, gyy, gym):
        acc[...] = jnp.zeros_like(acc)

    lane = lax.broadcasted_iota(jnp.int32, (IB, 128), 1)

    def pack(k):
        py = step(y, 1 + k)

        def block(b, carry):
            px, pz = b // 4, lax.rem(b, 4)
            off = PAIR * ((lax.rem(pz, 2) * 4 + px) * 8 + py * 2 + pz // 2)
            t0 = off // 128
            t1 = jnp.minimum(t0 + 1, COLS // 128 - 1)
            s = off - t0 * 128
            tiles = [None] * (PACK // 128)
            for j in range(JB):
                d, w = (j * PAIR) % 128, (j * PAIR) // 128
                sh = lax.rem(d - s + 128, 128)
                a = raw[j, :, pl.ds(pl.multiple_of(t0 * 128, 128), 128)]
                c = raw[j, :, pl.ds(pl.multiple_of(t1 * 128, 128), 128)]
                a = pltpu.roll(a, sh, 1)
                c = pltpu.roll(c, sh, 1)
                q = lax.rem(lane - d + 128, 128)
                v = jnp.where(q < 128 - s, a, c)
                tiles[w] = v if tiles[w] is None else jnp.where(lane < d, tiles[w], v)
                if d + PAIR > 128:
                    tiles[w + 1] = v
            tiles[-1] = jnp.where(lane < JB * PAIR - (PACK - 128), tiles[-1], 0.0)
            n = HALF // 128
            for w in range(n):
                s1a[k, px, pz, :, w * 128 : (w + 1) * 128] = tiles[w]
                s1b[k, pz, px, :, w * 128 : (w + 1) * 128] = tiles[n + w]
            return carry

        lax.fori_loop(0, 16, block, 0)

    def remote(src, dst, ssem, rsem, dev):
        return pltpu.make_async_remote_copy(
            src_ref=src, dst_ref=dst, send_sem=ssem, recv_sem=rsem, device_id=dev, device_id_type=MESH
        )

    def first_hop(k):
        out = []
        for d in (2, 1, 3):
            px, pz = step(x, d), step(zz, d)
            out.append(remote(s1a.at[k, px], r1a.at[k, x], s1_send.at[k, 0, d - 1], s1_recv.at[k, 0, d - 1], device(px, y, zz, core)))
            out.append(remote(s1b.at[k, pz], r1b.at[k, zz], s1_send.at[k, 1, d - 1], s1_recv.at[k, 1, d - 1], device(x, y, pz, core)))
        own = [
            pltpu.make_async_copy(s1a.at[k, x], r1a.at[k, x], own_sem.at[k, 0]),
            pltpu.make_async_copy(s1b.at[k, zz], r1b.at[k, zz], own_sem.at[k, 1]),
        ]
        for c in out + own:
            c.start()
        return out, own

    def second_hop(k):
        out = []
        for d in (2, 1, 3):
            px, pz = step(x, d), step(zz, d)
            out.append(remote(r1a.at[k, :, pz], g.at[k, 0, zz], s2_send.at[k, 0, d - 1], s2_recv.at[k, 0, d - 1], device(x, y, pz, core)))
            out.append(remote(r1b.at[k, :, px], g.at[k, 1, :, x], s2_send.at[k, 1, d - 1], s2_recv.at[k, 1, d - 1], device(px, y, zz, core)))
        own = [
            pltpu.make_async_copy(r1a.at[k, :, zz], g.at[k, 0, zz], own_sem.at[k, 2]),
            pltpu.make_async_copy(r1b.at[k, :, x], g.at[k, 1, :, x], own_sem.at[k, 3]),
        ]
        for c in out + own:
            c.start()
        return out, own

    def arrive(hop):
        out, own = hop
        for c in out:
            c.wait_recv()
        for c in own:
            c.wait()

    low = lax.broadcasted_iota(jnp.int32, (JB, 128), 1) < 64

    def project(k):
        def block(u, carry):
            h, v = u // 2, lax.rem(u, 2)
            a = g[k, h, pl.ds(v * 2, 2)].reshape(MIDX, HALF)
            hi, lo = split(a)
            gxx[...] += dot(hi, hi, NT)
            gxm[...] += dot(hi, lo, NT)
            bhi, blo = split(bb[...])
            f = dot(bhi, hi, NN) + (dot(blo, hi, NN) + dot(bhi, lo, NN))
            ft[v, pl.ds(pl.multiple_of(h * HALF, HALF), HALF), :] = f.T
            return carry

        lax.fori_loop(0, 4, block, 0)

        def pairs(p, carry):
            for c in (0, 1):
                for v in (0, 1):
                    a = ft[v, pl.ds(c * OWN + p, JB, PAIR), :]
                    b = ft[v, pl.ds(c * OWN + HP + p, JB, PAIR), :]
                    fs[k, c, p, v * JB : (v + 1) * JB, :] = jnp.where(low, a, b)
            return carry

        lax.fori_loop(0, HP, pairs, 0)

    def spread(k):
        py = step(y, 1 + k)
        if k < CHUNKS - 1:
            out = [
                remote(fs.at[k, c], fr.at[y, core], y_send.at[k, c], y_recv.at[k, core], device(x, py, zz, c))
                for c in (0, 1)
            ]
            own = []
        else:
            c = 1 - core
            out = [remote(fs.at[k, c], fr.at[y, core], y_send.at[k, 0], y_recv.at[k, core], device(x, y, zz, c))]
            own = [pltpu.make_async_copy(fs.at[k, core], fr.at[y, core], y_send.at[k, 1])]
        for c in out + own:
            c.start()
        return out, own

    for c in loads:
        c.wait()
    pack(0)
    pl.semaphore_wait(barrier, len(partners))
    hops1, hops2, hops3 = [first_hop(0)], [], []
    pack(1)
    hops1.append(first_hop(1))
    for k in range(CHUNKS):
        arrive(hops1[k])
        hops2.append(second_hop(k))
        if k + 2 < CHUNKS:
            pack(k + 2)
            hops1.append(first_hop(k + 2))
        if k > 0:
            arrive(hops2[k - 1])
            project(k - 1)
            hops3.append(spread(k - 1))
    arrive(hops2[-1])
    project(CHUNKS - 1)
    hops3.append(spread(CHUNKS - 1))

    for k in range(CHUNKS - 1):
        for c in (0, 1):
            remote(fs.at[k, c], fr.at[step(y, 3 - k), c], y_send.at[k, c], y_recv.at[k, c], device(x, y, zz, c)).wait_recv()
    out, own = hops3[-1]
    remote(fs.at[CHUNKS - 1, core], fr.at[y, 1 - core], y_send.at[CHUNKS - 1, 0], y_recv.at[CHUNKS - 1, 1 - core], device(x, y, zz, 1 - core)).wait_recv()
    own[0].wait()

    qhi, qlo = split(bq[...])
    wide = 5

    def finish(u, carry):
        parts = []
        for e in range(wide):
            p = u * wide + e
            rows = []
            for s in range(4):
                a, b = fr[s, 0, p], fr[s, 1, p]
                rows += [a[:JB], b[:JB], a[JB:], b[JB:]]
            parts.append(jnp.concatenate(rows, axis=0))
        hi, lo = split(jnp.concatenate(parts, axis=1))
        gyy[...] += dot(hi, hi, NT)
        gym[...] += dot(hi, lo, NT)
        c = dot(qhi, hi, NN) + (dot(qlo, hi, NN) + dot(qhi, lo, NN))
        for e in range(wide):
            p = u * wide + e
            v = c[:, e * 128 : (e + 1) * 128]
            core_out[p] = v[:RANK, :RANK]
            core_out[p + HP] = pltpu.roll(v, 64, 1)[:RANK, :RANK]
        return carry

    lax.fori_loop(0, HP // wide, finish, 0)
    gx_out[...] = (gxx[...] + (gxm[...] + gxm[...].T)) * (1.0 / (MIDY * COLS))
    gy_out[...] = (gyy[...] + (gym[...] + gym[...].T)) * (1.0 / (RANK * COLS))

    for out, _ in hops1 + hops2 + hops3:
        for c in out:
            c.wait_send()


def body(slab, basis_x, basis_y):
    vmem = pl.BlockSpec(memory_space=pltpu.VMEM)
    gx, gy, core = pl.pallas_call(
        kernel,
        out_shape=(
            jax.ShapeDtypeStruct((MIDX, MIDX), F32),
            jax.ShapeDtypeStruct((MIDY, MIDY), F32),
            jax.ShapeDtypeStruct((OWN, RANK, RANK), F32),
        ),
        in_specs=[pl.BlockSpec(memory_space=pl.ANY), vmem, vmem],
        out_specs=(vmem, vmem, vmem),
        scratch_shapes=[
            pltpu.VMEM((JB, IB, COLS), F32),
            pltpu.VMEM((CHUNKS, 4, 4, IB, HALF), F32),
            pltpu.VMEM((CHUNKS, 4, 4, IB, HALF), F32),
            pltpu.VMEM((CHUNKS, 4, 4, IB, HALF), F32),
            pltpu.VMEM((CHUNKS, 4, 4, IB, HALF), F32),
            pltpu.VMEM((CHUNKS, 2, 4, 4, IB, HALF), F32),
            pltpu.VMEM((2, PACK, 128), F32),
            pltpu.VMEM((CHUNKS, 2, HP, 2 * JB, 128), F32),
            pltpu.VMEM((4, 2, HP, 2 * JB, 128), F32),
            pltpu.VMEM((128, MIDX), F32),
            pltpu.VMEM((64, MIDY), F32),
            pltpu.VMEM((MIDX, MIDX), F32),
            pltpu.VMEM((MIDX, MIDX), F32),
            pltpu.VMEM((MIDY, MIDY), F32),
            pltpu.VMEM((MIDY, MIDY), F32),
            pltpu.SemaphoreType.DMA((JB,)),
            pltpu.SemaphoreType.DMA((CHUNKS, 4)),
            pltpu.SemaphoreType.DMA((CHUNKS, 2, 3)),
            pltpu.SemaphoreType.DMA((CHUNKS, 2, 3)),
            pltpu.SemaphoreType.DMA((CHUNKS, 2, 3)),
            pltpu.SemaphoreType.DMA((CHUNKS, 2, 3)),
            pltpu.SemaphoreType.DMA((CHUNKS, 2)),
            pltpu.SemaphoreType.DMA((CHUNKS, 2)),
        ],
        compiler_params=pltpu.CompilerParams(
            collective_id=0, has_side_effects=True, vmem_limit_bytes=58 * 2**20
        ),
    )(jnp.transpose(slab, (1, 0, 2)), basis_x.T, basis_y.T)
    gx, gy = lax.psum((gx, gy), ("mx", "my"))
    return gx, gy, jnp.transpose(core, (1, 2, 0))


def solution(mesh):
    return jax.shard_map(
        body,
        mesh=mesh,
        in_specs=(P("mx", "my", None), P(), P()),
        out_specs=(P(), P(), P(None, None, ("mx", "my"))),
        check_vma=False,
    )
```

```python
import functools

import jax
import jax.numpy as jnp
from jax import lax
from jax.experimental import pallas as pl
from jax.experimental.pallas import tpu as pltpu
from jax.sharding import PartitionSpec as P

MESH = pl.DeviceIdType.MESH
F32 = jnp.float32
BF16 = jnp.bfloat16

MIDX = 192
MIDY = 192
RANK = 60
COLS = 6400
JB = 12
IB = 24
OWN = 50
PAIR = 2 * OWN
PACK = 1280
HALF = PACK // 2
HP = OWN // 2
CHUNKS = 4

NT = (((1,), (1,)), ((), ()))
NN = (((1,), (0,)), ((), ()))


def split(a):
    hi = a.astype(BF16)
    return hi, (a - hi.astype(F32)).astype(BF16)


def dot(a, b, dims):
    return lax.dot_general(a, b, dims, preferred_element_type=F32)


def kernel(
    slab, bxt, byt, gx_out, gy_out, core_out,
    raw, s1a, s1b, r1a, r1b, g, ft, fs, fr, bb, bq, gxx, gxm, gyy, gym,
    part, parts8, sums, parts16, full,
    raw_sem, own_sem, s1_send, s1_recv, s2_send, s2_recv, y_send, y_recv,
    rs_send, rs_recv, bc_send, bc_recv, ag_send, ag_recv,
):
    mx, my = lax.axis_index("mx"), lax.axis_index("my")
    x, zh = lax.rem(mx, 4), mx // 4
    y, zl, core = my // 4, lax.rem(my // 2, 2), lax.rem(my, 2)
    zz = zl * 2 + zh

    def device(px, py, pz, pc):
        return (lax.rem(pz, 2) * 4 + px, py * 4 + (pz // 2) * 2 + pc)

    def step(v, d):
        return lax.rem(v + d, 4)

    loads = []
    for j in range(JB):
        loads.append(pltpu.make_async_copy(slab.at[j], raw.at[j], raw_sem.at[j]))
        loads[-1].start()

    barrier = pltpu.get_barrier_semaphore()
    partners = [device(step(x, d), y, zz, core) for d in (1, 2, 3)]
    partners += [device(x, y, step(zz, d), core) for d in (1, 2, 3)]
    partners += [device(x, step(y, d), zz, c) for d in (1, 2, 3) for c in (0, 1)]
    partners += [device(x, y, zz, 1 - core)]
    partners += [device(step(x, d), y, zz, 1 - core) for d in (1, 2, 3)]
    partners += [device(x, step(y, d), step(zz, e), core) for d in (1, 2, 3) for e in (1, 2, 3)]
    for p in partners:
        pl.semaphore_signal(barrier, inc=1, device_id=p, device_id_type=MESH)

    bb[...] = jnp.zeros_like(bb)
    bb[0:RANK, :] = bxt[...]
    bb[64 : 64 + RANK, :] = bxt[...]
    bq[...] = jnp.zeros_like(bq)
    bq[0:RANK, :] = byt[...]
    for acc in (gxx, gxm, gyy, gym):
        acc[...] = jnp.zeros_like(acc)

    lane = lax.broadcasted_iota(jnp.int32, (IB, 128), 1)

    def pack(k):
        py = step(y, 1 + k)

        def block(b, carry):
            px, pz = b // 4, lax.rem(b, 4)
            off = PAIR * ((lax.rem(pz, 2) * 4 + px) * 8 + py * 2 + pz // 2)
            t0 = off // 128
            t1 = jnp.minimum(t0 + 1, COLS // 128 - 1)
            s = off - t0 * 128
            tiles = [None] * (PACK // 128)
            for j in range(JB):
                d, w = (j * PAIR) % 128, (j * PAIR) // 128
                sh = lax.rem(d - s + 128, 128)
                a = raw[j, :, pl.ds(pl.multiple_of(t0 * 128, 128), 128)]
                c = raw[j, :, pl.ds(pl.multiple_of(t1 * 128, 128), 128)]
                a = pltpu.roll(a, sh, 1)
                c = pltpu.roll(c, sh, 1)
                q = lax.rem(lane - d + 128, 128)
                v = jnp.where(q < 128 - s, a, c)
                tiles[w] = v if tiles[w] is None else jnp.where(lane < d, tiles[w], v)
                if d + PAIR > 128:
                    tiles[w + 1] = v
            tiles[-1] = jnp.where(lane < JB * PAIR - (PACK - 128), tiles[-1], 0.0)
            n = HALF // 128
            for w in range(n):
                s1a[k, px, pz, :, w * 128 : (w + 1) * 128] = tiles[w]
                s1b[k, pz, px, :, w * 128 : (w + 1) * 128] = tiles[n + w]
            return carry

        lax.fori_loop(0, 16, block, 0)

    def remote(src, dst, ssem, rsem, dev):
        return pltpu.make_async_remote_copy(
            src_ref=src, dst_ref=dst, send_sem=ssem, recv_sem=rsem, device_id=dev, device_id_type=MESH
        )

    def first_hop(k):
        out = []
        for d in (2, 1, 3):
            px, pz = step(x, d), step(zz, d)
            out.append(remote(s1a.at[k, px], r1a.at[k, x], s1_send.at[k, 0, d - 1], s1_recv.at[k, 0, d - 1], device(px, y, zz, core)))
            out.append(remote(s1b.at[k, pz], r1b.at[k, zz], s1_send.at[k, 1, d - 1], s1_recv.at[k, 1, d - 1], device(x, y, pz, core)))
        own = [
            pltpu.make_async_copy(s1a.at[k, x], r1a.at[k, x], own_sem.at[k, 0]),
            pltpu.make_async_copy(s1b.at[k, zz], r1b.at[k, zz], own_sem.at[k, 1]),
        ]
        for c in out + own:
            c.start()
        return out, own

    def second_hop(k):
        out = []
        for d in (2, 1, 3):
            px, pz = step(x, d), step(zz, d)
            out.append(remote(r1a.at[k, :, pz], g.at[k, 0, zz], s2_send.at[k, 0, d - 1], s2_recv.at[k, 0, d - 1], device(x, y, pz, core)))
            out.append(remote(r1b.at[k, :, px], g.at[k, 1, :, x], s2_send.at[k, 1, d - 1], s2_recv.at[k, 1, d - 1], device(px, y, zz, core)))
        own = [
            pltpu.make_async_copy(r1a.at[k, :, zz], g.at[k, 0, zz], own_sem.at[k, 2]),
            pltpu.make_async_copy(r1b.at[k, :, x], g.at[k, 1, :, x], own_sem.at[k, 3]),
        ]
        for c in out + own:
            c.start()
        return out, own

    def arrive(hop):
        out, own = hop
        for c in out:
            c.wait_recv()
        for c in own:
            c.wait()

    low = lax.broadcasted_iota(jnp.int32, (JB, 128), 1) < 64

    def project(k):
        def block(u, carry):
            h, v = u // 2, lax.rem(u, 2)
            a = g[k, h, pl.ds(v * 2, 2)].reshape(MIDX, HALF)
            hi, lo = split(a)
            gxx[...] += dot(hi, hi, NT)
            gxm[...] += dot(hi, lo, NT)
            bhi, blo = split(bb[...])
            f = dot(bhi, hi, NN) + (dot(blo, hi, NN) + dot(bhi, lo, NN))
            ft[v, pl.ds(pl.multiple_of(h * HALF, HALF), HALF), :] = f.T
            return carry

        lax.fori_loop(0, 4, block, 0)

        def pairs(p, carry):
            for c in (0, 1):
                for v in (0, 1):
                    a = ft[v, pl.ds(c * OWN + p, JB, PAIR), :]
                    b = ft[v, pl.ds(c * OWN + HP + p, JB, PAIR), :]
                    fs[k, c, p, v * JB : (v + 1) * JB, :] = jnp.where(low, a, b)
            return carry

        lax.fori_loop(0, HP, pairs, 0)

    def spread(k):
        py = step(y, 1 + k)
        if k < CHUNKS - 1:
            out = [
                remote(fs.at[k, c], fr.at[y, core], y_send.at[k, c], y_recv.at[k, core], device(x, py, zz, c))
                for c in (0, 1)
            ]
            own = []
        else:
            c = 1 - core
            out = [remote(fs.at[k, c], fr.at[y, core], y_send.at[k, 0], y_recv.at[k, core], device(x, y, zz, c))]
            own = [pltpu.make_async_copy(fs.at[k, core], fr.at[y, core], y_send.at[k, 1])]
        for c in out + own:
            c.start()
        return out, own

    for c in loads:
        c.wait()
    pack(0)
    pl.semaphore_wait(barrier, len(partners))
    hops1, hops2, hops3 = [first_hop(0)], [], []
    pack(1)
    hops1.append(first_hop(1))
    for k in range(CHUNKS):
        arrive(hops1[k])
        hops2.append(second_hop(k))
        if k + 2 < CHUNKS:
            pack(k + 2)
            hops1.append(first_hop(k + 2))
        if k > 0:
            arrive(hops2[k - 1])
            project(k - 1)
            hops3.append(spread(k - 1))
    arrive(hops2[-1])
    project(CHUNKS - 1)
    hops3.append(spread(CHUNKS - 1))

    eights = [(d, e) for d in range(4) for e in range(2)]
    sixteens = [(d, e) for d in range(4) for e in range(4)]
    left = lax.broadcasted_iota(jnp.int32, (64, 128), 1) < 64

    def own_rows(px, pc):
        return pl.ds(pl.multiple_of((px * 2 + pc) * 24, 24), 24)

    def scatter(i, main, cross, scale):
        m = cross[...]
        main[...] = (main[...] + (m + m.T)) * scale
        part[i, 0:64] = main[0:64, 0:128]
        high = jnp.concatenate([main[64:128, 128:192], jnp.zeros((64, 64), F32)], axis=1)
        part[i, 64:128] = jnp.where(left, pltpu.roll(main[64:128, 0:128], 64, 1), pltpu.roll(high, 64, 1))
        top = jnp.concatenate([main[0:64, 128:192], jnp.zeros((64, 64), F32)], axis=1)
        end = jnp.concatenate([main[128:192, 128:192], jnp.zeros((64, 64), F32)], axis=1)
        part[i, 128:192] = jnp.where(left, top, pltpu.roll(end, 64, 1))
        out = []
        for n, (d, e) in enumerate(eights):
            if n:
                px, pc = step(x, d), lax.rem(core + e, 2)
                out.append(remote(part.at[i, own_rows(px, pc)], parts8.at[i, n - 1], rs_send.at[i, n - 1], rs_recv.at[i, n - 1], device(px, y, zz, pc)))
                out[-1].start()
        return out

    def share(i, hop):
        for c in hop:
            c.wait_recv()
        total = part[i, own_rows(x, core)]
        for n in range(7):
            total += parts8[i, n]
        sums[i] = total
        out = []
        for n, (d, e) in enumerate(sixteens):
            if n:
                out.append(remote(sums.at[i], parts16.at[i, y * 4 + zz], bc_send.at[i, n - 1], bc_recv.at[i, n - 1], device(x, step(y, d), step(zz, e), core)))
                out[-1].start()
        parts16[i, y * 4 + zz] = total
        return out

    def gather(i, hop):
        for c in hop:
            c.wait_recv()
        total = parts16[i, 0]
        for n in range(1, 16):
            total += parts16[i, n]
        full[i, own_rows(x, core)] = total
        out = []
        for n, (d, e) in enumerate(eights):
            if n:
                px, pc = step(x, d), lax.rem(core + e, 2)
                out.append(remote(full.at[i, own_rows(x, core)], full.at[i, own_rows(x, core)], ag_send.at[i, n - 1], ag_recv.at[i, n - 1], device(px, y, zz, pc)))
                out[-1].start()
        return out

    def unfold(i, hop, ref):
        for c in hop:
            c.wait_recv()
        p0, p1, p2 = full[i, 0:64], full[i, 64:128], full[i, 128:192]
        t0 = full[i, 0:128].T
        t2 = jnp.concatenate([p2, p2], axis=0).T
        q1, q2 = pltpu.roll(p1, 64, 1), pltpu.roll(p2, 64, 1)
        ref[0:64, 0:128] = p0
        ref[0:64, 128:192] = p2[:, :64]
        ref[64:128, 0:128] = jnp.where(left, t0[64:128], q1)
        ref[64:128, 128:192] = q1[:, :64]
        ref[128:192, 0:128] = jnp.where(left, t2[0:64], t0[64:128])
        ref[128:192, 128:192] = q2[:, :64]

    def columns(u):
        parts = []
        for e in range(wide):
            p = u * wide + e
            rows = []
            for s in range(4):
                a, b = fr[s, 0, p], fr[s, 1, p]
                rows += [a[:JB], b[:JB], a[JB:], b[JB:]]
            parts.append(jnp.concatenate(rows, axis=0))
        return split(jnp.concatenate(parts, axis=1))

    wide = 5

    def gram(u, carry):
        hi, lo = columns(u)
        gyy[...] += dot(hi, hi, NT)
        gym[...] += dot(hi, lo, NT)
        return carry

    qhi, qlo = split(bq[...])

    def finish(u, carry):
        hi, lo = columns(u)
        c = dot(qhi, hi, NN) + (dot(qlo, hi, NN) + dot(qhi, lo, NN))
        for e in range(wide):
            p = u * wide + e
            v = c[:, e * 128 : (e + 1) * 128]
            core_out[p] = v[:RANK, :RANK]
            core_out[p + HP] = pltpu.roll(v, 64, 1)[:RANK, :RANK]
        return carry

    rs0 = scatter(0, gxx, gxm, 1.0 / (MIDY * COLS))
    for k in range(CHUNKS - 1):
        for c in (0, 1):
            remote(fs.at[k, c], fr.at[step(y, 3 - k), c], y_send.at[k, c], y_recv.at[k, c], device(x, y, zz, c)).wait_recv()
    out, own = hops3[-1]
    remote(fs.at[CHUNKS - 1, core], fr.at[y, 1 - core], y_send.at[CHUNKS - 1, 0], y_recv.at[CHUNKS - 1, 1 - core], device(x, y, zz, 1 - core)).wait_recv()
    own[0].wait()
    lax.fori_loop(0, HP // wide, gram, 0)
    rs1 = scatter(1, gyy, gym, 1.0 / (RANK * COLS))
    bc0 = share(0, rs0)
    lax.fori_loop(0, HP // wide, finish, 0)
    bc1 = share(1, rs1)
    ag0 = gather(0, bc0)
    ag1 = gather(1, bc1)
    unfold(0, ag0, gx_out)
    unfold(1, ag1, gy_out)

    for out, _ in hops1 + hops2 + hops3:
        for c in out:
            c.wait_send()
    for c in rs0 + rs1 + bc0 + bc1 + ag0 + ag1:
        c.wait_send()


def body(slab, basis_x, basis_y):
    vmem = pl.BlockSpec(memory_space=pltpu.VMEM)
    gx, gy, core = pl.pallas_call(
        kernel,
        out_shape=(
            jax.ShapeDtypeStruct((MIDX, MIDX), F32),
            jax.ShapeDtypeStruct((MIDY, MIDY), F32),
            jax.ShapeDtypeStruct((OWN, RANK, RANK), F32),
        ),
        in_specs=[pl.BlockSpec(memory_space=pl.ANY), vmem, vmem],
        out_specs=(vmem, vmem, vmem),
        scratch_shapes=[
            pltpu.VMEM((JB, IB, COLS), F32),
            pltpu.VMEM((CHUNKS, 4, 4, IB, HALF), F32),
            pltpu.VMEM((CHUNKS, 4, 4, IB, HALF), F32),
            pltpu.VMEM((CHUNKS, 4, 4, IB, HALF), F32),
            pltpu.VMEM((CHUNKS, 4, 4, IB, HALF), F32),
            pltpu.VMEM((CHUNKS, 2, 4, 4, IB, HALF), F32),
            pltpu.VMEM((2, PACK, 128), F32),
            pltpu.VMEM((CHUNKS, 2, HP, 2 * JB, 128), F32),
            pltpu.VMEM((4, 2, HP, 2 * JB, 128), F32),
            pltpu.VMEM((128, MIDX), F32),
            pltpu.VMEM((64, MIDY), F32),
            pltpu.VMEM((MIDX, MIDX), F32),
            pltpu.VMEM((MIDX, MIDX), F32),
            pltpu.VMEM((MIDY, MIDY), F32),
            pltpu.VMEM((MIDY, MIDY), F32),
            pltpu.VMEM((2, 192, 128), F32),
            pltpu.VMEM((2, 7, 24, 128), F32),
            pltpu.VMEM((2, 24, 128), F32),
            pltpu.VMEM((2, 16, 24, 128), F32),
            pltpu.VMEM((2, 192, 128), F32),
            pltpu.SemaphoreType.DMA((JB,)),
            pltpu.SemaphoreType.DMA((CHUNKS, 4)),
            pltpu.SemaphoreType.DMA((CHUNKS, 2, 3)),
            pltpu.SemaphoreType.DMA((CHUNKS, 2, 3)),
            pltpu.SemaphoreType.DMA((CHUNKS, 2, 3)),
            pltpu.SemaphoreType.DMA((CHUNKS, 2, 3)),
            pltpu.SemaphoreType.DMA((CHUNKS, 2)),
            pltpu.SemaphoreType.DMA((CHUNKS, 2)),
            pltpu.SemaphoreType.DMA((2, 7)),
            pltpu.SemaphoreType.DMA((2, 7)),
            pltpu.SemaphoreType.DMA((2, 15)),
            pltpu.SemaphoreType.DMA((2, 15)),
            pltpu.SemaphoreType.DMA((2, 7)),
            pltpu.SemaphoreType.DMA((2, 7)),
        ],
        compiler_params=pltpu.CompilerParams(
            collective_id=0, has_side_effects=True, vmem_limit_bytes=58 * 2**20
        ),
    )(jnp.transpose(slab, (1, 0, 2)), basis_x.T, basis_y.T)
    return gx, gy, jnp.transpose(core, (1, 2, 0))


def solution(mesh):
    return jax.shard_map(
        body,
        mesh=mesh,
        in_specs=(P("mx", "my", None), P(), P()),
        out_specs=(P(), P(), P(None, None, ("mx", "my"))),
        check_vma=False,
    )
```

```python
import jax
import jax.numpy as jnp
from jax import lax
from jax.experimental import pallas as pl
from jax.experimental.pallas import tpu as pltpu
from jax.sharding import PartitionSpec as P

MESH = pl.DeviceIdType.MESH
F32 = jnp.float32
BF16 = jnp.bfloat16

MIDX = 192
MIDY = 192
RANK = 60
COLS = 6400
JB = 12
IB = 24
OWN = 50
PAIR = 2 * OWN
HP = OWN // 2
CHUNKS = 4
SEGS = CHUNKS * JB
PARTS = (((0, 5), (5, 5)), ((10, 5), (15, 5)), ((20, 5), (25, 4)), ((29, 3), (32, 3)), ((35, 1), (36, 2)))
TILES = 38
LANES = TILES // 2 * 128
STARTS = ((0, 0), (5, 5), (10, 10), (15, 14), (18, 17))
READY = {0: 0, 1: 1, 2: 2, 4: 3}

NT = (((1,), (1,)), ((), ()))
NN = (((1,), (0,)), ((), ()))


def split(a):
    hi = a.astype(BF16)
    return hi, (a - hi.astype(F32)).astype(BF16)


def dot(a, b, dims):
    return lax.dot_general(a, b, dims, preferred_element_type=F32)


def kernel(
    slab, bxt, byt, full_out, core_out,
    raw, s1a, s1b, r1a, r1b, g, ft, fs, fr, bases_v, bb, bq, gxx, gxm, gyy, gym,
    part, parts8, sums, parts16, full, core_v,
    load_sem, hop_send, s1_recv, s2_recv, y_send, y_recv, store_sem,
    rs_send, rs_recv, bc_send, bc_recv, ag_send, ag_recv,
):
    mx, my = lax.axis_index("mx"), lax.axis_index("my")
    x, zh = lax.rem(mx, 4), mx // 4
    y, zl, core = my // 4, lax.rem(my // 2, 2), lax.rem(my, 2)
    zz = zl * 2 + zh

    def device(px, py, pz, pc):
        return (lax.rem(pz, 2) * 4 + px, py * 4 + (pz // 2) * 2 + pc)

    def step(v, d):
        return lax.rem(v + d, 4)

    barrier = pltpu.get_barrier_semaphore()
    partners = [device(step(x, d), y, zz, core) for d in (1, 2, 3)]
    partners += [device(x, y, step(zz, d), core) for d in (1, 2, 3)]
    partners += [device(x, step(y, d), zz, c) for d in (1, 2, 3) for c in (0, 1)]
    partners += [device(x, y, zz, 1 - core)]
    for p in partners:
        pl.semaphore_signal(barrier, inc=1, device_id=p, device_id_type=MESH)


    early, late = pl.ds(0, 7), pl.ds(7, JB - 7)
    loads = [pltpu.make_async_copy(slab.at[r], raw.at[r], load_sem.at[n]) for n, r in enumerate((early, late))]
    bases = [pltpu.make_async_copy(b, bases_v.at[n], load_sem.at[2]) for n, b in enumerate((bxt, byt))]
    for c in loads + bases:
        c.start()

    def landed(ref, sem):
        pltpu.make_async_copy(ref, ref, sem).wait()

    lane = lax.broadcasted_iota(jnp.int32, (IB, 128), 1)

    def lanes(t, h):
        return pl.ds(STARTS[t][h] * 128, PARTS[t][h][1] * 128)

    def pack(t, h, px, pz, dst):
        first, count = PARTS[t][h]
        tiles = [None] * count
        where = {}
        for n in range(first * 128 // PAIR, min(SEGS, -(-(first + count) * 128 // PAIR))):
            k, j = divmod(n, JB)
            if k not in where:
                off = PAIR * ((lax.rem(pz, 2) * 4 + px) * 8 + step(y, 1 + k) * 2 + pz // 2)
                t0 = off // 128
                t1 = jnp.minimum(t0 + 1, COLS // 128 - 1)
                where[k] = (pl.multiple_of(t0 * 128, 128), pl.multiple_of(t1 * 128, 128), off - t0 * 128)
            l0, l1, s = where[k]
            d, w = (n * PAIR) % 128, (n * PAIR) // 128 - first
            sh = lax.rem(d - s + 128, 128)
            v0 = pltpu.roll(raw[j, :, pl.ds(l0, 128)], sh, 1)
            v1 = pltpu.roll(raw[j, :, pl.ds(l1, 128)], sh, 1)
            v = jnp.where(lax.rem(lane - d + 128, 128) < 128 - s, v0, v1)
            if 0 <= w < count:
                tiles[w] = v if tiles[w] is None else jnp.where(lane < d, tiles[w], v)
            if d + PAIR > 128 and w + 1 < count:
                tiles[w + 1] = v
        if first + count == TILES:
            tiles[-1] = jnp.where(lane < SEGS * PAIR - (TILES - 1) * 128, tiles[-1], 0.0)
        for w in range(count):
            lo = (STARTS[t][h] + w) * 128
            dst[:, lo : lo + 128] = tiles[w]

    def pack_a(t, px, dst):
        lax.fori_loop(0, 4, lambda pz, c: (pack(t, 0, px, pz, dst.at[pz]), c)[1], 0)

    def pack_b(t, pz, dst):
        lax.fori_loop(0, 4, lambda px, c: (pack(t, 1, px, pz, dst.at[px]), c)[1], 0)

    def remote(src, dst, ssem, rsem, dev):
        return pltpu.make_async_remote_copy(
            src_ref=src, dst_ref=dst, send_sem=ssem, recv_sem=rsem, device_id=dev, device_id_type=MESH
        )

    def first_copy(t, h, d):
        w = lanes(t, h)
        if h == 0:
            px = step(x, d)
            return remote(s1a.at[px, :, :, w], r1a.at[x, :, :, w], hop_send.at[0], s1_recv.at[t, 0], device(px, y, zz, core))
        pz = step(zz, d)
        return remote(s1b.at[pz, :, :, w], r1b.at[zz, :, :, w], hop_send.at[1], s1_recv.at[t, 1], device(x, y, pz, core))

    def send_a(t, d):
        px = step(x, d)
        pack_a(t, px, s1a.at[px])
        first_copy(t, 0, d).start()

    def send_b(t, d):
        pz = step(zz, d)
        pack_b(t, pz, s1b.at[pz])
        first_copy(t, 1, d).start()

    def first_hop(t, begun=False):
        def message(n, carry):
            d = 2 - n + 3 * (n // 2)
            send_a(t, d)
            send_b(t, d)
            return carry

        lax.fori_loop(1 if begun else 0, 3, message, 0)
        pack_a(t, x, r1a.at[x])
        pack_b(t, zz, r1b.at[zz])

    def second_hop(t):
        wa, wb = lanes(t, 0), lanes(t, 1)
        landed(r1a.at[0:3, :, :, wa], s1_recv.at[t, 0])
        landed(r1b.at[0:3, :, :, wb], s1_recv.at[t, 1])
        for d in (2, 1, 3):
            px, pz = step(x, d), step(zz, d)
            remote(r1a.at[:, pz, :, wa], g.at[0, zz, :, :, wa], hop_send.at[2], s2_recv.at[t, 0], device(x, y, pz, core)).start()
            remote(r1b.at[:, px, :, wb], g.at[1, :, x, :, wb], hop_send.at[3], s2_recv.at[t, 1], device(px, y, zz, core)).start()
        pltpu.make_async_copy(r1a.at[:, zz, :, wa], g.at[0, zz, :, :, wa], s2_recv.at[t, 0]).start()
        pltpu.make_async_copy(r1b.at[:, x, :, wb], g.at[1, :, x, :, wb], s2_recv.at[t, 1]).start()

    low = lax.broadcasted_iota(jnp.int32, (JB, 128), 1) < 64

    def project(t):
        for h in (0, 1):
            first, count = PARTS[t][h]

            def block(v, carry, h=h, first=first, count=count):
                a = g[h, pl.ds(v * 2, 2), :, :, lanes(t, h)].reshape(MIDX, count * 128)
                hi, lo = split(a)
                gxx[...] += dot(hi, hi, NT)
                gxm[...] += dot(hi, lo, NT)
                bhi, blo = split(bb[...])
                f = dot(bhi, hi, NN) + (dot(blo, hi, NN) + dot(bhi, lo, NN))
                ft[v, first * 128 : (first + count) * 128, :] = f.T
                return carry

            lax.fori_loop(0, 2, block, 0)

    def pair(k):
        def pairs(p, carry):
            for c in (0, 1):
                for v in (0, 1):
                    row = k * JB * PAIR + c * OWN + p
                    a = ft[v, pl.ds(row, JB, PAIR), :]
                    b = ft[v, pl.ds(row + HP, JB, PAIR), :]
                    fs[k, c, p, v * JB : (v + 1) * JB, :] = jnp.where(low, a, b)
            return carry

        lax.fori_loop(0, HP, pairs, 0)

    def spread(k):
        py = step(y, 1 + k)
        if k < CHUNKS - 1:
            for c in (0, 1):
                remote(fs.at[k, c], fr.at[y, core], y_send.at[0], y_recv.at[k], device(x, py, zz, c)).start()
        else:
            c = 1 - core
            remote(fs.at[k, c], fr.at[y, core], y_send.at[1], y_recv.at[k], device(x, y, zz, c)).start()
            pltpu.make_async_copy(fs.at[k, core], fr.at[y, core], y_recv.at[k]).start()

    def chunk(t):
        landed(g.at[0, :, :, :, lanes(t, 0)], s2_recv.at[t, 0])
        landed(g.at[1, :, :, :, lanes(t, 1)], s2_recv.at[t, 1])
        project(t)
        if t in READY:
            pair(READY[t])
            spread(READY[t])

    loads[0].wait()
    pl.semaphore_wait(barrier, len(partners))
    send_a(0, 2)
    loads[1].wait()
    send_b(0, 2)
    first_hop(0, True)
    first_hop(1)
    landed(bases_v, load_sem.at[2])
    bb[...] = jnp.zeros_like(bb)
    bb[0:RANK, :] = bases_v[0]
    bb[64 : 64 + RANK, :] = bases_v[0]
    bq[...] = jnp.zeros_like(bq)
    bq[0:RANK, :] = bases_v[1]
    for acc in (gxx, gxm, gyy, gym):
        acc[...] = jnp.zeros_like(acc)
    second_hop(0)
    first_hop(2)
    second_hop(1)
    chunk(0)
    second_hop(2)
    first_hop(3)
    first_hop(4)
    chunk(1)
    chunk(2)
    second_hop(3)
    second_hop(4)
    chunk(3)
    chunk(4)

    eights = [(d, e) for d in range(4) for e in range(2)]
    sixteens = [(d, e) for d in (2, 1, 3, 0) for e in (2, 1, 3, 0)]
    left = lax.broadcasted_iota(jnp.int32, (64, 128), 1) < 64

    def own_rows(px, pc):
        return pl.ds(pl.multiple_of((px * 2 + pc) * 24, 24), 24)

    def scatter(i, main, cross, scale):
        m = cross[...]
        main[...] = (main[...] + (m + m.T)) * scale
        part[i, 0:64] = main[0:64, 0:128]
        high = jnp.concatenate([main[64:128, 128:192], jnp.zeros((64, 64), F32)], axis=1)
        part[i, 64:128] = jnp.where(left, pltpu.roll(main[64:128, 0:128], 64, 1), pltpu.roll(high, 64, 1))
        top = jnp.concatenate([main[0:64, 128:192], jnp.zeros((64, 64), F32)], axis=1)
        end = jnp.concatenate([main[128:192, 128:192], jnp.zeros((64, 64), F32)], axis=1)
        part[i, 128:192] = jnp.where(left, top, pltpu.roll(end, 64, 1))
        for d, e in eights[::-1]:
            if d or e:
                px, pc = step(x, d), lax.rem(core + e, 2)
                remote(part.at[i, own_rows(px, pc)], parts8.at[i, d * 2 + e - 1], rs_send.at[i], rs_recv.at[i], device(px, y, zz, pc)).start()

    def share(i):
        landed(parts8.at[i], rs_recv.at[i])
        total = part[i, own_rows(x, core)]
        for n in range(7):
            total += parts8[i, n]
        sums[i] = total
        for d, e in sixteens:
            if d or e:
                remote(sums.at[i], parts16.at[i, y * 4 + zz], bc_send.at[i], bc_recv.at[i], device(x, step(y, d), step(zz, e), core)).start()
        parts16[i, y * 4 + zz] = total

    def gather(i):
        landed(parts16.at[i, 0:15], bc_recv.at[i])
        total = parts16[i, 0]
        for n in range(1, 16):
            total += parts16[i, n]
        full[i, own_rows(x, core)] = total
        for d, e in eights[::-1]:
            if d or e:
                px, pc = step(x, d), lax.rem(core + e, 2)
                remote(full.at[i, own_rows(x, core)], full.at[i, own_rows(x, core)], ag_send.at[i], ag_recv.at[i], device(px, y, zz, pc)).start()

    wide = 5

    def columns(u):
        parts = []
        for e in range(wide):
            p = u * wide + e
            rows = []
            for s in range(4):
                a, b = fr[s, 0, p], fr[s, 1, p]
                rows += [a[:JB], b[:JB], a[JB:], b[JB:]]
            parts.append(jnp.concatenate(rows, axis=0))
        return split(jnp.concatenate(parts, axis=1))

    def gram(u, carry):
        hi, lo = columns(u)
        gyy[...] += dot(hi, hi, NT)
        gym[...] += dot(hi, lo, NT)
        return carry

    qhi, qlo = split(bq[...])

    def finish(u, carry):
        hi, lo = columns(u)
        c = dot(qhi, hi, NN) + (dot(qlo, hi, NN) + dot(qhi, lo, NN))
        for e in range(wide):
            p = u * wide + e
            core_v[p] = c[:, e * 128 : (e + 1) * 128]
        return carry

    for k in range(CHUNKS):
        landed(fr.at[0], y_recv.at[k])
    scatter(0, gxx, gxm, 1.0 / (MIDY * COLS))
    lax.fori_loop(0, HP // wide, gram, 0)
    scatter(1, gyy, gym, 1.0 / (RANK * COLS))
    share(0)
    lax.fori_loop(0, HP // wide, finish, 0)
    core_store = pltpu.make_async_copy(core_v, core_out, store_sem.at[0])
    core_store.start()
    share(1)
    gather(0)
    gather(1)
    landed(s1a.at[0:3], hop_send.at[0])
    landed(s1b.at[0:3], hop_send.at[1])
    landed(r1a.at[0:3], hop_send.at[2])
    landed(r1b.at[0:3], hop_send.at[3])
    landed(fs.at[0:3], y_send.at[0])
    landed(fs.at[3, 0], y_send.at[1])
    for i in (0, 1):
        landed(parts8.at[i], rs_send.at[i])
        landed(parts16.at[i, 0:15], bc_send.at[i])
    core_store.wait()
    for i in (0, 1):
        landed(full.at[i, 0:168], ag_recv.at[i])
    store = pltpu.make_async_copy(full, full_out, store_sem.at[1])
    store.start()
    for i in (0, 1):
        landed(full.at[i, 0:168], ag_send.at[i])
    store.wait()


def unfold(full, core, gx_out, gy_out, core_out):
    left = lax.broadcasted_iota(jnp.int32, (64, 128), 1) < 64
    for i, ref in enumerate((gx_out, gy_out)):
        p0, p1, p2 = full[i, 0:64], full[i, 64:128], full[i, 128:192]
        t0 = full[i, 0:128].T
        t2 = jnp.concatenate([p2, p2], axis=0).T
        q1, q2 = pltpu.roll(p1, 64, 1), pltpu.roll(p2, 64, 1)
        ref[0:64, 0:128] = p0
        ref[0:64, 128:192] = p2[:, :64]
        ref[64:128, 0:128] = jnp.where(left, t0[64:128], q1)
        ref[64:128, 128:192] = q1[:, :64]
        ref[128:192, 0:128] = jnp.where(left, t2[0:64], t0[64:128])
        ref[128:192, 128:192] = q2[:, :64]
    for p in range(HP):
        v = core[p]
        core_out[p] = v[:RANK, :RANK]
        core_out[p + HP] = pltpu.roll(v, 64, 1)[:RANK, :RANK]


def body(slab, basis_x, basis_y):
    anywhere = pl.BlockSpec(memory_space=pl.ANY)
    vmem = pl.BlockSpec(memory_space=pltpu.VMEM)
    full, core = pl.pallas_call(
        kernel,
        out_shape=(
            jax.ShapeDtypeStruct((2, 192, 128), F32),
            jax.ShapeDtypeStruct((HP, 64, 128), F32),
        ),
        in_specs=[anywhere] * 3,
        out_specs=(anywhere, anywhere),
        scratch_shapes=[
            pltpu.VMEM((JB, IB, COLS), F32),
            pltpu.VMEM((4, 4, IB, LANES), F32),
            pltpu.VMEM((4, 4, IB, LANES), F32),
            pltpu.VMEM((4, 4, IB, LANES), F32),
            pltpu.VMEM((4, 4, IB, LANES), F32),
            pltpu.VMEM((2, 4, 4, IB, LANES), F32),
            pltpu.VMEM((2, TILES * 128, 128), F32),
            pltpu.VMEM((CHUNKS, 2, HP, 2 * JB, 128), F32),
            pltpu.VMEM((4, 2, HP, 2 * JB, 128), F32),
            pltpu.VMEM((2, RANK, MIDX), F32),
            pltpu.VMEM((128, MIDX), F32),
            pltpu.VMEM((64, MIDY), F32),
            pltpu.VMEM((MIDX, MIDX), F32),
            pltpu.VMEM((MIDX, MIDX), F32),
            pltpu.VMEM((MIDY, MIDY), F32),
            pltpu.VMEM((MIDY, MIDY), F32),
            pltpu.VMEM((2, 192, 128), F32),
            pltpu.VMEM((2, 7, 24, 128), F32),
            pltpu.VMEM((2, 24, 128), F32),
            pltpu.VMEM((2, 16, 24, 128), F32),
            pltpu.VMEM((2, 192, 128), F32),
            pltpu.VMEM((HP, 64, 128), F32),
            pltpu.SemaphoreType.DMA((3,)),
            pltpu.SemaphoreType.DMA((4,)),
            pltpu.SemaphoreType.DMA((len(PARTS), 2)),
            pltpu.SemaphoreType.DMA((len(PARTS), 2)),
            pltpu.SemaphoreType.DMA((2,)),
            pltpu.SemaphoreType.DMA((CHUNKS,)),
            pltpu.SemaphoreType.DMA((2,)),
            pltpu.SemaphoreType.DMA((2,)),
            pltpu.SemaphoreType.DMA((2,)),
            pltpu.SemaphoreType.DMA((2,)),
            pltpu.SemaphoreType.DMA((2,)),
            pltpu.SemaphoreType.DMA((2,)),
            pltpu.SemaphoreType.DMA((2,)),
        ],
        compiler_params=pltpu.CompilerParams(
            collective_id=0, has_side_effects=True, vmem_limit_bytes=58 * 2**20
        ),
    )(jnp.transpose(slab, (1, 0, 2)), basis_x.T, basis_y.T)
    gx, gy, core = pl.pallas_call(
        unfold,
        out_shape=(
            jax.ShapeDtypeStruct((MIDX, MIDX), F32),
            jax.ShapeDtypeStruct((MIDY, MIDY), F32),
            jax.ShapeDtypeStruct((OWN, RANK, RANK), F32),
        ),
        in_specs=[vmem, vmem],
        out_specs=(vmem, vmem, vmem),
    )(full, core)
    return gx, gy, jnp.transpose(core, (1, 2, 0))


def solution(mesh):
    return jax.shard_map(
        body,
        mesh=mesh,
        in_specs=(P("mx", "my", None), P(), P()),
        out_specs=(P(), P(), P(None, None, ("mx", "my"))),
        check_vma=False,
    )
```

```python
import jax
import jax.numpy as jnp
from jax import lax
from jax.experimental import pallas as pl
from jax.experimental.pallas import tpu as pltpu
from jax.sharding import PartitionSpec as P

MESH = pl.DeviceIdType.MESH
F32 = jnp.float32
BF16 = jnp.bfloat16

MIDX = 192
MIDY = 192
RANK = 60
COLS = 6400
JB = 12
IB = 24
OWN = 50
PAIR = 2 * OWN
HP = OWN // 2
CHUNKS = 4
EARLY, LATE = 34, 16
EP, LP = EARLY // 2, LATE // 2
RUNS = [(k * JB * PAIR + j * PAIR, k, j, 0, PAIR) for k in range(CHUNKS - 1) for j in range(JB)]
FIRST = (CHUNKS - 1) * JB * PAIR
RUNS += [(FIRST + (2 * j + i) * EARLY, CHUNKS - 1, j, i * (PAIR - EARLY), EARLY) for j in range(JB) for i in (0, 1)]
FILLED = FIRST + 2 * JB * EARLY
SECOND = -(-FILLED // 128) * 128
RUNS += [(SECOND + j * 2 * LATE, CHUNKS - 1, j, EARLY, 2 * LATE) for j in range(JB)]
PARTS = (
    ((0, 2), (2, 2)), ((4, 3), (7, 3)), ((10, 5), (15, 5)),
    ((20, 5), (25, 4)), ((29, 3), (32, 3)), ((35, 1), (36, 2)),
)
TILES = 38
LANES = TILES // 2 * 128
STARTS = ((0, 0), (2, 2), (5, 5), (10, 10), (15, 14), (18, 17))

NT = (((1,), (1,)), ((), ()))
NN = (((1,), (0,)), ((), ()))


def split(a):
    hi = a.astype(BF16)
    return hi, (a - hi.astype(F32)).astype(BF16)


def dot(a, b, dims):
    return lax.dot_general(a, b, dims, preferred_element_type=F32)


def kernel(
    slab, bxt, byt, full_out, core_out,
    raw, s1a, s1b, r1a, r1b, g, ft, fs, fr, bases_v, bb, bq, gxx, gxm, gyy, gym,
    part, parts8, sums, parts16, full, core_v,
    load_sem, hop_send, s1_recv, s2_recv, y_send, y_recv, store_sem,
    rs_send, rs_recv, bc_send, bc_recv, ag_send, ag_recv,
):
    mx, my = lax.axis_index("mx"), lax.axis_index("my")
    x, zh = lax.rem(mx, 4), mx // 4
    y, zl, core = my // 4, lax.rem(my // 2, 2), lax.rem(my, 2)
    zz = zl * 2 + zh

    def device(px, py, pz, pc):
        return (lax.rem(pz, 2) * 4 + px, py * 4 + (pz // 2) * 2 + pc)

    def step(v, d):
        return lax.rem(v + d, 4)

    barrier = pltpu.get_barrier_semaphore()
    partners = [device(step(x, d), y, zz, core) for d in (1, 2, 3)]
    partners += [device(x, y, step(zz, d), core) for d in (1, 2, 3)]
    partners += [device(x, step(y, d), zz, c) for d in (1, 2, 3) for c in (0, 1)]
    partners += [device(step(x, d), y, zz, 1 - core) for d in range(4)]
    for p in partners:
        pl.semaphore_signal(barrier, inc=1, device_id=p, device_id_type=MESH)


    rows = (pl.ds(0, 3), pl.ds(3, 3), pl.ds(6, 6))
    loads = [pltpu.make_async_copy(slab.at[r], raw.at[r], load_sem.at[n]) for n, r in enumerate(rows)]
    bases = [pltpu.make_async_copy(b, bases_v.at[n], load_sem.at[3]) for n, b in enumerate((bxt, byt))]
    for c in loads + bases:
        c.start()

    def landed(ref, sem):
        pltpu.make_async_copy(ref, ref, sem).wait()

    lane = lax.broadcasted_iota(jnp.int32, (IB, 128), 1)

    def lanes(t, h):
        return pl.ds(STARTS[t][h] * 128, PARTS[t][h][1] * 128)

    def pack(t, h, px, pz, dst):
        first, count = PARTS[t][h]
        tiles = [None] * count
        base = {}
        for at, k, j, col, size in RUNS:
            d, w = at % 128, at // 128 - first
            if w >= count or at + size <= first * 128:
                continue
            if k not in base:
                base[k] = PAIR * ((lax.rem(pz, 2) * 4 + px) * 8 + step(y, 1 + k) * 2 + pz // 2)
            off = base[k] + col
            t0 = off // 128
            t1 = jnp.minimum(t0 + 1, COLS // 128 - 1)
            s = off - t0 * 128
            sh = lax.rem(d - s + 128, 128)
            v0 = pltpu.roll(raw[j, :, pl.ds(pl.multiple_of(t0 * 128, 128), 128)], sh, 1)
            v1 = pltpu.roll(raw[j, :, pl.ds(pl.multiple_of(t1 * 128, 128), 128)], sh, 1)
            v = jnp.where(lax.rem(lane - d + 128, 128) < 128 - s, v0, v1)
            if w >= 0:
                tiles[w] = v if tiles[w] is None else jnp.where(lane < d, tiles[w], v)
            if d + size > 128 and w + 1 < count:
                tiles[w + 1] = v
        if first <= FILLED // 128 < first + count:
            w = FILLED // 128 - first
            tiles[w] = jnp.where(lane < FILLED % 128, tiles[w], 0.0)
        for w in range(count):
            lo = (STARTS[t][h] + w) * 128
            dst[:, lo : lo + 128] = tiles[w]

    def pack_a(t, px, dst):
        lax.fori_loop(0, 4, lambda pz, c: (pack(t, 0, px, pz, dst.at[pz]), c)[1], 0)

    def pack_b(t, pz, dst):
        lax.fori_loop(0, 4, lambda px, c: (pack(t, 1, px, pz, dst.at[px]), c)[1], 0)

    def remote(src, dst, ssem, rsem, dev):
        return pltpu.make_async_remote_copy(
            src_ref=src, dst_ref=dst, send_sem=ssem, recv_sem=rsem, device_id=dev, device_id_type=MESH
        )

    def first_copy(t, h, d):
        w = lanes(t, h)
        if h == 0:
            px = step(x, d)
            return remote(s1a.at[px, :, :, w], r1a.at[x, :, :, w], hop_send.at[0], s1_recv.at[t, 0], device(px, y, zz, core))
        pz = step(zz, d)
        return remote(s1b.at[pz, :, :, w], r1b.at[zz, :, :, w], hop_send.at[1], s1_recv.at[t, 1], device(x, y, pz, core))

    def send_a(t, d):
        px = step(x, d)
        pack_a(t, px, s1a.at[px])
        first_copy(t, 0, d).start()

    def send_b(t, d):
        pz = step(zz, d)
        pack_b(t, pz, s1b.at[pz])
        first_copy(t, 1, d).start()

    def first_hop(t, begun=False):
        def message(n, carry):
            d = 2 - n + 3 * (n // 2)
            send_a(t, d)
            send_b(t, d)
            return carry

        lax.fori_loop(1 if begun else 0, 3, message, 0)
        pack_a(t, x, r1a.at[x])
        pack_b(t, zz, r1b.at[zz])

    def second_hop(t):
        wa, wb = lanes(t, 0), lanes(t, 1)
        landed(r1a.at[0:3, :, :, wa], s1_recv.at[t, 0])
        landed(r1b.at[0:3, :, :, wb], s1_recv.at[t, 1])
        for d in (2, 1, 3):
            px, pz = step(x, d), step(zz, d)
            remote(r1a.at[:, pz, :, wa], g.at[0, zz, :, :, wa], hop_send.at[2], s2_recv.at[t, 0], device(x, y, pz, core)).start()
            remote(r1b.at[:, px, :, wb], g.at[1, :, x, :, wb], hop_send.at[3], s2_recv.at[t, 1], device(px, y, zz, core)).start()
        pltpu.make_async_copy(r1a.at[:, zz, :, wa], g.at[0, zz, :, :, wa], s2_recv.at[t, 0]).start()
        pltpu.make_async_copy(r1b.at[:, x, :, wb], g.at[1, :, x, :, wb], s2_recv.at[t, 1]).start()

    low = lax.broadcasted_iota(jnp.int32, (JB, 128), 1) < 64

    def project(t):
        both = [(h, v) for h in (0, 1) for v in (0, 1)]
        for group in (both,) if t > 3 else (both[:2], both[2:]):
            blocks = [g[h, v * 2 : v * 2 + 2, :, :, lanes(t, h)].reshape(MIDX, -1) for h, v in group]
            hi, lo = split(jnp.concatenate(blocks, axis=1))
            gxx[...] += dot(hi, hi, NT)
            gxm[...] += dot(hi, lo, NT)
            bhi, blo = split(bb[...])
            f = dot(bhi, hi, NN) + (dot(blo, hi, NN) + dot(bhi, lo, NN))
            at = 0
            for h, v in group:
                first, size = PARTS[t][h][0] * 128, PARTS[t][h][1] * 128
                ft[v, first : first + size, :] = f[:, at : at + size].T
                at += size

    def pair(k, c, row, gap, stride, at, n):
        def pairs(p, carry):
            for v in (0, 1):
                a = ft[v, pl.ds(row + p, JB, stride), :]
                b = ft[v, pl.ds(row + gap + p, JB, stride), :]
                fs[k, c, at + p, v * JB : (v + 1) * JB, :] = jnp.where(low, a, b)
            return carry

        lax.fori_loop(0, n, pairs, 0)

    def spread(k):
        py = step(y, 1 + k)
        for c in (0, 1):
            row = k * JB * PAIR + c * (OWN + LATE)
            pair(k, c, row, EP, PAIR, 0, EP)
            pair(k, c, k * JB * PAIR + (OWN if c else EARLY), LP, PAIR, EP, LP)
            remote(fs.at[k, c], fr.at[y, core], y_send.at[0], y_recv.at[k], device(x, py, zz, c)).start()

    def swap(part):
        k, c = CHUNKS - 1, 1 - core
        at, n = ((0, EP), (EP, LP))[part]
        for i in (0, 1):
            row = SECOND + i * LATE if part else FIRST + i * EARLY
            pair(k, i, row, n, 2 * (LATE if part else EARLY), at, n)
        w = pl.ds(at, n)
        remote(fs.at[k, c, w], fr.at[y, core, w], y_send.at[1], y_recv.at[k + part], device(x, y, zz, c)).start()
        pltpu.make_async_copy(fs.at[k, core, w], fr.at[y, core, w], y_recv.at[k + part]).start()

    def chunk(t):
        landed(g.at[0, :, :, :, lanes(t, 0)], s2_recv.at[t, 0])
        landed(g.at[1, :, :, :, lanes(t, 1)], s2_recv.at[t, 1])
        project(t)

    loads[0].wait()
    pack_a(0, step(x, 2), s1a.at[step(x, 2)])
    loads[1].wait()
    pack_b(0, step(zz, 2), s1b.at[step(zz, 2)])
    pl.semaphore_wait(barrier, len(partners))
    first_copy(0, 0, 2).start()
    first_copy(0, 1, 2).start()
    first_hop(0, True)
    loads[2].wait()
    first_hop(1)
    first_hop(2)
    landed(bases_v, load_sem.at[3])
    bb[...] = jnp.zeros_like(bb)
    bb[0:RANK, :] = bases_v[0]
    bb[64 : 64 + RANK, :] = bases_v[0]
    bq[...] = jnp.zeros_like(bq)
    bq[0:RANK, :] = bases_v[1]
    for acc in (gxx, gxm, gyy, gym):
        acc[...] = jnp.zeros_like(acc)
    second_hop(0)
    second_hop(1)
    first_hop(3)
    second_hop(2)
    chunk(0)
    chunk(1)
    spread(0)
    second_hop(3)
    first_hop(4)
    first_hop(5)
    chunk(2)
    spread(1)
    chunk(3)
    spread(2)
    second_hop(4)
    second_hop(5)
    chunk(4)
    swap(0)
    chunk(5)
    swap(1)

    eights = [(d, e) for d in range(4) for e in range(2)]
    sixteens = [(d, e) for d in (2, 1, 3, 0) for e in (2, 1, 3, 0)]
    left = lax.broadcasted_iota(jnp.int32, (64, 128), 1) < 64

    def own_rows(px, pc):
        return pl.ds(pl.multiple_of((px * 2 + pc) * 24, 24), 24)

    def scatter(i, main, cross, scale):
        m = cross[...]
        main[...] = (main[...] + (m + m.T)) * scale
        part[i, 0:64] = main[0:64, 0:128]
        high = jnp.concatenate([main[64:128, 128:192], jnp.zeros((64, 64), F32)], axis=1)
        part[i, 64:128] = jnp.where(left, pltpu.roll(main[64:128, 0:128], 64, 1), pltpu.roll(high, 64, 1))
        top = jnp.concatenate([main[0:64, 128:192], jnp.zeros((64, 64), F32)], axis=1)
        end = jnp.concatenate([main[128:192, 128:192], jnp.zeros((64, 64), F32)], axis=1)
        part[i, 128:192] = jnp.where(left, top, pltpu.roll(end, 64, 1))
        for d, e in eights[::-1]:
            if d or e:
                px, pc = step(x, d), lax.rem(core + e, 2)
                remote(part.at[i, own_rows(px, pc)], parts8.at[i, d * 2 + e - 1], rs_send.at[i], rs_recv.at[i], device(px, y, zz, pc)).start()

    def share(i):
        landed(parts8.at[i], rs_recv.at[i])
        total = part[i, own_rows(x, core)]
        for n in range(7):
            total += parts8[i, n]
        sums[i] = total
        for d, e in sixteens:
            if d or e:
                remote(sums.at[i], parts16.at[i, y * 4 + zz], bc_send.at[i], bc_recv.at[i], device(x, step(y, d), step(zz, e), core)).start()
        parts16[i, y * 4 + zz] = total

    def gather(i):
        landed(parts16.at[i, 0:15], bc_recv.at[i])
        total = parts16[i, 0]
        for n in range(1, 16):
            total += parts16[i, n]
        full[i, own_rows(x, core)] = total
        for d, e in eights[::-1]:
            if d or e:
                px, pc = step(x, d), lax.rem(core + e, 2)
                remote(full.at[i, own_rows(x, core)], full.at[i, own_rows(x, core)], ag_send.at[i], ag_recv.at[i], device(px, y, zz, pc)).start()

    def columns(at, n):
        parts = []
        for p in range(n):
            rows = []
            for s in range(4):
                a, b = fr[s, 0, at + p], fr[s, 1, at + p]
                rows += [a[:JB], b[:JB], a[JB:], b[JB:]]
            parts.append(jnp.concatenate(rows, axis=0))
        return split(jnp.concatenate(parts, axis=1))

    def gram(at, n):
        hi, lo = columns(at, n)
        gyy[...] += dot(hi, hi, NT)
        gym[...] += dot(hi, lo, NT)

    qhi, qlo = split(bq[...])
    wide = 5

    def finish(u, carry):
        hi, lo = columns(u * wide, wide)
        c = dot(qhi, hi, NN) + (dot(qlo, hi, NN) + dot(qhi, lo, NN))
        for p in range(wide):
            core_v[u * wide + p] = c[:, p * 128 : (p + 1) * 128]
        return carry

    scatter(0, gxx, gxm, 1.0 / (MIDY * COLS))
    for k in range(CHUNKS - 1):
        landed(fr.at[0], y_recv.at[k])
    landed(fr.at[0, :, 0:EP], y_recv.at[CHUNKS - 1])
    gram(0, 6)
    gram(6, 6)
    gram(12, 5)
    landed(fr.at[0, :, EP:HP], y_recv.at[CHUNKS])
    gram(EP, LP)
    scatter(1, gyy, gym, 1.0 / (RANK * COLS))
    share(0)
    lax.fori_loop(0, HP // wide, finish, 0)
    core_store = pltpu.make_async_copy(core_v, core_out, store_sem.at[0])
    core_store.start()
    share(1)
    gather(0)
    gather(1)
    landed(s1a.at[0:3], hop_send.at[0])
    landed(s1b.at[0:3], hop_send.at[1])
    landed(r1a.at[0:3], hop_send.at[2])
    landed(r1b.at[0:3], hop_send.at[3])
    landed(fs.at[0:3], y_send.at[0])
    landed(fs.at[3, 0], y_send.at[1])
    for i in (0, 1):
        landed(parts8.at[i], rs_send.at[i])
        landed(parts16.at[i, 0:15], bc_send.at[i])
    core_store.wait()
    for i in (0, 1):
        landed(full.at[i, 0:168], ag_recv.at[i])
    store = pltpu.make_async_copy(full, full_out, store_sem.at[1])
    store.start()
    for i in (0, 1):
        landed(full.at[i, 0:168], ag_send.at[i])
    store.wait()


def unfold(full, core, gx_out, gy_out, core_out):
    left = lax.broadcasted_iota(jnp.int32, (64, 128), 1) < 64
    for i, ref in enumerate((gx_out, gy_out)):
        p0, p1, p2 = full[i, 0:64], full[i, 64:128], full[i, 128:192]
        t0 = full[i, 0:128].T
        t2 = jnp.concatenate([p2, p2], axis=0).T
        q1, q2 = pltpu.roll(p1, 64, 1), pltpu.roll(p2, 64, 1)
        ref[0:64, 0:128] = p0
        ref[0:64, 128:192] = p2[:, :64]
        ref[64:128, 0:128] = jnp.where(left, t0[64:128], q1)
        ref[64:128, 128:192] = q1[:, :64]
        ref[128:192, 0:128] = jnp.where(left, t2[0:64], t0[64:128])
        ref[128:192, 128:192] = q2[:, :64]
    odd = lax.rem(lax.axis_index("my"), 2)
    for p in range(HP):
        v = core[p]
        first, gap = (LATE * odd + p, EP) if p < EP else (EARLY * (1 - odd) + p - EP, LP)
        core_out[first] = v[:RANK, :RANK]
        core_out[first + gap] = pltpu.roll(v, 64, 1)[:RANK, :RANK]


def body(slab, basis_x, basis_y):
    anywhere = pl.BlockSpec(memory_space=pl.ANY)
    vmem = pl.BlockSpec(memory_space=pltpu.VMEM)
    full, core = pl.pallas_call(
        kernel,
        out_shape=(
            jax.ShapeDtypeStruct((2, 192, 128), F32),
            jax.ShapeDtypeStruct((HP, 64, 128), F32),
        ),
        in_specs=[anywhere] * 3,
        out_specs=(anywhere, anywhere),
        scratch_shapes=[
            pltpu.VMEM((JB, IB, COLS), F32),
            pltpu.VMEM((4, 4, IB, LANES), F32),
            pltpu.VMEM((4, 4, IB, LANES), F32),
            pltpu.VMEM((4, 4, IB, LANES), F32),
            pltpu.VMEM((4, 4, IB, LANES), F32),
            pltpu.VMEM((2, 4, 4, IB, LANES), F32),
            pltpu.VMEM((2, TILES * 128, 128), F32),
            pltpu.VMEM((CHUNKS, 2, HP, 2 * JB, 128), F32),
            pltpu.VMEM((4, 2, HP, 2 * JB, 128), F32),
            pltpu.VMEM((2, RANK, MIDX), F32),
            pltpu.VMEM((128, MIDX), F32),
            pltpu.VMEM((64, MIDY), F32),
            pltpu.VMEM((MIDX, MIDX), F32),
            pltpu.VMEM((MIDX, MIDX), F32),
            pltpu.VMEM((MIDY, MIDY), F32),
            pltpu.VMEM((MIDY, MIDY), F32),
            pltpu.VMEM((2, 192, 128), F32),
            pltpu.VMEM((2, 7, 24, 128), F32),
            pltpu.VMEM((2, 24, 128), F32),
            pltpu.VMEM((2, 16, 24, 128), F32),
            pltpu.VMEM((2, 192, 128), F32),
            pltpu.VMEM((HP, 64, 128), F32),
            pltpu.SemaphoreType.DMA((4,)),
            pltpu.SemaphoreType.DMA((4,)),
            pltpu.SemaphoreType.DMA((len(PARTS), 2)),
            pltpu.SemaphoreType.DMA((len(PARTS), 2)),
            pltpu.SemaphoreType.DMA((2,)),
            pltpu.SemaphoreType.DMA((CHUNKS + 1,)),
            pltpu.SemaphoreType.DMA((2,)),
            pltpu.SemaphoreType.DMA((2,)),
            pltpu.SemaphoreType.DMA((2,)),
            pltpu.SemaphoreType.DMA((2,)),
            pltpu.SemaphoreType.DMA((2,)),
            pltpu.SemaphoreType.DMA((2,)),
            pltpu.SemaphoreType.DMA((2,)),
        ],
        compiler_params=pltpu.CompilerParams(
            collective_id=0, has_side_effects=True, vmem_limit_bytes=58 * 2**20
        ),
    )(jnp.transpose(slab, (1, 0, 2)), basis_x.T, basis_y.T)
    gx, gy, core = pl.pallas_call(
        unfold,
        out_shape=(
            jax.ShapeDtypeStruct((MIDX, MIDX), F32),
            jax.ShapeDtypeStruct((MIDY, MIDY), F32),
            jax.ShapeDtypeStruct((OWN, RANK, RANK), F32),
        ),
        in_specs=[vmem, vmem],
        out_specs=(vmem, vmem, vmem),
    )(full, core)
    return gx, gy, jnp.transpose(core, (1, 2, 0))


def solution(mesh):
    return jax.shard_map(
        body,
        mesh=mesh,
        in_specs=(P("mx", "my", None), P(), P()),
        out_specs=(P(), P(), P(None, None, ("mx", "my"))),
        check_vma=False,
    )
```

```python
import jax
import jax.numpy as jnp
from jax import lax
from jax.experimental import pallas as pl
from jax.experimental.pallas import tpu as pltpu
from jax.sharding import PartitionSpec as P

MESH = pl.DeviceIdType.MESH
F32 = jnp.float32
BF16 = jnp.bfloat16

MIDX = 192
MIDY = 192
RANK = 60
COLS = 6400
JB = 12
IB = 24
OWN = 50
PAIR = 2 * OWN
HP = OWN // 2
CHUNKS = 4
AHEAD = (2, 1, 3, 0)
EARLY, LATE = 34, 16
EP, LP = EARLY // 2, LATE // 2
RUNS = [(k * JB * PAIR + j * PAIR, k, j, 0, PAIR) for k in range(CHUNKS - 1) for j in range(JB)]
FIRST = (CHUNKS - 1) * JB * PAIR
RUNS += [(FIRST + (2 * j + i) * EARLY, CHUNKS - 1, j, i * (PAIR - EARLY), EARLY) for j in range(JB) for i in (0, 1)]
FILLED = FIRST + 2 * JB * EARLY
SECOND = -(-FILLED // 128) * 128
RUNS += [(SECOND + j * 2 * LATE, CHUNKS - 1, j, EARLY, 2 * LATE) for j in range(JB)]
PARTS = (
    ((0, 2), (2, 2)), ((4, 3), (7, 3)), ((10, 5), (15, 5)),
    ((20, 5), (25, 4)), ((29, 3), (32, 3)), ((35, 1), (36, 2)),
)
TILES = 38
LANES = TILES // 2 * 128
STARTS = ((0, 0), (2, 2), (5, 5), (10, 10), (15, 14), (18, 17))

NT = (((1,), (1,)), ((), ()))
NN = (((1,), (0,)), ((), ()))


def split(a):
    hi = a.astype(BF16)
    return hi, (a - hi.astype(F32)).astype(BF16)


def dot(a, b, dims):
    return lax.dot_general(a, b, dims, preferred_element_type=F32)


def kernel(
    slab, bxt, byt, full_out, core_out,
    raw, s1a, s1b, r1a, r1b, g, ft, fs, fr, bases_v, bb, bq, gxx, gxm, gyy, gym,
    part, parts8, sums, parts16, full, core_v,
    load_sem, hop_send, s1_recv, s2_recv, y_send, y_recv, store_sem,
    rs_send, rs_recv, bc_send, bc_recv, ag_send, ag_recv,
):
    mx, my = lax.axis_index("mx"), lax.axis_index("my")
    x, zh = lax.rem(mx, 4), mx // 4
    y, zl, core = my // 4, lax.rem(my // 2, 2), lax.rem(my, 2)
    zz = zl * 2 + zh

    def device(px, py, pz, pc):
        return (lax.rem(pz, 2) * 4 + px, py * 4 + (pz // 2) * 2 + pc)

    def step(v, d):
        return lax.rem(v + d, 4)

    barrier = pltpu.get_barrier_semaphore()
    partners = [device(step(x, d), y, zz, core) for d in (1, 2, 3)]
    partners += [device(x, y, step(zz, d), core) for d in (1, 2, 3)]
    partners += [device(x, step(y, d), zz, c) for d in (1, 2, 3) for c in (0, 1)]
    partners += [device(step(x, d), y, zz, 1 - core) for d in range(4)]
    for p in partners:
        pl.semaphore_signal(barrier, inc=1, device_id=p, device_id_type=MESH)


    rows = (pl.ds(0, 3), pl.ds(3, 3), pl.ds(6, 6))
    loads = [pltpu.make_async_copy(slab.at[r], raw.at[r], load_sem.at[n]) for n, r in enumerate(rows)]
    bases = [pltpu.make_async_copy(b, bases_v.at[n], load_sem.at[3]) for n, b in enumerate((bxt, byt))]
    for c in loads + bases:
        c.start()

    def landed(ref, sem):
        pltpu.make_async_copy(ref, ref, sem).wait()

    lane = lax.broadcasted_iota(jnp.int32, (IB, 128), 1)

    def lanes(t, h):
        return pl.ds(STARTS[t][h] * 128, PARTS[t][h][1] * 128)

    def pack(t, h, px, pz, dst):
        first, count = PARTS[t][h]
        tiles = [None] * count
        base = {}
        for at, k, j, col, size in RUNS:
            d, w = at % 128, at // 128 - first
            if w >= count or at + size <= first * 128:
                continue
            if k not in base:
                base[k] = PAIR * ((lax.rem(pz, 2) * 4 + px) * 8 + step(y, AHEAD[k]) * 2 + pz // 2)
            off = base[k] + col
            t0 = off // 128
            t1 = jnp.minimum(t0 + 1, COLS // 128 - 1)
            s = off - t0 * 128
            sh = lax.rem(d - s + 128, 128)
            v0 = pltpu.roll(raw[j, :, pl.ds(pl.multiple_of(t0 * 128, 128), 128)], sh, 1)
            v1 = pltpu.roll(raw[j, :, pl.ds(pl.multiple_of(t1 * 128, 128), 128)], sh, 1)
            v = jnp.where(lax.rem(lane - d + 128, 128) < 128 - s, v0, v1)
            if w >= 0:
                tiles[w] = v if tiles[w] is None else jnp.where(lane < d, tiles[w], v)
            if d + size > 128 and w + 1 < count:
                tiles[w + 1] = v
        if first <= FILLED // 128 < first + count:
            w = FILLED // 128 - first
            tiles[w] = jnp.where(lane < FILLED % 128, tiles[w], 0.0)
        for w in range(count):
            lo = (STARTS[t][h] + w) * 128
            dst[:, lo : lo + 128] = tiles[w]

    def pack_a(t, px, dst):
        lax.fori_loop(0, 4, lambda pz, c: (pack(t, 0, px, pz, dst.at[pz]), c)[1], 0)

    def pack_b(t, pz, dst):
        lax.fori_loop(0, 4, lambda px, c: (pack(t, 1, px, pz, dst.at[px]), c)[1], 0)

    def remote(src, dst, ssem, rsem, dev):
        return pltpu.make_async_remote_copy(
            src_ref=src, dst_ref=dst, send_sem=ssem, recv_sem=rsem, device_id=dev, device_id_type=MESH
        )

    def first_copy(t, h, d):
        w = lanes(t, h)
        if h == 0:
            px = step(x, d)
            return remote(s1a.at[px, :, :, w], r1a.at[x, :, :, w], hop_send.at[0], s1_recv.at[t, 0], device(px, y, zz, core))
        pz = step(zz, d)
        return remote(s1b.at[pz, :, :, w], r1b.at[zz, :, :, w], hop_send.at[1], s1_recv.at[t, 1], device(x, y, pz, core))

    def send_a(t, d):
        px = step(x, d)
        pack_a(t, px, s1a.at[px])
        first_copy(t, 0, d).start()

    def send_b(t, d):
        pz = step(zz, d)
        pack_b(t, pz, s1b.at[pz])
        first_copy(t, 1, d).start()

    def first_hop(t, begun=False):
        def message(n, carry):
            d = 2 - n + 3 * (n // 2)
            send_a(t, d)
            send_b(t, d)
            return carry

        lax.fori_loop(1 if begun else 0, 3, message, 0)
        pack_a(t, x, r1a.at[x])
        pack_b(t, zz, r1b.at[zz])

    def second_hop(t):
        wa, wb = lanes(t, 0), lanes(t, 1)
        landed(r1a.at[0:3, :, :, wa], s1_recv.at[t, 0])
        landed(r1b.at[0:3, :, :, wb], s1_recv.at[t, 1])
        for d in (2, 1, 3):
            px, pz = step(x, d), step(zz, d)
            remote(r1a.at[:, pz, :, wa], g.at[0, zz, :, :, wa], hop_send.at[2], s2_recv.at[t, 0], device(x, y, pz, core)).start()
            remote(r1b.at[:, px, :, wb], g.at[1, :, x, :, wb], hop_send.at[3], s2_recv.at[t, 1], device(px, y, zz, core)).start()
        pltpu.make_async_copy(r1a.at[:, zz, :, wa], g.at[0, zz, :, :, wa], s2_recv.at[t, 0]).start()
        pltpu.make_async_copy(r1b.at[:, x, :, wb], g.at[1, :, x, :, wb], s2_recv.at[t, 1]).start()

    low = lax.broadcasted_iota(jnp.int32, (JB, 128), 1) < 64

    def project(t):
        both = [(h, v) for h in (0, 1) for v in (0, 1)]
        for group in (both,) if t > 3 else (both[:2], both[2:]):
            blocks = [g[h, v * 2 : v * 2 + 2, :, :, lanes(t, h)].reshape(MIDX, -1) for h, v in group]
            hi, lo = split(jnp.concatenate(blocks, axis=1))
            gxx[...] += dot(hi, hi, NT)
            gxm[...] += dot(hi, lo, NT)
            bhi, blo = split(bb[...])
            f = dot(bhi, hi, NN) + (dot(blo, hi, NN) + dot(bhi, lo, NN))
            at = 0
            for h, v in group:
                first, size = PARTS[t][h][0] * 128, PARTS[t][h][1] * 128
                ft[v, first : first + size, :] = f[:, at : at + size].T
                at += size

    def pair(k, c, row, gap, stride, at, n):
        def pairs(p, carry):
            for v in (0, 1):
                a = ft[v, pl.ds(row + p, JB, stride), :]
                b = ft[v, pl.ds(row + gap + p, JB, stride), :]
                fs[k, c, at + p, v * JB : (v + 1) * JB, :] = jnp.where(low, a, b)
            return carry

        lax.fori_loop(0, n, pairs, 0)

    def spread(k):
        py = step(y, AHEAD[k])
        for c in (0, 1):
            row = k * JB * PAIR + c * (OWN + LATE)
            pair(k, c, row, EP, PAIR, 0, EP)
            pair(k, c, k * JB * PAIR + (OWN if c else EARLY), LP, PAIR, EP, LP)
            remote(fs.at[k, c], fr.at[y, core], y_send.at[0], y_recv.at[k], device(x, py, zz, c)).start()

    def swap(part):
        k, c = CHUNKS - 1, 1 - core
        at, n = ((0, EP), (EP, LP))[part]
        w = pl.ds(at, n)

        def collect(i):
            row = SECOND + i * LATE if part else FIRST + i * EARLY
            pair(k, i, row, n, 2 * (LATE if part else EARLY), at, n)

        collect(c)
        remote(fs.at[k, c, w], fr.at[y, core, w], y_send.at[1], y_recv.at[k + part], device(x, y, zz, c)).start()
        collect(core)
        pltpu.make_async_copy(fs.at[k, core, w], fr.at[y, core, w], y_recv.at[k + part]).start()

    def chunk(t):
        landed(g.at[0, :, :, :, lanes(t, 0)], s2_recv.at[t, 0])
        landed(g.at[1, :, :, :, lanes(t, 1)], s2_recv.at[t, 1])
        project(t)

    eights = [(d, e) for d in (2, 1, 3, 0) for e in (1, 0)]
    sixteens = [(d, e) for d in (2, 1, 3, 0) for e in (2, 1, 3, 0)]
    left = lax.broadcasted_iota(jnp.int32, (64, 128), 1) < 64

    def own_rows(px, pc):
        return pl.ds(pl.multiple_of((px * 2 + pc) * 24, 24), 24)

    def scatter(i, main, cross, scale):
        m = cross[...]
        main[...] = (main[...] + (m + m.T)) * scale
        part[i, 0:64] = main[0:64, 0:128]
        high = jnp.concatenate([main[64:128, 128:192], jnp.zeros((64, 64), F32)], axis=1)
        part[i, 64:128] = jnp.where(left, pltpu.roll(main[64:128, 0:128], 64, 1), pltpu.roll(high, 64, 1))
        top = jnp.concatenate([main[0:64, 128:192], jnp.zeros((64, 64), F32)], axis=1)
        end = jnp.concatenate([main[128:192, 128:192], jnp.zeros((64, 64), F32)], axis=1)
        part[i, 128:192] = jnp.where(left, top, pltpu.roll(end, 64, 1))
        for d, e in eights:
            if d or e:
                px, pc = step(x, d), lax.rem(core + e, 2)
                remote(part.at[i, own_rows(px, pc)], parts8.at[i, d * 2 + e - 1], rs_send.at[i], rs_recv.at[i], device(px, y, zz, pc)).start()

    def share(i):
        landed(parts8.at[i], rs_recv.at[i])
        total = part[i, own_rows(x, core)]
        for n in range(7):
            total += parts8[i, n]
        sums[i] = total

    def spread_yz(i):
        parts16[i, y * 4 + zz] = sums[i]
        for d, e in sixteens:
            if d or e:
                remote(sums.at[i], parts16.at[i, y * 4 + zz], bc_send.at[i], bc_recv.at[i], device(x, step(y, d), step(zz, e), core)).start()

    def gather_yz(i):
        landed(parts16.at[i, 0:15], bc_recv.at[i])
        total = parts16[i, 0]
        for n in range(1, 16):
            total += parts16[i, n]
        return total

    def publish(i, total):
        full[i, own_rows(x, core)] = total
        for d, e in eights:
            if d or e:
                px, pc = step(x, d), lax.rem(core + e, 2)
                remote(full.at[i, own_rows(x, core)], full.at[i, own_rows(x, core)], ag_send.at[i], ag_recv.at[i], device(px, y, zz, pc)).start()

    def columns(at, n):
        parts = []
        for p in range(n):
            rows = []
            for s in range(4):
                a, b = fr[s, 0, at + p], fr[s, 1, at + p]
                rows += [a[:JB], b[:JB], a[JB:], b[JB:]]
            parts.append(jnp.concatenate(rows, axis=0))
        return split(jnp.concatenate(parts, axis=1))

    def gram(at, n):
        hi, lo = columns(at, n)
        gyy[...] += dot(hi, hi, NT)
        gym[...] += dot(hi, lo, NT)

    wide = 5

    def finish(u, carry):
        qhi, qlo = split(bq[...])
        hi, lo = columns(u * wide, wide)
        c = dot(qhi, hi, NN) + (dot(qlo, hi, NN) + dot(qhi, lo, NN))
        for p in range(wide):
            core_v[u * wide + p] = c[:, p * 128 : (p + 1) * 128]
        return carry

    loads[0].wait()
    pack_a(0, step(x, 2), s1a.at[step(x, 2)])
    loads[1].wait()
    pack_b(0, step(zz, 2), s1b.at[step(zz, 2)])
    pl.semaphore_wait(barrier, len(partners))
    first_copy(0, 0, 2).start()
    first_copy(0, 1, 2).start()
    first_hop(0, True)
    loads[2].wait()
    first_hop(1)
    first_hop(2)
    landed(bases_v, load_sem.at[3])
    bb[...] = jnp.zeros_like(bb)
    bb[0:RANK, :] = bases_v[0]
    bb[64 : 64 + RANK, :] = bases_v[0]
    bq[...] = jnp.zeros_like(bq)
    bq[0:RANK, :] = bases_v[1]
    for acc in (gxx, gxm, gyy, gym):
        acc[...] = jnp.zeros_like(acc)
    second_hop(0)
    second_hop(1)
    first_hop(3)
    second_hop(2)
    chunk(0)
    chunk(1)
    spread(0)
    second_hop(3)
    first_hop(4)
    first_hop(5)
    chunk(2)
    spread(1)
    chunk(3)
    spread(2)
    second_hop(4)
    second_hop(5)
    chunk(4)
    swap(0)
    chunk(5)
    scatter(0, gxx, gxm, 1.0 / (MIDY * COLS))
    swap(1)

    for k in range(CHUNKS - 1):
        landed(fr.at[0], y_recv.at[k])
    landed(fr.at[0, :, 0:EP], y_recv.at[CHUNKS - 1])
    gram(0, 6)
    gram(6, 6)
    gram(12, 5)
    landed(fr.at[0, :, EP:HP], y_recv.at[CHUNKS])
    gram(EP, LP)
    scatter(1, gyy, gym, 1.0 / (RANK * COLS))
    share(0)
    spread_yz(0)
    share(1)
    spread_yz(1)
    lax.fori_loop(0, HP // wide, finish, 0)
    core_store = pltpu.make_async_copy(core_v, core_out, store_sem.at[0])
    core_store.start()
    publish(0, gather_yz(0))
    publish(1, gather_yz(1))
    landed(s1a.at[0:3], hop_send.at[0])
    landed(s1b.at[0:3], hop_send.at[1])
    landed(r1a.at[0:3], hop_send.at[2])
    landed(r1b.at[0:3], hop_send.at[3])
    landed(fs.at[0:3], y_send.at[0])
    landed(fs.at[3, 0], y_send.at[1])
    for i in (0, 1):
        landed(parts8.at[i], rs_send.at[i])
        landed(parts16.at[i, 0:15], bc_send.at[i])
    core_store.wait()
    for i in (0, 1):
        landed(full.at[i, 0:168], ag_recv.at[i])
    store = pltpu.make_async_copy(full, full_out, store_sem.at[1])
    store.start()
    for i in (0, 1):
        landed(full.at[i, 0:168], ag_send.at[i])
    store.wait()


def unfold(full, core, gx_out, gy_out, core_out):
    left = lax.broadcasted_iota(jnp.int32, (64, 128), 1) < 64
    for i, ref in enumerate((gx_out, gy_out)):
        p0, p1, p2 = full[i, 0:64], full[i, 64:128], full[i, 128:192]
        t0 = full[i, 0:128].T
        t2 = jnp.concatenate([p2, p2], axis=0).T
        q1, q2 = pltpu.roll(p1, 64, 1), pltpu.roll(p2, 64, 1)
        ref[0:64, 0:128] = p0
        ref[0:64, 128:192] = p2[:, :64]
        ref[64:128, 0:128] = jnp.where(left, t0[64:128], q1)
        ref[64:128, 128:192] = q1[:, :64]
        ref[128:192, 0:128] = jnp.where(left, t2[0:64], t0[64:128])
        ref[128:192, 128:192] = q2[:, :64]
    odd = lax.rem(lax.axis_index("my"), 2)
    for p in range(HP):
        v = core[p]
        first, gap = (LATE * odd + p, EP) if p < EP else (EARLY * (1 - odd) + p - EP, LP)
        core_out[first] = v[:RANK, :RANK]
        core_out[first + gap] = pltpu.roll(v, 64, 1)[:RANK, :RANK]


def body(slab, basis_x, basis_y):
    anywhere = pl.BlockSpec(memory_space=pl.ANY)
    vmem = pl.BlockSpec(memory_space=pltpu.VMEM)
    full, core = pl.pallas_call(
        kernel,
        out_shape=(
            jax.ShapeDtypeStruct((2, 192, 128), F32),
            jax.ShapeDtypeStruct((HP, 64, 128), F32),
        ),
        in_specs=[anywhere] * 3,
        out_specs=(anywhere, anywhere),
        scratch_shapes=[
            pltpu.VMEM((JB, IB, COLS), F32),
            pltpu.VMEM((4, 4, IB, LANES), F32),
            pltpu.VMEM((4, 4, IB, LANES), F32),
            pltpu.VMEM((4, 4, IB, LANES), F32),
            pltpu.VMEM((4, 4, IB, LANES), F32),
            pltpu.VMEM((2, 4, 4, IB, LANES), F32),
            pltpu.VMEM((2, TILES * 128, 128), F32),
            pltpu.VMEM((CHUNKS, 2, HP, 2 * JB, 128), F32),
            pltpu.VMEM((4, 2, HP, 2 * JB, 128), F32),
            pltpu.VMEM((2, RANK, MIDX), F32),
            pltpu.VMEM((128, MIDX), F32),
            pltpu.VMEM((64, MIDY), F32),
            pltpu.VMEM((MIDX, MIDX), F32),
            pltpu.VMEM((MIDX, MIDX), F32),
            pltpu.VMEM((MIDY, MIDY), F32),
            pltpu.VMEM((MIDY, MIDY), F32),
            pltpu.VMEM((2, 192, 128), F32),
            pltpu.VMEM((2, 7, 24, 128), F32),
            pltpu.VMEM((2, 24, 128), F32),
            pltpu.VMEM((2, 16, 24, 128), F32),
            pltpu.VMEM((2, 192, 128), F32),
            pltpu.VMEM((HP, 64, 128), F32),
            pltpu.SemaphoreType.DMA((4,)),
            pltpu.SemaphoreType.DMA((4,)),
            pltpu.SemaphoreType.DMA((len(PARTS), 2)),
            pltpu.SemaphoreType.DMA((len(PARTS), 2)),
            pltpu.SemaphoreType.DMA((2,)),
            pltpu.SemaphoreType.DMA((CHUNKS + 1,)),
            pltpu.SemaphoreType.DMA((2,)),
            pltpu.SemaphoreType.DMA((2,)),
            pltpu.SemaphoreType.DMA((2,)),
            pltpu.SemaphoreType.DMA((2,)),
            pltpu.SemaphoreType.DMA((2,)),
            pltpu.SemaphoreType.DMA((2,)),
            pltpu.SemaphoreType.DMA((2,)),
        ],
        compiler_params=pltpu.CompilerParams(
            collective_id=0, has_side_effects=True, vmem_limit_bytes=58 * 2**20
        ),
    )(jnp.transpose(slab, (1, 0, 2)), basis_x.T, basis_y.T)
    gx, gy, core = pl.pallas_call(
        unfold,
        out_shape=(
            jax.ShapeDtypeStruct((MIDX, MIDX), F32),
            jax.ShapeDtypeStruct((MIDY, MIDY), F32),
            jax.ShapeDtypeStruct((OWN, RANK, RANK), F32),
        ),
        in_specs=[vmem, vmem],
        out_specs=(vmem, vmem, vmem),
    )(full, core)
    return gx, gy, jnp.transpose(core, (1, 2, 0))


def solution(mesh):
    return jax.shard_map(
        body,
        mesh=mesh,
        in_specs=(P("mx", "my", None), P(), P()),
        out_specs=(P(), P(), P(None, None, ("mx", "my"))),
        check_vma=False,
    )
```

```python
import jax
import jax.numpy as jnp
from jax import lax
from jax.experimental import pallas as pl
from jax.experimental.pallas import tpu as pltpu
from jax.sharding import PartitionSpec as P

MESH = pl.DeviceIdType.MESH
F32 = jnp.float32
BF16 = jnp.bfloat16

MIDX = 192
MIDY = 192
RANK = 60
COLS = 6400
JB = 12
IB = 24
OWN = 50
PAIR = 2 * OWN
HP = OWN // 2
CHUNKS = 4
AHEAD = (2, 1, 3, 0)
EARLY, LATE = 34, 16
EP, LP = EARLY // 2, LATE // 2
RUNS = [(k * JB * PAIR + j * PAIR, k, j, 0, PAIR) for k in range(CHUNKS - 1) for j in range(JB)]
FIRST = (CHUNKS - 1) * JB * PAIR
RUNS += [(FIRST + (2 * j + i) * EARLY, CHUNKS - 1, j, i * (PAIR - EARLY), EARLY) for j in range(JB) for i in (0, 1)]
FILLED = FIRST + 2 * JB * EARLY
SECOND = -(-FILLED // 128) * 128
RUNS += [(SECOND + j * 2 * LATE, CHUNKS - 1, j, EARLY, 2 * LATE) for j in range(JB)]
PARTS = (
    ((0, 2), (2, 2)), ((4, 3), (7, 3)), ((10, 5), (15, 5)),
    ((20, 5), (25, 4)), ((29, 3), (32, 3)), ((35, 1), (36, 2)),
)
TILES = 38
LANES = TILES // 2 * 128
STARTS = ((0, 0), (2, 2), (5, 5), (10, 10), (15, 14), (18, 17))

NT = (((1,), (1,)), ((), ()))
NN = (((1,), (0,)), ((), ()))


def split(a):
    hi = a.astype(BF16)
    return hi, (a - hi.astype(F32)).astype(BF16)


def dot(a, b, dims):
    return lax.dot_general(a, b, dims, preferred_element_type=F32)


def kernel(
    slab, bxt, byt, full_out, core_out,
    raw, s1a, s1b, r1a, r1b, g, ft, fs, fr, bases_v, bb, bq, gxx, gxm, gyy, gym,
    part, parts8, sums, parts16, full, core_v,
    load_sem, hop_send, s1_recv, s2_recv, y_send, y_recv, store_sem,
    rs_send, rs_recv, bc_send, bc_recv, ag_send, ag_recv,
):
    mx, my = lax.axis_index("mx"), lax.axis_index("my")
    x, zh = lax.rem(mx, 4), mx // 4
    y, zl, core = my // 4, lax.rem(my // 2, 2), lax.rem(my, 2)
    zz = zl * 2 + zh

    def device(px, py, pz, pc):
        return (lax.rem(pz, 2) * 4 + px, py * 4 + (pz // 2) * 2 + pc)

    def step(v, d):
        return lax.rem(v + d, 4)

    barrier = pltpu.get_barrier_semaphore()
    partners = [device(step(x, d), y, zz, core) for d in (1, 2, 3)]
    partners += [device(x, y, step(zz, d), core) for d in (1, 2, 3)]
    partners += [device(x, step(y, d), zz, c) for d in (1, 2, 3) for c in (0, 1)]
    partners += [device(step(x, d), y, zz, 1 - core) for d in range(4)]
    for p in partners:
        pl.semaphore_signal(barrier, inc=1, device_id=p, device_id_type=MESH)


    rows = (pl.ds(0, 3), pl.ds(3, 3), pl.ds(6, 6))
    loads = [pltpu.make_async_copy(slab.at[r], raw.at[r], load_sem.at[n]) for n, r in enumerate(rows)]
    bases = [pltpu.make_async_copy(b, bases_v.at[n], load_sem.at[3]) for n, b in enumerate((bxt, byt))]
    for c in loads + bases:
        c.start()

    def landed(ref, sem):
        pltpu.make_async_copy(ref, ref, sem).wait()

    lane = lax.broadcasted_iota(jnp.int32, (IB, 128), 1)

    def lanes(t, h):
        return pl.ds(STARTS[t][h] * 128, PARTS[t][h][1] * 128)

    def pack(t, h, px, pz, dst):
        first, count = PARTS[t][h]
        tiles = [None] * count
        base = {}
        for at, k, j, col, size in RUNS:
            d, w = at % 128, at // 128 - first
            if w >= count or at + size <= first * 128:
                continue
            if k not in base:
                base[k] = PAIR * ((lax.rem(pz, 2) * 4 + px) * 8 + step(y, AHEAD[k]) * 2 + pz // 2)
            off = base[k] + col
            t0 = off // 128
            t1 = jnp.minimum(t0 + 1, COLS // 128 - 1)
            s = off - t0 * 128
            sh = lax.rem(d - s + 128, 128)
            v0 = pltpu.roll(raw[j, :, pl.ds(pl.multiple_of(t0 * 128, 128), 128)], sh, 1)
            v1 = pltpu.roll(raw[j, :, pl.ds(pl.multiple_of(t1 * 128, 128), 128)], sh, 1)
            v = jnp.where(lax.rem(lane - d + 128, 128) < 128 - s, v0, v1)
            if w >= 0:
                tiles[w] = v if tiles[w] is None else jnp.where(lane < d, tiles[w], v)
            if d + size > 128 and w + 1 < count:
                tiles[w + 1] = v
        if first <= FILLED // 128 < first + count:
            w = FILLED // 128 - first
            tiles[w] = jnp.where(lane < FILLED % 128, tiles[w], 0.0)
        for w in range(count):
            lo = (STARTS[t][h] + w) * 128
            dst[:, lo : lo + 128] = tiles[w]

    def pack_a(t, px, dst):
        lax.fori_loop(0, 4, lambda pz, c: (pack(t, 0, px, pz, dst.at[pz]), c)[1], 0)

    def pack_b(t, pz, dst):
        lax.fori_loop(0, 4, lambda px, c: (pack(t, 1, px, pz, dst.at[px]), c)[1], 0)

    def remote(src, dst, ssem, rsem, dev):
        return pltpu.make_async_remote_copy(
            src_ref=src, dst_ref=dst, send_sem=ssem, recv_sem=rsem, device_id=dev, device_id_type=MESH
        )

    def first_copy(t, h, d):
        w = lanes(t, h)
        if h == 0:
            px = step(x, d)
            return remote(s1a.at[px, :, :, w], r1a.at[x, :, :, w], hop_send.at[0], s1_recv.at[t, 0], device(px, y, zz, core))
        pz = step(zz, d)
        return remote(s1b.at[pz, :, :, w], r1b.at[zz, :, :, w], hop_send.at[1], s1_recv.at[t, 1], device(x, y, pz, core))

    def send_a(t, d):
        px = step(x, d)
        pack_a(t, px, s1a.at[px])
        first_copy(t, 0, d).start()

    def send_b(t, d):
        pz = step(zz, d)
        pack_b(t, pz, s1b.at[pz])
        first_copy(t, 1, d).start()

    def first_hop(t, begun=False):
        def message(n, carry):
            d = 2 - n + 3 * (n // 2)
            send_a(t, d)
            send_b(t, d)
            return carry

        lax.fori_loop(1 if begun else 0, 3, message, 0)
        pack_a(t, x, r1a.at[x])
        pack_b(t, zz, r1b.at[zz])

    def second_hop(t):
        wa, wb = lanes(t, 0), lanes(t, 1)
        landed(r1a.at[0:3, :, :, wa], s1_recv.at[t, 0])
        landed(r1b.at[0:3, :, :, wb], s1_recv.at[t, 1])
        for d in (2, 1, 3):
            px, pz = step(x, d), step(zz, d)
            remote(r1a.at[:, pz, :, wa], g.at[0, zz, :, :, wa], hop_send.at[2], s2_recv.at[t, 0], device(x, y, pz, core)).start()
            remote(r1b.at[:, px, :, wb], g.at[1, :, x, :, wb], hop_send.at[3], s2_recv.at[t, 1], device(px, y, zz, core)).start()
        pltpu.make_async_copy(r1a.at[:, zz, :, wa], g.at[0, zz, :, :, wa], s2_recv.at[t, 0]).start()
        pltpu.make_async_copy(r1b.at[:, x, :, wb], g.at[1, :, x, :, wb], s2_recv.at[t, 1]).start()

    low = lax.broadcasted_iota(jnp.int32, (JB, 128), 1) < 64

    def project(t):
        both = [(h, v) for h in (0, 1) for v in (0, 1)]
        for group in (both,) if t > 3 else (both[:2], both[2:]):
            blocks = [g[h, v * 2 : v * 2 + 2, :, :, lanes(t, h)].reshape(MIDX, -1) for h, v in group]
            hi, lo = split(jnp.concatenate(blocks, axis=1))
            gxx[...] += dot(hi, hi, NT)
            gxm[...] += dot(hi, lo, NT)
            f = dot(bb[...], hi, NN)
            f = f[0:64] + (f[64:128] + dot(bb[0:64], lo, NN))
            f = jnp.concatenate([f, f], axis=0)
            at = 0
            for h, v in group:
                first, size = PARTS[t][h][0] * 128, PARTS[t][h][1] * 128
                ft[v, first : first + size, :] = f[:, at : at + size].T
                at += size

    def pair(k, c, row, gap, stride, at, n):
        def pairs(p, carry):
            for v in (0, 1):
                a = ft[v, pl.ds(row + p, JB, stride), :]
                b = ft[v, pl.ds(row + gap + p, JB, stride), :]
                fs[k, c, at + p, v * JB : (v + 1) * JB, :] = jnp.where(low, a, b)
            return carry

        lax.fori_loop(0, n, pairs, 0, unroll=True)

    def spread(k):
        py = step(y, AHEAD[k])
        for c in (0, 1):
            row = k * JB * PAIR + c * (OWN + LATE)
            pair(k, c, row, EP, PAIR, 0, EP)
            pair(k, c, k * JB * PAIR + (OWN if c else EARLY), LP, PAIR, EP, LP)
            remote(fs.at[k, c], fr.at[y, core], y_send.at[0], y_recv.at[k], device(x, py, zz, c)).start()

    def swap(part):
        k, c = CHUNKS - 1, 1 - core
        at, n = ((0, EP), (EP, LP))[part]
        w = pl.ds(at, n)

        def collect(i):
            row = SECOND + i * LATE if part else FIRST + i * EARLY
            pair(k, i, row, n, 2 * (LATE if part else EARLY), at, n)

        collect(c)
        remote(fs.at[k, c, w], fr.at[y, core, w], y_send.at[1], y_recv.at[k + part], device(x, y, zz, c)).start()
        collect(core)
        pltpu.make_async_copy(fs.at[k, core, w], fr.at[y, core, w], y_recv.at[k + part]).start()

    def chunk(t):
        landed(g.at[0, :, :, :, lanes(t, 0)], s2_recv.at[t, 0])
        landed(g.at[1, :, :, :, lanes(t, 1)], s2_recv.at[t, 1])
        project(t)

    eights = [(d, e) for d in (2, 1, 3, 0) for e in (1, 0)]
    sixteens = [(d, e) for d in (2, 1, 3, 0) for e in (2, 1, 3, 0)]
    left = lax.broadcasted_iota(jnp.int32, (64, 128), 1) < 64

    def own_rows(px, pc):
        return pl.ds(pl.multiple_of((px * 2 + pc) * 24, 24), 24)

    def scatter(i, main, cross, scale):
        m = cross[...]
        main[...] = (main[...] + (m + m.T)) * scale
        part[i, 0:64] = main[0:64, 0:128]
        high = jnp.concatenate([main[64:128, 128:192], jnp.zeros((64, 64), F32)], axis=1)
        part[i, 64:128] = jnp.where(left, pltpu.roll(main[64:128, 0:128], 64, 1), pltpu.roll(high, 64, 1))
        top = jnp.concatenate([main[0:64, 128:192], jnp.zeros((64, 64), F32)], axis=1)
        end = jnp.concatenate([main[128:192, 128:192], jnp.zeros((64, 64), F32)], axis=1)
        part[i, 128:192] = jnp.where(left, top, pltpu.roll(end, 64, 1))
        for d, e in eights:
            if d or e:
                px, pc = step(x, d), lax.rem(core + e, 2)
                remote(part.at[i, own_rows(px, pc)], parts8.at[i, d * 2 + e - 1], rs_send.at[i], rs_recv.at[i], device(px, y, zz, pc)).start()

    def share(i):
        landed(parts8.at[i], rs_recv.at[i])
        total = part[i, own_rows(x, core)]
        for n in range(7):
            total += parts8[i, n]
        sums[i] = total

    def spread_yz(i):
        parts16[i, y * 4 + zz] = sums[i]
        for d, e in sixteens:
            if d or e:
                remote(sums.at[i], parts16.at[i, y * 4 + zz], bc_send.at[i], bc_recv.at[i], device(x, step(y, d), step(zz, e), core)).start()

    def gather_yz(i):
        landed(parts16.at[i, 0:15], bc_recv.at[i])
        total = parts16[i, 0]
        for n in range(1, 16):
            total += parts16[i, n]
        return total

    def publish(i, total):
        full[i, own_rows(x, core)] = total
        for d, e in eights:
            if d or e:
                px, pc = step(x, d), lax.rem(core + e, 2)
                remote(full.at[i, own_rows(x, core)], full.at[i, own_rows(x, core)], ag_send.at[i], ag_recv.at[i], device(px, y, zz, pc)).start()

    def columns(at, n):
        parts = []
        for p in range(n):
            rows = []
            for s in range(4):
                a, b = fr[s, 0, at + p], fr[s, 1, at + p]
                rows += [a[:JB], b[:JB], a[JB:], b[JB:]]
            parts.append(jnp.concatenate(rows, axis=0))
        return split(jnp.concatenate(parts, axis=1))

    def gram(at, n):
        hi, lo = columns(at, n)
        gyy[...] += dot(hi, hi, NT)
        gym[...] += dot(hi, lo, NT)

    wide = 5

    def finish(u, carry):
        hi, lo = columns(u * wide, wide)
        c = dot(bq[...], hi, NN)
        c = c[0:64] + (c[64:128] + dot(bq[0:64], lo, NN))
        for p in range(wide):
            core_v[u * wide + p] = c[:, p * 128 : (p + 1) * 128]
        return carry

    loads[0].wait()
    pack_a(0, step(x, 2), s1a.at[step(x, 2)])
    loads[1].wait()
    pack_b(0, step(zz, 2), s1b.at[step(zz, 2)])
    pl.semaphore_wait(barrier, len(partners))
    first_copy(0, 0, 2).start()
    first_copy(0, 1, 2).start()
    first_hop(0, True)
    loads[2].wait()
    first_hop(1)
    first_hop(2)
    landed(bases_v, load_sem.at[3])
    for n, ref in enumerate((bb, bq)):
        hi, lo = split(jnp.concatenate([bases_v[n], jnp.zeros((64 - RANK, MIDX), F32)], axis=0))
        ref[0:64] = hi
        ref[64:128] = lo
    for acc in (gxx, gxm, gyy, gym):
        acc[...] = jnp.zeros_like(acc)
    second_hop(0)
    second_hop(1)
    first_hop(3)
    second_hop(2)
    chunk(0)
    chunk(1)
    spread(0)
    second_hop(3)
    first_hop(4)
    first_hop(5)
    chunk(2)
    spread(1)
    chunk(3)
    spread(2)
    second_hop(4)
    second_hop(5)
    chunk(4)
    swap(0)
    chunk(5)
    scatter(0, gxx, gxm, 1.0 / (MIDY * COLS))
    swap(1)

    for k in range(CHUNKS - 1):
        landed(fr.at[0], y_recv.at[k])
    landed(fr.at[0, :, 0:EP], y_recv.at[CHUNKS - 1])
    gram(0, 6)
    gram(6, 6)
    gram(12, 5)
    landed(fr.at[0, :, EP:HP], y_recv.at[CHUNKS])
    gram(EP, LP)
    scatter(1, gyy, gym, 1.0 / (RANK * COLS))
    share(0)
    spread_yz(0)
    share(1)
    spread_yz(1)
    lax.fori_loop(0, HP // wide, finish, 0)
    core_store = pltpu.make_async_copy(core_v, core_out, store_sem.at[0])
    core_store.start()
    publish(0, gather_yz(0))
    publish(1, gather_yz(1))
    landed(s1a.at[0:3], hop_send.at[0])
    landed(s1b.at[0:3], hop_send.at[1])
    landed(r1a.at[0:3], hop_send.at[2])
    landed(r1b.at[0:3], hop_send.at[3])
    landed(fs.at[0:3], y_send.at[0])
    landed(fs.at[3, 0], y_send.at[1])
    for i in (0, 1):
        landed(parts8.at[i], rs_send.at[i])
        landed(parts16.at[i, 0:15], bc_send.at[i])
    core_store.wait()
    for i in (0, 1):
        landed(full.at[i, 0:168], ag_recv.at[i])
    store = pltpu.make_async_copy(full, full_out, store_sem.at[1])
    store.start()
    for i in (0, 1):
        landed(full.at[i, 0:168], ag_send.at[i])
    store.wait()


def unfold(full, core, gx_out, gy_out, core_out):
    left = lax.broadcasted_iota(jnp.int32, (64, 128), 1) < 64
    for i, ref in enumerate((gx_out, gy_out)):
        p0, p1, p2 = full[i, 0:64], full[i, 64:128], full[i, 128:192]
        t0 = full[i, 0:128].T
        t2 = jnp.concatenate([p2, p2], axis=0).T
        q1, q2 = pltpu.roll(p1, 64, 1), pltpu.roll(p2, 64, 1)
        ref[0:64, 0:128] = p0
        ref[0:64, 128:192] = p2[:, :64]
        ref[64:128, 0:128] = jnp.where(left, t0[64:128], q1)
        ref[64:128, 128:192] = q1[:, :64]
        ref[128:192, 0:128] = jnp.where(left, t2[0:64], t0[64:128])
        ref[128:192, 128:192] = q2[:, :64]
    odd = lax.rem(lax.axis_index("my"), 2)
    for p in range(HP):
        v = core[p]
        first, gap = (LATE * odd + p, EP) if p < EP else (EARLY * (1 - odd) + p - EP, LP)
        core_out[first] = v[:RANK, :RANK]
        core_out[first + gap] = pltpu.roll(v, 64, 1)[:RANK, :RANK]


def body(slab, basis_x, basis_y):
    anywhere = pl.BlockSpec(memory_space=pl.ANY)
    vmem = pl.BlockSpec(memory_space=pltpu.VMEM)
    full, core = pl.pallas_call(
        kernel,
        out_shape=(
            jax.ShapeDtypeStruct((2, 192, 128), F32),
            jax.ShapeDtypeStruct((HP, 64, 128), F32),
        ),
        in_specs=[anywhere] * 3,
        out_specs=(anywhere, anywhere),
        scratch_shapes=[
            pltpu.VMEM((JB, IB, COLS), F32),
            pltpu.VMEM((4, 4, IB, LANES), F32),
            pltpu.VMEM((4, 4, IB, LANES), F32),
            pltpu.VMEM((4, 4, IB, LANES), F32),
            pltpu.VMEM((4, 4, IB, LANES), F32),
            pltpu.VMEM((2, 4, 4, IB, LANES), F32),
            pltpu.VMEM((2, TILES * 128, 128), F32),
            pltpu.VMEM((CHUNKS, 2, HP, 2 * JB, 128), F32),
            pltpu.VMEM((4, 2, HP, 2 * JB, 128), F32),
            pltpu.VMEM((2, RANK, MIDX), F32),
            pltpu.VMEM((128, MIDX), BF16),
            pltpu.VMEM((128, MIDY), BF16),
            pltpu.VMEM((MIDX, MIDX), F32),
            pltpu.VMEM((MIDX, MIDX), F32),
            pltpu.VMEM((MIDY, MIDY), F32),
            pltpu.VMEM((MIDY, MIDY), F32),
            pltpu.VMEM((2, 192, 128), F32),
            pltpu.VMEM((2, 7, 24, 128), F32),
            pltpu.VMEM((2, 24, 128), F32),
            pltpu.VMEM((2, 16, 24, 128), F32),
            pltpu.VMEM((2, 192, 128), F32),
            pltpu.VMEM((HP, 64, 128), F32),
            pltpu.SemaphoreType.DMA((4,)),
            pltpu.SemaphoreType.DMA((4,)),
            pltpu.SemaphoreType.DMA((len(PARTS), 2)),
            pltpu.SemaphoreType.DMA((len(PARTS), 2)),
            pltpu.SemaphoreType.DMA((2,)),
            pltpu.SemaphoreType.DMA((CHUNKS + 1,)),
            pltpu.SemaphoreType.DMA((2,)),
            pltpu.SemaphoreType.DMA((2,)),
            pltpu.SemaphoreType.DMA((2,)),
            pltpu.SemaphoreType.DMA((2,)),
            pltpu.SemaphoreType.DMA((2,)),
            pltpu.SemaphoreType.DMA((2,)),
            pltpu.SemaphoreType.DMA((2,)),
        ],
        compiler_params=pltpu.CompilerParams(
            collective_id=0, has_side_effects=True, vmem_limit_bytes=58 * 2**20
        ),
    )(jnp.transpose(slab, (1, 0, 2)), basis_x.T, basis_y.T)
    gx, gy, core = pl.pallas_call(
        unfold,
        out_shape=(
            jax.ShapeDtypeStruct((MIDX, MIDX), F32),
            jax.ShapeDtypeStruct((MIDY, MIDY), F32),
            jax.ShapeDtypeStruct((OWN, RANK, RANK), F32),
        ),
        in_specs=[vmem, vmem],
        out_specs=(vmem, vmem, vmem),
    )(full, core)
    return gx, gy, jnp.transpose(core, (1, 2, 0))


def solution(mesh):
    return jax.shard_map(
        body,
        mesh=mesh,
        in_specs=(P("mx", "my", None), P(), P()),
        out_specs=(P(), P(), P(None, None, ("mx", "my"))),
        check_vma=False,
    )
```

```python
import jax
import jax.numpy as jnp
from jax import lax
from jax.experimental import pallas as pl
from jax.experimental.pallas import tpu as pltpu
from jax.sharding import PartitionSpec as P

MESH = pl.DeviceIdType.MESH
F32 = jnp.float32
BF16 = jnp.bfloat16

MIDX = 192
MIDY = 192
RANK = 60
COLS = 6400
JB = 12
IB = 24
OWN = 50
PAIR = 2 * OWN
HP = OWN // 2
CHUNKS = 4
AHEAD = (2, 1, 3, 0)
EARLY, LATE = 34, 16
EP, LP = EARLY // 2, LATE // 2
RUNS = [(k * JB * PAIR + j * PAIR, k, j, 0, PAIR) for k in range(CHUNKS - 1) for j in range(JB)]
FIRST = (CHUNKS - 1) * JB * PAIR
RUNS += [(FIRST + (2 * j + i) * EARLY, CHUNKS - 1, j, i * (PAIR - EARLY), EARLY) for j in range(JB) for i in (0, 1)]
FILLED = FIRST + 2 * JB * EARLY
SECOND = -(-FILLED // 128) * 128
RUNS += [(SECOND + j * 2 * LATE, CHUNKS - 1, j, EARLY, 2 * LATE) for j in range(JB)]
PARTS = (
    ((0, 2), (2, 2)), ((4, 3), (7, 3)), ((10, 5), (15, 5)),
    ((20, 5), (25, 4)), ((29, 3), (32, 3)), ((35, 1), (36, 2)),
)
TILES = 38
LANES = TILES // 2 * 128
STARTS = ((0, 0), (2, 2), (5, 5), (10, 10), (15, 14), (18, 17))

NT = (((1,), (1,)), ((), ()))
NN = (((1,), (0,)), ((), ()))


def split(a):
    hi = a.astype(BF16)
    return hi, (a - hi.astype(F32)).astype(BF16)


def dot(a, b, dims):
    return lax.dot_general(a, b, dims, preferred_element_type=F32)


def kernel(
    slab, bxt, byt, full_out, core_out,
    raw, s1a, s1b, r1a, r1b, g, ft, fs, fr, bases_v, bb, bq, gxx, gxm, gyy, gym,
    part, parts8, sums, parts16, done, core_v,
    load_sem, hop_send, s1_recv, s2_recv, y_send, y_recv, store_sem,
    sum_send, rs_recv, bc_recv, ag_recv,
):
    mx, my = lax.axis_index("mx"), lax.axis_index("my")
    x, zh = lax.rem(mx, 4), mx // 4
    y, zl, core = my // 4, lax.rem(my // 2, 2), lax.rem(my, 2)
    zz = zl * 2 + zh

    def device(px, py, pz, pc):
        return (lax.rem(pz, 2) * 4 + px, py * 4 + (pz // 2) * 2 + pc)

    def step(v, d):
        return lax.rem(v + d, 4)

    barrier = pltpu.get_barrier_semaphore()
    partners = [device(step(x, d), y, zz, core) for d in (1, 2, 3)]
    partners += [device(x, y, step(zz, d), core) for d in (1, 2, 3)]
    partners += [device(x, step(y, d), zz, c) for d in (1, 2, 3) for c in (0, 1)]
    partners += [device(step(x, d), y, zz, 1 - core) for d in range(4)]
    for p in partners:
        pl.semaphore_signal(barrier, inc=1, device_id=p, device_id_type=MESH)


    rows = (pl.ds(0, 3), pl.ds(3, 3), pl.ds(6, 6))
    loads = [pltpu.make_async_copy(slab.at[r], raw.at[r], load_sem.at[n]) for n, r in enumerate(rows)]
    bases = [pltpu.make_async_copy(b, bases_v.at[n], load_sem.at[3]) for n, b in enumerate((bxt, byt))]
    for c in loads + bases:
        c.start()

    def landed(ref, sem):
        pltpu.make_async_copy(ref, ref, sem).wait()

    lane = lax.broadcasted_iota(jnp.int32, (IB, 128), 1)

    def lanes(t, h):
        return pl.ds(STARTS[t][h] * 128, PARTS[t][h][1] * 128)

    def whole(t):
        return pl.ds(0, (PARTS[t][0][1] + PARTS[t][1][1]) * 128)

    def pack(t, h, px, pz, dst):
        first, count = PARTS[t][h]
        tiles = [None] * count
        base = {}
        for at, k, j, col, size in RUNS:
            d, w = at % 128, at // 128 - first
            if w >= count or at + size <= first * 128:
                continue
            if k not in base:
                base[k] = PAIR * ((lax.rem(pz, 2) * 4 + px) * 8 + step(y, AHEAD[k]) * 2 + pz // 2)
            off = base[k] + col
            t0 = off // 128
            t1 = jnp.minimum(t0 + 1, COLS // 128 - 1)
            s = off - t0 * 128
            sh = lax.rem(d - s + 128, 128)
            v0 = pltpu.roll(raw[j, :, pl.ds(pl.multiple_of(t0 * 128, 128), 128)], sh, 1)
            v1 = pltpu.roll(raw[j, :, pl.ds(pl.multiple_of(t1 * 128, 128), 128)], sh, 1)
            v = jnp.where(lax.rem(lane - d + 128, 128) < 128 - s, v0, v1)
            if w >= 0:
                tiles[w] = v if tiles[w] is None else jnp.where(lane < d, tiles[w], v)
            if d + size > 128 and w + 1 < count:
                tiles[w + 1] = v
        if first <= FILLED // 128 < first + count:
            w = FILLED // 128 - first
            tiles[w] = jnp.where(lane < FILLED % 128, tiles[w], 0.0)
        for w in range(count):
            lo = (STARTS[t][h] + w) * 128
            dst[:, lo : lo + 128] = tiles[w]

    def pack_a(t, px, dst):
        lax.fori_loop(0, 4, lambda pz, c: (pack(t, 0, px, pz, dst.at[pz]), c)[1], 0)

    def pack_b(t, pz, dst):
        lax.fori_loop(0, 4, lambda px, c: (pack(t, 1, px, pz, dst.at[px]), c)[1], 0)

    def remote(src, dst, ssem, rsem, dev):
        return pltpu.make_async_remote_copy(
            src_ref=src, dst_ref=dst, send_sem=ssem, recv_sem=rsem, device_id=dev, device_id_type=MESH
        )

    def first_copy(t, h, d):
        w = lanes(t, h)
        if h == 0:
            px = step(x, d)
            return remote(s1a.at[px, :, :, w], r1a.at[x, :, :, w], hop_send.at[0], s1_recv.at[t], device(px, y, zz, core))
        pz = step(zz, d)
        return remote(s1b.at[pz, :, :, w], r1b.at[zz, :, :, w], hop_send.at[0], s1_recv.at[t], device(x, y, pz, core))

    def send_a(t, d):
        px = step(x, d)
        pack_a(t, px, s1a.at[px])
        first_copy(t, 0, d).start()

    def send_b(t, d):
        pz = step(zz, d)
        pack_b(t, pz, s1b.at[pz])
        first_copy(t, 1, d).start()

    def first_hop(t, begun=False):
        def message(n, carry):
            d = 2 - n + 3 * (n // 2)
            send_a(t, d)
            send_b(t, d)
            return carry

        lax.fori_loop(1 if begun else 0, 3, message, 0)
        pack_a(t, x, r1a.at[x])
        pack_b(t, zz, r1b.at[zz])

    def second_hop(t):
        wa, wb = lanes(t, 0), lanes(t, 1)
        landed(r1a.at[0:3, :, :, whole(t)], s1_recv.at[t])
        for d in (2, 1, 3):
            px, pz = step(x, d), step(zz, d)
            remote(r1a.at[:, pz, :, wa], g.at[0, zz, :, :, wa], hop_send.at[1], s2_recv.at[t], device(x, y, pz, core)).start()
            remote(r1b.at[:, px, :, wb], g.at[1, :, x, :, wb], hop_send.at[1], s2_recv.at[t], device(px, y, zz, core)).start()
        pltpu.make_async_copy(r1a.at[:, zz, :, wa], g.at[0, zz, :, :, wa], s2_recv.at[t]).start()
        pltpu.make_async_copy(r1b.at[:, x, :, wb], g.at[1, :, x, :, wb], s2_recv.at[t]).start()

    low = lax.broadcasted_iota(jnp.int32, (JB, 128), 1) < 64

    def project(t):
        both = [(h, v) for h in (0, 1) for v in (0, 1)]
        for group in (both,) if t > 3 else (both[:2], both[2:]):
            blocks = [g[h, v * 2 : v * 2 + 2, :, :, lanes(t, h)].reshape(MIDX, -1) for h, v in group]
            hi, lo = split(jnp.concatenate(blocks, axis=1))
            gxx[...] += dot(hi, hi, NT)
            gxm[...] += dot(hi, lo, NT)
            f = dot(bb[...], hi, NN)
            f = f[0:64] + (f[64:128] + dot(bb[0:64], lo, NN))
            f = jnp.concatenate([f, f], axis=0)
            at = 0
            for h, v in group:
                first, size = PARTS[t][h][0] * 128, PARTS[t][h][1] * 128
                ft[v, first : first + size, :] = f[:, at : at + size].T
                at += size

    def pair(k, c, row, gap, stride, at, n):
        def pairs(p, carry):
            for v in (0, 1):
                a = ft[v, pl.ds(row + p, JB, stride), :]
                b = ft[v, pl.ds(row + gap + p, JB, stride), :]
                fs[k, c, at + p, v * JB : (v + 1) * JB, :] = jnp.where(low, a, b)
            return carry

        lax.fori_loop(0, n, pairs, 0, unroll=True)

    def spread(k):
        py = step(y, AHEAD[k])
        for c in (0, 1):
            row = k * JB * PAIR + c * (OWN + LATE)
            pair(k, c, row, EP, PAIR, 0, EP)
            pair(k, c, k * JB * PAIR + (OWN if c else EARLY), LP, PAIR, EP, LP)
            remote(fs.at[k, c], fr.at[y, core], y_send, y_recv.at[k], device(x, py, zz, c)).start()

    def swap(part):
        k, c = CHUNKS - 1, 1 - core
        at, n = ((0, EP), (EP, LP))[part]
        w = pl.ds(at, n)

        def collect(i):
            row = SECOND + i * LATE if part else FIRST + i * EARLY
            pair(k, i, row, n, 2 * (LATE if part else EARLY), at, n)

        collect(c)
        remote(fs.at[k, c, w], fr.at[y, core, w], y_send, y_recv.at[k + part], device(x, y, zz, c)).start()
        collect(core)
        pltpu.make_async_copy(fs.at[k, core, w], fr.at[y, core, w], y_recv.at[k + part]).start()

    def chunk(t):
        landed(g.at[0, :, :, :, whole(t)], s2_recv.at[t])
        project(t)

    eights = [(d, e) for d in (2, 1, 3, 0) for e in (1, 0)]
    sixteens = [(d, e) for d in (2, 1, 3, 0) for e in (2, 1, 3, 0)]
    left = lax.broadcasted_iota(jnp.int32, (64, 128), 1) < 64

    def own_rows(px, pc):
        return pl.ds(pl.multiple_of((px * 2 + pc) * 24, 24), 24)

    def scatter(i, main, cross, scale):
        m = cross[...]
        main[...] = (main[...] + (m + m.T)) * scale
        part[i, 0:64] = main[0:64, 0:128]
        high = jnp.concatenate([main[64:128, 128:192], jnp.zeros((64, 64), F32)], axis=1)
        part[i, 64:128] = jnp.where(left, pltpu.roll(main[64:128, 0:128], 64, 1), pltpu.roll(high, 64, 1))
        top = jnp.concatenate([main[0:64, 128:192], jnp.zeros((64, 64), F32)], axis=1)
        end = jnp.concatenate([main[128:192, 128:192], jnp.zeros((64, 64), F32)], axis=1)
        part[i, 128:192] = jnp.where(left, top, pltpu.roll(end, 64, 1))
        for d, e in eights:
            if d or e:
                px, pc = step(x, d), lax.rem(core + e, 2)
                remote(part.at[i, own_rows(px, pc)], parts8.at[i, d * 2 + e - 1], sum_send, rs_recv.at[i], device(px, y, zz, pc)).start()

    def share(i):
        landed(parts8.at[i], rs_recv.at[i])
        total = part[i, own_rows(x, core)]
        for n in range(7):
            total += parts8[i, n]
        sums[i] = total

    def spread_yz(i):
        parts16[i, y * 4 + zz] = sums[i]
        for d, e in sixteens:
            if d or e:
                remote(sums.at[i], parts16.at[i, y * 4 + zz], sum_send, bc_recv.at[i], device(x, step(y, d), step(zz, e), core)).start()

    def gather_yz(i):
        landed(parts16.at[i, 0:15], bc_recv.at[i])
        total = parts16[i, 0]
        for n in range(1, 16):
            total += parts16[i, n]
        return total

    def publish(i, total):
        done[i] = total
        mine = full_out.at[i, own_rows(x, core)]
        for d, e in eights:
            if d or e:
                px, pc = step(x, d), lax.rem(core + e, 2)
                remote(done.at[i], mine, sum_send, ag_recv.at[i], device(px, y, zz, pc)).start()
        pltpu.make_async_copy(done.at[i], mine, ag_recv.at[i]).start()

    def columns(at, n):
        parts = []
        for p in range(n):
            rows = []
            for s in range(4):
                a, b = fr[s, 0, at + p], fr[s, 1, at + p]
                rows += [a[:JB], b[:JB], a[JB:], b[JB:]]
            parts.append(jnp.concatenate(rows, axis=0))
        return split(jnp.concatenate(parts, axis=1))

    def gram(at, n):
        hi, lo = columns(at, n)
        gyy[...] += dot(hi, hi, NT)
        gym[...] += dot(hi, lo, NT)

    wide = 5

    def finish(u, carry):
        hi, lo = columns(u * wide, wide)
        c = dot(bq[...], hi, NN)
        c = c[0:64] + (c[64:128] + dot(bq[0:64], lo, NN))
        for p in range(wide):
            core_v[u * wide + p] = c[:, p * 128 : (p + 1) * 128]
        return carry

    loads[0].wait()
    pack_a(0, step(x, 2), s1a.at[step(x, 2)])
    loads[1].wait()
    pack_b(0, step(zz, 2), s1b.at[step(zz, 2)])
    pl.semaphore_wait(barrier, len(partners))
    first_copy(0, 0, 2).start()
    first_copy(0, 1, 2).start()
    first_hop(0, True)
    loads[2].wait()
    first_hop(1)
    first_hop(2)
    landed(bases_v, load_sem.at[3])
    for n, ref in enumerate((bb, bq)):
        hi, lo = split(jnp.concatenate([bases_v[n], jnp.zeros((64 - RANK, MIDX), F32)], axis=0))
        ref[0:64] = hi
        ref[64:128] = lo
    for acc in (gxx, gxm, gyy, gym):
        acc[...] = jnp.zeros_like(acc)
    second_hop(0)
    second_hop(1)
    first_hop(3)
    second_hop(2)
    chunk(0)
    chunk(1)
    spread(0)
    second_hop(3)
    first_hop(4)
    first_hop(5)
    chunk(2)
    spread(1)
    chunk(3)
    spread(2)
    second_hop(4)
    second_hop(5)
    chunk(4)
    swap(0)
    chunk(5)
    scatter(0, gxx, gxm, 1.0 / (MIDY * COLS))
    swap(1)

    for k in range(CHUNKS - 1):
        landed(fr.at[0], y_recv.at[k])
    landed(fr.at[0, :, 0:EP], y_recv.at[CHUNKS - 1])
    gram(0, 6)
    gram(6, 6)
    gram(12, 5)
    landed(fr.at[0, :, EP:HP], y_recv.at[CHUNKS])
    gram(EP, LP)
    scatter(1, gyy, gym, 1.0 / (RANK * COLS))
    share(0)
    spread_yz(0)
    share(1)
    spread_yz(1)
    lax.fori_loop(0, HP // wide, finish, 0)
    core_store = pltpu.make_async_copy(core_v, core_out, store_sem)
    core_store.start()
    publish(0, gather_yz(0))
    publish(1, gather_yz(1))
    landed(g.at[:, 0:3], hop_send.at[0])
    landed(g.at[:, 0:3], hop_send.at[1])
    landed(ft.at[0, 0 : 7 * HP * 2 * JB], y_send)
    core_store.wait()
    for i in (0, 1):
        landed(full_out.at[i], ag_recv.at[i])
    landed(ft.at[0, 0 : 2 * (7 + 15 + 7) * 24], sum_send)


def unfold(full, core, gx_out, gy_out, core_out):
    left = lax.broadcasted_iota(jnp.int32, (64, 128), 1) < 64
    for i, ref in enumerate((gx_out, gy_out)):
        p0, p1, p2 = full[i, 0:64], full[i, 64:128], full[i, 128:192]
        t0 = full[i, 0:128].T
        t2 = jnp.concatenate([p2, p2], axis=0).T
        q1, q2 = pltpu.roll(p1, 64, 1), pltpu.roll(p2, 64, 1)
        ref[0:64, 0:128] = p0
        ref[0:64, 128:192] = p2[:, :64]
        ref[64:128, 0:128] = jnp.where(left, t0[64:128], q1)
        ref[64:128, 128:192] = q1[:, :64]
        ref[128:192, 0:128] = jnp.where(left, t2[0:64], t0[64:128])
        ref[128:192, 128:192] = q2[:, :64]
    odd = lax.rem(lax.axis_index("my"), 2)
    for p in range(HP):
        v = core[p]
        first, gap = (LATE * odd + p, EP) if p < EP else (EARLY * (1 - odd) + p - EP, LP)
        core_out[first] = v[:RANK, :RANK]
        core_out[first + gap] = pltpu.roll(v, 64, 1)[:RANK, :RANK]


def body(slab, basis_x, basis_y):
    anywhere = pl.BlockSpec(memory_space=pl.ANY)
    vmem = pl.BlockSpec(memory_space=pltpu.VMEM)
    full, core = pl.pallas_call(
        kernel,
        out_shape=(
            jax.ShapeDtypeStruct((2, 192, 128), F32),
            jax.ShapeDtypeStruct((HP, 64, 128), F32),
        ),
        in_specs=[anywhere] * 3,
        out_specs=(anywhere, anywhere),
        scratch_shapes=[
            pltpu.VMEM((JB, IB, COLS), F32),
            pltpu.VMEM((4, 4, IB, LANES), F32),
            pltpu.VMEM((4, 4, IB, LANES), F32),
            pltpu.VMEM((4, 4, IB, LANES), F32),
            pltpu.VMEM((4, 4, IB, LANES), F32),
            pltpu.VMEM((2, 4, 4, IB, LANES), F32),
            pltpu.VMEM((2, TILES * 128, 128), F32),
            pltpu.VMEM((CHUNKS, 2, HP, 2 * JB, 128), F32),
            pltpu.VMEM((4, 2, HP, 2 * JB, 128), F32),
            pltpu.VMEM((2, RANK, MIDX), F32),
            pltpu.VMEM((128, MIDX), BF16),
            pltpu.VMEM((128, MIDY), BF16),
            pltpu.VMEM((MIDX, MIDX), F32),
            pltpu.VMEM((MIDX, MIDX), F32),
            pltpu.VMEM((MIDY, MIDY), F32),
            pltpu.VMEM((MIDY, MIDY), F32),
            pltpu.VMEM((2, 192, 128), F32),
            pltpu.VMEM((2, 7, 24, 128), F32),
            pltpu.VMEM((2, 24, 128), F32),
            pltpu.VMEM((2, 16, 24, 128), F32),
            pltpu.VMEM((2, 24, 128), F32),
            pltpu.VMEM((HP, 64, 128), F32),
            pltpu.SemaphoreType.DMA((4,)),
            pltpu.SemaphoreType.DMA((2,)),
            pltpu.SemaphoreType.DMA((len(PARTS),)),
            pltpu.SemaphoreType.DMA((len(PARTS),)),
            pltpu.SemaphoreType.DMA,
            pltpu.SemaphoreType.DMA((CHUNKS + 1,)),
            pltpu.SemaphoreType.DMA,
            pltpu.SemaphoreType.DMA,
            pltpu.SemaphoreType.DMA((2,)),
            pltpu.SemaphoreType.DMA((2,)),
            pltpu.SemaphoreType.DMA((2,)),
        ],
        compiler_params=pltpu.CompilerParams(
            collective_id=0, has_side_effects=True, vmem_limit_bytes=58 * 2**20
        ),
    )(jnp.transpose(slab, (1, 0, 2)), basis_x.T, basis_y.T)
    gx, gy, core = pl.pallas_call(
        unfold,
        out_shape=(
            jax.ShapeDtypeStruct((MIDX, MIDX), F32),
            jax.ShapeDtypeStruct((MIDY, MIDY), F32),
            jax.ShapeDtypeStruct((OWN, RANK, RANK), F32),
        ),
        in_specs=[vmem, vmem],
        out_specs=(vmem, vmem, vmem),
    )(full, core)
    return gx, gy, jnp.transpose(core, (1, 2, 0))


def solution(mesh):
    return jax.shard_map(
        body,
        mesh=mesh,
        in_specs=(P("mx", "my", None), P(), P()),
        out_specs=(P(), P(), P(None, None, ("mx", "my"))),
        check_vma=False,
    )
```

```python
import jax
import jax.numpy as jnp
from jax import lax
from jax.experimental import pallas as pl
from jax.experimental.pallas import tpu as pltpu
from jax.sharding import PartitionSpec as P

MESH = pl.DeviceIdType.MESH
F32 = jnp.float32
BF16 = jnp.bfloat16

MIDX = 192
MIDY = 192
RANK = 60
COLS = 6400
JB = 12
IB = 24
OWN = 50
PAIR = 2 * OWN
HP = OWN // 2
CHUNKS = 4
AHEAD = (2, 1, 3, 0)
EARLY, LATE = 34, 16
EP, LP = EARLY // 2, LATE // 2
RUNS = [(k * JB * PAIR + j * PAIR, k, j, 0, PAIR) for k in range(CHUNKS - 1) for j in range(JB)]
FIRST = (CHUNKS - 1) * JB * PAIR
RUNS += [(FIRST + (2 * j + i) * EARLY, CHUNKS - 1, j, i * (PAIR - EARLY), EARLY) for j in range(JB) for i in (0, 1)]
FILLED = FIRST + 2 * JB * EARLY
SECOND = -(-FILLED // 128) * 128
RUNS += [(SECOND + j * 2 * LATE, CHUNKS - 1, j, EARLY, 2 * LATE) for j in range(JB)]
PARTS = (
    ((0, 2), (2, 2)), ((4, 3), (7, 3)), ((10, 5), (15, 5)),
    ((20, 5), (25, 4)), ((29, 3), (32, 3)), ((35, 1), (36, 2)),
)
TILES = 38
LANES = TILES // 2 * 128
FOLDED = 4
STARTS = ((0, 0), (2, 2), (5, 5), (10, 10), (15, 14), (18, 17))

NT = (((1,), (1,)), ((), ()))
NN = (((1,), (0,)), ((), ()))


def split(a):
    hi = a.astype(BF16)
    return hi, (a - hi.astype(F32)).astype(BF16)


def dot(a, b, dims):
    return lax.dot_general(a, b, dims, preferred_element_type=F32)


def kernel(
    slab, bxt, byt, full_out, core_out,
    raw, s1a, s1b, r1a, r1b, g, s1f, r1f, s2f, gf, ft, fs, fr, bases_v, bb, bq, gxx, gxm, gyy, gym,
    part, parts8, sums, parts16, done, core_v,
    load_sem, hop_send, fold_sem, s1_recv, s2_recv, y_send, y_recv, store_sem,
    sum_send, rs_recv, bc_recv, ag_recv,
):
    mx, my = lax.axis_index("mx"), lax.axis_index("my")
    x, zh = lax.rem(mx, 4), mx // 4
    y, zl, core = my // 4, lax.rem(my // 2, 2), lax.rem(my, 2)
    zz = zl * 2 + zh

    def device(px, py, pz, pc):
        return (lax.rem(pz, 2) * 4 + px, py * 4 + (pz // 2) * 2 + pc)

    def step(v, d):
        return lax.rem(v + d, 4)

    barrier = pltpu.get_barrier_semaphore()
    partners = [device(step(x, d), y, zz, core) for d in (1, 2, 3)]
    partners += [device(x, y, step(zz, d), core) for d in (1, 2, 3)]
    partners += [device(x, step(y, d), zz, c) for d in (1, 2, 3) for c in (0, 1)]
    partners += [device(step(x, d), y, zz, 1 - core) for d in range(4)]
    for p in partners:
        pl.semaphore_signal(barrier, inc=1, device_id=p, device_id_type=MESH)


    rows = (pl.ds(0, 3), pl.ds(3, 3), pl.ds(6, 6))
    loads = [pltpu.make_async_copy(slab.at[r], raw.at[r], load_sem.at[n]) for n, r in enumerate(rows)]
    bases = [pltpu.make_async_copy(b, bases_v.at[n], load_sem.at[3]) for n, b in enumerate((bxt, byt))]
    for c in loads + bases:
        c.start()

    def landed(ref, sem):
        pltpu.make_async_copy(ref, ref, sem).wait()

    lane = lax.broadcasted_iota(jnp.int32, (IB, 128), 1)

    def held(t, h):
        return pl.ds(STARTS[t][h] * 128, PARTS[t][h][1] * 128)

    def tiles_sent(t, h):
        return PARTS[t][h][1] - ((t, h) == (FOLDED, 1))

    def lanes(t, h):
        return pl.ds(STARTS[t][h] * 128, tiles_sent(t, h) * 128)

    fold_tile = pl.ds((STARTS[FOLDED][1] + tiles_sent(FOLDED, 1)) * 128, 128)
    half = lane < 64

    def joined(a, b):
        return jnp.where(half, a, pltpu.roll(b, 64, 1))

    def fold(blocks, dst):
        for n in (0, 1):
            dst[n] = joined(blocks[2 * n, :, fold_tile], blocks[2 * n + 1, :, fold_tile])

    def whole(t):
        return pl.ds(0, (tiles_sent(t, 0) + tiles_sent(t, 1)) * 128)

    def pack(t, h, px, pz, dst):
        first, count = PARTS[t][h]
        tiles = [None] * count
        base = {}
        for at, k, j, col, size in RUNS:
            d, w = at % 128, at // 128 - first
            if w >= count or at + size <= first * 128:
                continue
            if k not in base:
                base[k] = PAIR * ((lax.rem(pz, 2) * 4 + px) * 8 + step(y, AHEAD[k]) * 2 + pz // 2)
            off = base[k] + col
            t0 = off // 128
            t1 = jnp.minimum(t0 + 1, COLS // 128 - 1)
            s = off - t0 * 128
            sh = lax.rem(d - s + 128, 128)
            v0 = pltpu.roll(raw[j, :, pl.ds(pl.multiple_of(t0 * 128, 128), 128)], sh, 1)
            v1 = pltpu.roll(raw[j, :, pl.ds(pl.multiple_of(t1 * 128, 128), 128)], sh, 1)
            v = jnp.where(lax.rem(lane - d + 128, 128) < 128 - s, v0, v1)
            if w >= 0:
                tiles[w] = v if tiles[w] is None else jnp.where(lane < d, tiles[w], v)
            if d + size > 128 and w + 1 < count:
                tiles[w + 1] = v
        if first <= FILLED // 128 < first + count:
            w = FILLED // 128 - first
            tiles[w] = jnp.where(lane < FILLED % 128, tiles[w], 0.0)
        for w in range(count):
            lo = (STARTS[t][h] + w) * 128
            dst[:, lo : lo + 128] = tiles[w]

    def pack_a(t, px, dst):
        lax.fori_loop(0, 4, lambda pz, c: (pack(t, 0, px, pz, dst.at[pz]), c)[1], 0)

    def pack_b(t, pz, dst):
        lax.fori_loop(0, 4, lambda px, c: (pack(t, 1, px, pz, dst.at[px]), c)[1], 0)

    def remote(src, dst, ssem, rsem, dev):
        return pltpu.make_async_remote_copy(
            src_ref=src, dst_ref=dst, send_sem=ssem, recv_sem=rsem, device_id=dev, device_id_type=MESH
        )

    def first_copy(t, h, d):
        w = lanes(t, h)
        if h == 0:
            px = step(x, d)
            return remote(s1a.at[px, :, :, w], r1a.at[x, :, :, w], hop_send.at[0], s1_recv.at[t], device(px, y, zz, core))
        pz = step(zz, d)
        return remote(s1b.at[pz, :, :, w], r1b.at[zz, :, :, w], hop_send.at[0], s1_recv.at[t], device(x, y, pz, core))

    def send_a(t, d):
        px = step(x, d)
        pack_a(t, px, s1a.at[px])
        first_copy(t, 0, d).start()

    def send_b(t, d):
        pz = step(zz, d)
        pack_b(t, pz, s1b.at[pz])
        first_copy(t, 1, d).start()
        if t == FOLDED:
            fold(s1b.at[pz], s1f.at[pz])
            remote(s1f.at[pz], r1f.at[zz], fold_sem.at[0], fold_sem.at[1], device(x, y, pz, core)).start()

    def first_hop(t, begun=False):
        def message(n, carry):
            d = 2 - n + 3 * (n // 2)
            send_a(t, d)
            send_b(t, d)
            return carry

        lax.fori_loop(1 if begun else 0, 3, message, 0)
        pack_a(t, x, r1a.at[x])
        pack_b(t, zz, r1b.at[zz])
        if t == FOLDED:
            fold(r1b.at[zz], r1f.at[zz])

    def second_hop(t):
        wa, wb = lanes(t, 0), lanes(t, 1)
        landed(r1a.at[0:3, :, :, whole(t)], s1_recv.at[t])
        for d in (2, 1, 3):
            px, pz = step(x, d), step(zz, d)
            remote(r1a.at[:, pz, :, wa], g.at[0, zz, :, :, wa], hop_send.at[1], s2_recv.at[t], device(x, y, pz, core)).start()
            remote(r1b.at[:, px, :, wb], g.at[1, :, x, :, wb], hop_send.at[1], s2_recv.at[t], device(px, y, zz, core)).start()
        if t == FOLDED:
            landed(r1f.at[0:3], fold_sem.at[1])
            for px in range(4):
                for n in (0, 1):
                    a, b = r1f[2 * n, px // 2], r1f[2 * n + 1, px // 2]
                    s2f[px, n] = joined(a, b) if px % 2 == 0 else jnp.where(half, pltpu.roll(a, 64, 1), b)
            for d in (2, 1, 3):
                px = step(x, d)
                remote(s2f.at[px], gf.at[x], fold_sem.at[0], fold_sem.at[2], device(px, y, zz, core)).start()
            gf[x] = s2f[x]
        pltpu.make_async_copy(r1a.at[:, zz, :, wa], g.at[0, zz, :, :, wa], s2_recv.at[t]).start()
        pltpu.make_async_copy(r1b.at[:, x, :, wb], g.at[1, :, x, :, wb], s2_recv.at[t]).start()

    low = lax.broadcasted_iota(jnp.int32, (JB, 128), 1) < 64

    def project(t):
        both = [(h, v) for h in (0, 1) for v in (0, 1)]
        for group in (both,) if t > 3 else (both[:2], both[2:]):
            blocks = [g[h, v * 2 : v * 2 + 2, :, :, held(t, h)].reshape(MIDX, -1) for h, v in group]
            hi, lo = split(jnp.concatenate(blocks, axis=1))
            gxx[...] += dot(hi, hi, NT)
            gxm[...] += dot(hi, lo, NT)
            f = dot(bb[...], hi, NN)
            f = f[0:64] + (f[64:128] + dot(bb[0:64], lo, NN))
            f = jnp.concatenate([f, f], axis=0)
            at = 0
            for h, v in group:
                first, size = PARTS[t][h][0] * 128, PARTS[t][h][1] * 128
                ft[v, first : first + size, :] = f[:, at : at + size].T
                at += size

    def pair(k, c, row, gap, stride, at, n):
        def pairs(p, carry):
            for v in (0, 1):
                a = ft[v, pl.ds(row + p, JB, stride), :]
                b = ft[v, pl.ds(row + gap + p, JB, stride), :]
                fs[k, c, at + p, v * JB : (v + 1) * JB, :] = jnp.where(low, a, b)
            return carry

        lax.fori_loop(0, n, pairs, 0, unroll=True)

    def spread(k):
        py = step(y, AHEAD[k])
        for c in (0, 1):
            row = k * JB * PAIR + c * (OWN + LATE)
            pair(k, c, row, EP, PAIR, 0, EP)
            pair(k, c, k * JB * PAIR + (OWN if c else EARLY), LP, PAIR, EP, LP)
            remote(fs.at[k, c], fr.at[y, core], y_send, y_recv.at[k], device(x, py, zz, c)).start()

    def swap(part):
        k, c = CHUNKS - 1, 1 - core
        at, n = ((0, EP), (EP, LP))[part]
        w = pl.ds(at, n)

        def collect(i):
            row = SECOND + i * LATE if part else FIRST + i * EARLY
            pair(k, i, row, n, 2 * (LATE if part else EARLY), at, n)

        collect(c)
        remote(fs.at[k, c, w], fr.at[y, core, w], y_send, y_recv.at[k + part], device(x, y, zz, c)).start()
        collect(core)
        pltpu.make_async_copy(fs.at[k, core, w], fr.at[y, core, w], y_recv.at[k + part]).start()

    def chunk(t):
        landed(g.at[0, :, :, :, whole(t)], s2_recv.at[t])
        if t == FOLDED:
            landed(gf.at[0:3], fold_sem.at[2])
            for v in (0, 1):
                for px in range(4):
                    both = gf[px, v]
                    g[1, 2 * v, px, :, fold_tile] = jnp.where(half, both, 0.0)
                    g[1, 2 * v + 1, px, :, fold_tile] = jnp.where(half, pltpu.roll(both, 64, 1), 0.0)
        project(t)

    eights = [(d, e) for d in (2, 1, 3, 0) for e in (1, 0)]
    sixteens = [(d, e) for d in (2, 1, 3, 0) for e in (2, 1, 3, 0)]
    left = lax.broadcasted_iota(jnp.int32, (64, 128), 1) < 64

    def own_rows(px, pc):
        return pl.ds(pl.multiple_of((px * 2 + pc) * 24, 24), 24)

    def scatter(i, main, cross, scale):
        m = cross[...]
        main[...] = (main[...] + (m + m.T)) * scale
        part[i, 0:64] = main[0:64, 0:128]
        high = jnp.concatenate([main[64:128, 128:192], jnp.zeros((64, 64), F32)], axis=1)
        part[i, 64:128] = jnp.where(left, pltpu.roll(main[64:128, 0:128], 64, 1), pltpu.roll(high, 64, 1))
        top = jnp.concatenate([main[0:64, 128:192], jnp.zeros((64, 64), F32)], axis=1)
        end = jnp.concatenate([main[128:192, 128:192], jnp.zeros((64, 64), F32)], axis=1)
        part[i, 128:192] = jnp.where(left, top, pltpu.roll(end, 64, 1))
        for d, e in eights:
            if d or e:
                px, pc = step(x, d), lax.rem(core + e, 2)
                remote(part.at[i, own_rows(px, pc)], parts8.at[i, d * 2 + e - 1], sum_send, rs_recv.at[i], device(px, y, zz, pc)).start()

    def share(i):
        landed(parts8.at[i], rs_recv.at[i])
        total = part[i, own_rows(x, core)]
        for n in range(7):
            total += parts8[i, n]
        sums[i] = total

    def spread_yz(i):
        parts16[i, y * 4 + zz] = sums[i]
        for d, e in sixteens:
            if d or e:
                remote(sums.at[i], parts16.at[i, y * 4 + zz], sum_send, bc_recv.at[i], device(x, step(y, d), step(zz, e), core)).start()

    def gather_yz(i):
        landed(parts16.at[i, 0:15], bc_recv.at[i])
        total = parts16[i, 0]
        for n in range(1, 16):
            total += parts16[i, n]
        return total

    def publish(i, total):
        done[i] = total
        mine = full_out.at[i, own_rows(x, core)]
        for d, e in eights:
            if d or e:
                px, pc = step(x, d), lax.rem(core + e, 2)
                remote(done.at[i], mine, sum_send, ag_recv.at[i], device(px, y, zz, pc)).start()
        pltpu.make_async_copy(done.at[i], mine, ag_recv.at[i]).start()

    def columns(at, n):
        parts = []
        for p in range(n):
            rows = []
            for s in range(4):
                a, b = fr[s, 0, at + p], fr[s, 1, at + p]
                rows += [a[:JB], b[:JB], a[JB:], b[JB:]]
            parts.append(jnp.concatenate(rows, axis=0))
        return split(jnp.concatenate(parts, axis=1))

    def gram(at, n):
        hi, lo = columns(at, n)
        gyy[...] += dot(hi, hi, NT)
        gym[...] += dot(hi, lo, NT)

    wide = 5

    def finish(u, carry):
        hi, lo = columns(u * wide, wide)
        c = dot(bq[...], hi, NN)
        c = c[0:64] + (c[64:128] + dot(bq[0:64], lo, NN))
        for p in range(wide):
            core_v[u * wide + p] = c[:, p * 128 : (p + 1) * 128]
        return carry

    loads[0].wait()
    pack_a(0, step(x, 2), s1a.at[step(x, 2)])
    loads[1].wait()
    pack_b(0, step(zz, 2), s1b.at[step(zz, 2)])
    pl.semaphore_wait(barrier, len(partners))
    first_copy(0, 0, 2).start()
    first_copy(0, 1, 2).start()
    first_hop(0, True)
    loads[2].wait()
    first_hop(1)
    first_hop(2)
    landed(bases_v, load_sem.at[3])
    for n, ref in enumerate((bb, bq)):
        hi, lo = split(jnp.concatenate([bases_v[n], jnp.zeros((64 - RANK, MIDX), F32)], axis=0))
        ref[0:64] = hi
        ref[64:128] = lo
    for acc in (gxx, gxm, gyy, gym):
        acc[...] = jnp.zeros_like(acc)
    second_hop(0)
    second_hop(1)
    first_hop(3)
    second_hop(2)
    chunk(0)
    chunk(1)
    spread(0)
    second_hop(3)
    first_hop(4)
    first_hop(5)
    chunk(2)
    spread(1)
    chunk(3)
    spread(2)
    second_hop(4)
    second_hop(5)
    chunk(4)
    swap(0)
    chunk(5)
    scatter(0, gxx, gxm, 1.0 / (MIDY * COLS))
    swap(1)

    for k in range(CHUNKS - 1):
        landed(fr.at[0], y_recv.at[k])
    landed(fr.at[0, :, 0:EP], y_recv.at[CHUNKS - 1])
    gram(0, 6)
    gram(6, 6)
    gram(12, 5)
    landed(fr.at[0, :, EP:HP], y_recv.at[CHUNKS])
    gram(EP, LP)
    scatter(1, gyy, gym, 1.0 / (RANK * COLS))
    share(0)
    spread_yz(0)
    share(1)
    spread_yz(1)
    lax.fori_loop(0, HP // wide, finish, 0)
    core_store = pltpu.make_async_copy(core_v, core_out, store_sem)
    core_store.start()
    publish(0, gather_yz(0))
    publish(1, gather_yz(1))
    for hop in (0, 1):
        landed(g.at[0, 0:3], hop_send.at[hop])
        landed(g.at[0, 0:3, :, :, 0 : LANES - 128], hop_send.at[hop])
    landed(ft.at[0, 0 : 6 * 2 * IB], fold_sem.at[0])
    landed(ft.at[0, 0 : 7 * HP * 2 * JB], y_send)
    core_store.wait()
    for i in (0, 1):
        landed(full_out.at[i], ag_recv.at[i])
    landed(ft.at[0, 0 : 2 * (7 + 15 + 7) * 24], sum_send)


def unfold(full, core, gx_out, gy_out, core_out):
    left = lax.broadcasted_iota(jnp.int32, (64, 128), 1) < 64
    for i, ref in enumerate((gx_out, gy_out)):
        p0, p1, p2 = full[i, 0:64], full[i, 64:128], full[i, 128:192]
        t0 = full[i, 0:128].T
        t2 = jnp.concatenate([p2, p2], axis=0).T
        q1, q2 = pltpu.roll(p1, 64, 1), pltpu.roll(p2, 64, 1)
        ref[0:64, 0:128] = p0
        ref[0:64, 128:192] = p2[:, :64]
        ref[64:128, 0:128] = jnp.where(left, t0[64:128], q1)
        ref[64:128, 128:192] = q1[:, :64]
        ref[128:192, 0:128] = jnp.where(left, t2[0:64], t0[64:128])
        ref[128:192, 128:192] = q2[:, :64]
    odd = lax.rem(lax.axis_index("my"), 2)
    for p in range(HP):
        v = core[p]
        first, gap = (LATE * odd + p, EP) if p < EP else (EARLY * (1 - odd) + p - EP, LP)
        core_out[first] = v[:RANK, :RANK]
        core_out[first + gap] = pltpu.roll(v, 64, 1)[:RANK, :RANK]


def body(slab, basis_x, basis_y):
    anywhere = pl.BlockSpec(memory_space=pl.ANY)
    vmem = pl.BlockSpec(memory_space=pltpu.VMEM)
    full, core = pl.pallas_call(
        kernel,
        out_shape=(
            jax.ShapeDtypeStruct((2, 192, 128), F32),
            jax.ShapeDtypeStruct((HP, 64, 128), F32),
        ),
        in_specs=[anywhere] * 3,
        out_specs=(anywhere, anywhere),
        scratch_shapes=[
            pltpu.VMEM((JB, IB, COLS), F32),
            pltpu.VMEM((4, 4, IB, LANES), F32),
            pltpu.VMEM((4, 4, IB, LANES), F32),
            pltpu.VMEM((4, 4, IB, LANES), F32),
            pltpu.VMEM((4, 4, IB, LANES), F32),
            pltpu.VMEM((2, 4, 4, IB, LANES), F32),
            pltpu.VMEM((4, 2, IB, 128), F32),
            pltpu.VMEM((4, 2, IB, 128), F32),
            pltpu.VMEM((4, 2, IB, 128), F32),
            pltpu.VMEM((4, 2, IB, 128), F32),
            pltpu.VMEM((2, TILES * 128, 128), F32),
            pltpu.VMEM((CHUNKS, 2, HP, 2 * JB, 128), F32),
            pltpu.VMEM((4, 2, HP, 2 * JB, 128), F32),
            pltpu.VMEM((2, RANK, MIDX), F32),
            pltpu.VMEM((128, MIDX), BF16),
            pltpu.VMEM((128, MIDY), BF16),
            pltpu.VMEM((MIDX, MIDX), F32),
            pltpu.VMEM((MIDX, MIDX), F32),
            pltpu.VMEM((MIDY, MIDY), F32),
            pltpu.VMEM((MIDY, MIDY), F32),
            pltpu.VMEM((2, 192, 128), F32),
            pltpu.VMEM((2, 7, 24, 128), F32),
            pltpu.VMEM((2, 24, 128), F32),
            pltpu.VMEM((2, 16, 24, 128), F32),
            pltpu.VMEM((2, 24, 128), F32),
            pltpu.VMEM((HP, 64, 128), F32),
            pltpu.SemaphoreType.DMA((4,)),
            pltpu.SemaphoreType.DMA((2,)),
            pltpu.SemaphoreType.DMA((3,)),
            pltpu.SemaphoreType.DMA((len(PARTS),)),
            pltpu.SemaphoreType.DMA((len(PARTS),)),
            pltpu.SemaphoreType.DMA,
            pltpu.SemaphoreType.DMA((CHUNKS + 1,)),
            pltpu.SemaphoreType.DMA,
            pltpu.SemaphoreType.DMA,
            pltpu.SemaphoreType.DMA((2,)),
            pltpu.SemaphoreType.DMA((2,)),
            pltpu.SemaphoreType.DMA((2,)),
        ],
        compiler_params=pltpu.CompilerParams(
            collective_id=0, has_side_effects=True, vmem_limit_bytes=58 * 2**20
        ),
    )(jnp.transpose(slab, (1, 0, 2)), basis_x.T, basis_y.T)
    gx, gy, core = pl.pallas_call(
        unfold,
        out_shape=(
            jax.ShapeDtypeStruct((MIDX, MIDX), F32),
            jax.ShapeDtypeStruct((MIDY, MIDY), F32),
            jax.ShapeDtypeStruct((OWN, RANK, RANK), F32),
        ),
        in_specs=[vmem, vmem],
        out_specs=(vmem, vmem, vmem),
    )(full, core)
    return gx, gy, jnp.transpose(core, (1, 2, 0))


def solution(mesh):
    return jax.shard_map(
        body,
        mesh=mesh,
        in_specs=(P("mx", "my", None), P(), P()),
        out_specs=(P(), P(), P(None, None, ("mx", "my"))),
        check_vma=False,
    )
```

```python
import jax
import jax.numpy as jnp
from jax import lax
from jax.experimental import pallas as pl
from jax.experimental.pallas import tpu as pltpu
from jax.sharding import PartitionSpec as P

MESH = pl.DeviceIdType.MESH
F32 = jnp.float32
BF16 = jnp.bfloat16

MIDX = 192
MIDY = 192
RANK = 60
COLS = 6400
JB = 12
IB = 24
OWN = 50
PAIR = 2 * OWN
HP = OWN // 2
CHUNKS = 4
AHEAD = (2, 1, 3, 0)
EARLY, LATE = 34, 16
EP, LP = EARLY // 2, LATE // 2
RUNS = [(k * JB * PAIR + j * PAIR, k, j, 0, PAIR) for k in range(CHUNKS - 1) for j in range(JB)]
FIRST = (CHUNKS - 1) * JB * PAIR
RUNS += [(FIRST + (2 * j + i) * EARLY, CHUNKS - 1, j, i * (PAIR - EARLY), EARLY) for j in range(JB) for i in (0, 1)]
FILLED = FIRST + 2 * JB * EARLY
SECOND = -(-FILLED // 128) * 128
RUNS += [(SECOND + j * 2 * LATE, CHUNKS - 1, j, EARLY, 2 * LATE) for j in range(JB)]
PARTS = (
    ((0, 2), (2, 2)), ((4, 3), (7, 3)), ((10, 5), (15, 5)),
    ((20, 5), (25, 4)), ((29, 3), (32, 3)), ((35, 1), (36, 2)),
)
TILES = 38
LANES = TILES // 2 * 128
FOLDED = 4
STARTS = ((0, 0), (2, 2), (5, 5), (10, 10), (15, 14), (18, 17))

NT = (((1,), (1,)), ((), ()))
NN = (((1,), (0,)), ((), ()))


def split(a):
    hi = a.astype(BF16)
    return hi, (a - hi.astype(F32)).astype(BF16)


def dot(a, b, dims):
    return lax.dot_general(a, b, dims, preferred_element_type=F32)


def kernel(
    slab, bxt, byt, full_out, core_out,
    raw, s1a, s1b, r1a, r1b, g, s1f, r1f, s2f, gf, ft, fs, fr, bases_v, bb, bq, gxx, gxm, gyy, gym,
    part, parts8, sums, parts16, done, core_v,
    load_sem, hop_send, fold_sem, s1_recv, s2_recv, y_send, y_recv, store_sem,
    sum_send, rs_recv, bc_recv, ag_recv,
):
    mx, my = lax.axis_index("mx"), lax.axis_index("my")
    x, zh = lax.rem(mx, 4), mx // 4
    y, zl, core = my // 4, lax.rem(my // 2, 2), lax.rem(my, 2)
    zz = zl * 2 + zh

    def device(px, py, pz, pc):
        return (lax.rem(pz, 2) * 4 + px, py * 4 + (pz // 2) * 2 + pc)

    def step(v, d):
        return lax.rem(v + d, 4)

    barrier = pltpu.get_barrier_semaphore()
    partners = [device(step(x, d), y, zz, core) for d in (1, 2, 3)]
    partners += [device(x, y, step(zz, d), core) for d in (1, 2, 3)]
    partners += [device(x, step(y, d), zz, c) for d in (1, 2, 3) for c in (0, 1)]
    partners += [device(step(x, d), y, zz, 1 - core) for d in range(4)]
    for p in partners:
        pl.semaphore_signal(barrier, inc=1, device_id=p, device_id_type=MESH)


    rows = (pl.ds(0, 3), pl.ds(3, 3), pl.ds(6, 6))
    loads = [pltpu.make_async_copy(slab.at[r], raw.at[r], load_sem.at[n]) for n, r in enumerate(rows)]
    bases = [pltpu.make_async_copy(b, bases_v.at[n], load_sem.at[3]) for n, b in enumerate((bxt, byt))]
    for c in loads + bases:
        c.start()

    def landed(ref, sem):
        pltpu.make_async_copy(ref, ref, sem).wait()

    lane = lax.broadcasted_iota(jnp.int32, (IB, 128), 1)

    def held(t, h):
        return pl.ds(STARTS[t][h] * 128, PARTS[t][h][1] * 128)

    def tiles_sent(t, h):
        return PARTS[t][h][1] - ((t, h) == (FOLDED, 1))

    def lanes(t, h):
        return pl.ds(STARTS[t][h] * 128, tiles_sent(t, h) * 128)

    fold_tile = pl.ds((STARTS[FOLDED][1] + tiles_sent(FOLDED, 1)) * 128, 128)
    half = lane < 64

    def joined(a, b):
        return jnp.where(half, a, pltpu.roll(b, 64, 1))

    def fold(blocks, dst):
        for n in (0, 1):
            dst[n] = joined(blocks[2 * n, :, fold_tile], blocks[2 * n + 1, :, fold_tile])

    def whole(t):
        return pl.ds(0, (tiles_sent(t, 0) + tiles_sent(t, 1)) * 128)

    def pack(t, h, px, pz, dst):
        first, count = PARTS[t][h]
        tiles = [None] * count
        base = {}
        for at, k, j, col, size in RUNS:
            d, w = at % 128, at // 128 - first
            if w >= count or at + size <= first * 128:
                continue
            if k not in base:
                base[k] = PAIR * ((lax.rem(pz, 2) * 4 + px) * 8 + step(y, AHEAD[k]) * 2 + pz // 2)
            off = base[k] + col
            t0 = off // 128
            t1 = jnp.minimum(t0 + 1, COLS // 128 - 1)
            s = off - t0 * 128
            sh = lax.rem(d - s + 128, 128)
            v0 = pltpu.roll(raw[j, :, pl.ds(pl.multiple_of(t0 * 128, 128), 128)], sh, 1)
            v1 = pltpu.roll(raw[j, :, pl.ds(pl.multiple_of(t1 * 128, 128), 128)], sh, 1)
            v = jnp.where(lax.rem(lane - d + 128, 128) < 128 - s, v0, v1)
            if w >= 0:
                tiles[w] = v if tiles[w] is None else jnp.where(lane < d, tiles[w], v)
            if d + size > 128 and w + 1 < count:
                tiles[w + 1] = v
        if first <= FILLED // 128 < first + count:
            w = FILLED // 128 - first
            tiles[w] = jnp.where(lane < FILLED % 128, tiles[w], 0.0)
        for w in range(count):
            lo = (STARTS[t][h] + w) * 128
            dst[:, lo : lo + 128] = tiles[w]

    def pack_a(t, px, dst):
        lax.fori_loop(0, 4, lambda pz, c: (pack(t, 0, px, pz, dst.at[pz]), c)[1], 0)

    def pack_b(t, pz, dst):
        lax.fori_loop(0, 4, lambda px, c: (pack(t, 1, px, pz, dst.at[px]), c)[1], 0)

    def remote(src, dst, ssem, rsem, dev):
        return pltpu.make_async_remote_copy(
            src_ref=src, dst_ref=dst, send_sem=ssem, recv_sem=rsem, device_id=dev, device_id_type=MESH
        )

    def first_copy(t, h, d):
        w = lanes(t, h)
        if h == 0:
            px = step(x, d)
            return remote(s1a.at[px, :, :, w], r1a.at[x, :, :, w], hop_send.at[0], s1_recv.at[t], device(px, y, zz, core))
        pz = step(zz, d)
        return remote(s1b.at[pz, :, :, w], r1b.at[zz, :, :, w], hop_send.at[0], s1_recv.at[t], device(x, y, pz, core))

    def send_a(t, d):
        px = step(x, d)
        pack_a(t, px, s1a.at[px])
        first_copy(t, 0, d).start()

    def send_b(t, d):
        pz = step(zz, d)
        pack_b(t, pz, s1b.at[pz])
        first_copy(t, 1, d).start()
        if t == FOLDED:
            fold(s1b.at[pz], s1f.at[pz])
            remote(s1f.at[pz], r1f.at[zz], fold_sem.at[0], fold_sem.at[1], device(x, y, pz, core)).start()

    def first_hop(t, begun=False):
        def message(n, carry):
            d = 2 - n + 3 * (n // 2)
            send_a(t, d)
            send_b(t, d)
            return carry

        lax.fori_loop(1 if begun else 0, 3, message, 0)
        pack_a(t, x, r1a.at[x])
        pack_b(t, zz, r1b.at[zz])
        if t == FOLDED:
            fold(r1b.at[zz], r1f.at[zz])

    def second_hop(t):
        wa, wb = lanes(t, 0), lanes(t, 1)
        landed(r1a.at[0:3, :, :, whole(t)], s1_recv.at[t])
        for d in (2, 1, 3):
            px, pz = step(x, d), step(zz, d)
            remote(r1a.at[:, pz, :, wa], g.at[0, zz, :, :, wa], hop_send.at[1], s2_recv.at[t], device(x, y, pz, core)).start()
            remote(r1b.at[:, px, :, wb], g.at[1, :, x, :, wb], hop_send.at[1], s2_recv.at[t], device(px, y, zz, core)).start()
        if t == FOLDED:
            landed(r1f.at[0:3], fold_sem.at[1])
            for px in range(4):
                for n in (0, 1):
                    a, b = r1f[2 * n, px // 2], r1f[2 * n + 1, px // 2]
                    s2f[px, n] = joined(a, b) if px % 2 == 0 else jnp.where(half, pltpu.roll(a, 64, 1), b)
            for d in (2, 1, 3):
                px = step(x, d)
                remote(s2f.at[px], gf.at[x], fold_sem.at[0], fold_sem.at[2], device(px, y, zz, core)).start()
            gf[x] = s2f[x]
        pltpu.make_async_copy(r1a.at[:, zz, :, wa], g.at[0, zz, :, :, wa], s2_recv.at[t]).start()
        pltpu.make_async_copy(r1b.at[:, x, :, wb], g.at[1, :, x, :, wb], s2_recv.at[t]).start()

    low = lax.broadcasted_iota(jnp.int32, (JB, 128), 1) < 64

    def project(t):
        both = [(h, v) for h in (0, 1) for v in (0, 1)]
        for group in (both,) if t > 3 else (both[:2], both[2:]):
            blocks = [g[h, v * 2 : v * 2 + 2, :, :, held(t, h)].reshape(MIDX, -1) for h, v in group]
            hi, lo = split(jnp.concatenate(blocks, axis=1))
            gxx[...] += dot(hi, hi, NT)
            gxm[...] += dot(hi, lo, NT)
            f = dot(bb[...], hi, NN)
            f = f[0:64] + (f[64:128] + dot(bb[0:64], lo, NN))
            f = jnp.concatenate([f, f], axis=0)
            at = 0
            for h, v in group:
                first, size = PARTS[t][h][0] * 128, PARTS[t][h][1] * 128
                ft[v, first : first + size, :] = f[:, at : at + size].T
                at += size

    def pair(k, c, row, gap, stride, at, n):
        def pairs(p, carry):
            for v in (0, 1):
                a = ft[v, pl.ds(row + p, JB, stride), :]
                b = ft[v, pl.ds(row + gap + p, JB, stride), :]
                fs[k, c, at + p, v * JB : (v + 1) * JB, :] = jnp.where(low, a, b)
            return carry

        lax.fori_loop(0, n, pairs, 0, unroll=True)

    def spread(k):
        py = step(y, AHEAD[k])
        for c in (0, 1):
            row = k * JB * PAIR + c * (OWN + LATE)
            pair(k, c, row, EP, PAIR, 0, EP)
            pair(k, c, k * JB * PAIR + (OWN if c else EARLY), LP, PAIR, EP, LP)
            remote(fs.at[k, c], fr.at[y, core], y_send, y_recv.at[k], device(x, py, zz, c)).start()

    def swap(part):
        k, c = CHUNKS - 1, 1 - core
        at, n = ((0, EP), (EP, LP))[part]
        w = pl.ds(at, n)

        def collect(i):
            row = SECOND + i * LATE if part else FIRST + i * EARLY
            pair(k, i, row, n, 2 * (LATE if part else EARLY), at, n)

        collect(c)
        remote(fs.at[k, c, w], fr.at[y, core, w], y_send, y_recv.at[k + part], device(x, y, zz, c)).start()
        collect(core)
        pltpu.make_async_copy(fs.at[k, core, w], fr.at[y, core, w], y_recv.at[k + part]).start()

    def chunk(t):
        landed(g.at[0, :, :, :, whole(t)], s2_recv.at[t])
        if t == FOLDED:
            landed(gf.at[0:3], fold_sem.at[2])
            for v in (0, 1):
                for px in range(4):
                    both = gf[px, v]
                    g[1, 2 * v, px, :, fold_tile] = jnp.where(half, both, 0.0)
                    g[1, 2 * v + 1, px, :, fold_tile] = jnp.where(half, pltpu.roll(both, 64, 1), 0.0)
        project(t)

    eights = [(d, e) for d in (2, 1, 3, 0) for e in (1, 0)]
    sixteens = [(2, 2), (2, 1), (1, 2), (2, 3), (3, 2), (1, 1), (3, 3), (1, 3), (3, 1)]
    sixteens += [(0, 2), (2, 0), (0, 1), (1, 0), (0, 3), (3, 0), (0, 0)]
    left = lax.broadcasted_iota(jnp.int32, (64, 128), 1) < 64

    def own_rows(px, pc):
        return pl.ds(pl.multiple_of((px * 2 + pc) * 24, 24), 24)

    def scatter(i, main, cross, scale):
        m = cross[...]
        main[...] = (main[...] + (m + m.T)) * scale
        part[i, 0:64] = main[0:64, 0:128]
        high = jnp.concatenate([main[64:128, 128:192], jnp.zeros((64, 64), F32)], axis=1)
        part[i, 64:128] = jnp.where(left, pltpu.roll(main[64:128, 0:128], 64, 1), pltpu.roll(high, 64, 1))
        top = jnp.concatenate([main[0:64, 128:192], jnp.zeros((64, 64), F32)], axis=1)
        end = jnp.concatenate([main[128:192, 128:192], jnp.zeros((64, 64), F32)], axis=1)
        part[i, 128:192] = jnp.where(left, top, pltpu.roll(end, 64, 1))
        for d, e in eights:
            if d or e:
                px, pc = step(x, d), lax.rem(core + e, 2)
                remote(part.at[i, own_rows(px, pc)], parts8.at[i, d * 2 + e - 1], sum_send, rs_recv.at[i], device(px, y, zz, pc)).start()

    def share(i):
        landed(parts8.at[i], rs_recv.at[i])
        total = part[i, own_rows(x, core)]
        for n in range(7):
            total += parts8[i, n]
        sums[i] = total

    def spread_yz(i):
        parts16[i, y * 4 + zz] = sums[i]
        for d, e in sixteens:
            if d or e:
                remote(sums.at[i], parts16.at[i, y * 4 + zz], sum_send, bc_recv.at[i], device(x, step(y, d), step(zz, e), core)).start()

    def gather_yz(i):
        landed(parts16.at[i, 0:15], bc_recv.at[i])
        total = parts16[i, 0]
        for n in range(1, 16):
            total += parts16[i, n]
        return total

    def publish(i, total):
        done[i] = total
        mine = full_out.at[i, own_rows(x, core)]
        for d, e in eights:
            if d or e:
                px, pc = step(x, d), lax.rem(core + e, 2)
                remote(done.at[i], mine, sum_send, ag_recv.at[i], device(px, y, zz, pc)).start()
        pltpu.make_async_copy(done.at[i], mine, ag_recv.at[i]).start()

    def columns(at, n):
        parts = []
        for p in range(n):
            rows = []
            for s in range(4):
                a, b = fr[s, 0, at + p], fr[s, 1, at + p]
                rows += [a[:JB], b[:JB], a[JB:], b[JB:]]
            parts.append(jnp.concatenate(rows, axis=0))
        return split(jnp.concatenate(parts, axis=1))

    def gram(at, n):
        hi, lo = columns(at, n)
        gyy[...] += dot(hi, hi, NT)
        gym[...] += dot(hi, lo, NT)

    wide = 5

    def finish(u, carry):
        hi, lo = columns(u * wide, wide)
        c = dot(bq[...], hi, NN)
        c = c[0:64] + (c[64:128] + dot(bq[0:64], lo, NN))
        for p in range(wide):
            core_v[u * wide + p] = c[:, p * 128 : (p + 1) * 128]
        return carry

    loads[0].wait()
    pack_a(0, step(x, 2), s1a.at[step(x, 2)])
    loads[1].wait()
    pack_b(0, step(zz, 2), s1b.at[step(zz, 2)])
    pl.semaphore_wait(barrier, len(partners))
    first_copy(0, 0, 2).start()
    first_copy(0, 1, 2).start()
    first_hop(0, True)
    loads[2].wait()
    first_hop(1)
    first_hop(2)
    landed(bases_v, load_sem.at[3])
    for n, ref in enumerate((bb, bq)):
        hi, lo = split(jnp.concatenate([bases_v[n], jnp.zeros((64 - RANK, MIDX), F32)], axis=0))
        ref[0:64] = hi
        ref[64:128] = lo
    for acc in (gxx, gxm, gyy, gym):
        acc[...] = jnp.zeros_like(acc)
    second_hop(0)
    second_hop(1)
    first_hop(3)
    second_hop(2)
    chunk(0)
    chunk(1)
    spread(0)
    second_hop(3)
    first_hop(4)
    first_hop(5)
    chunk(2)
    spread(1)
    chunk(3)
    spread(2)
    second_hop(4)
    second_hop(5)
    chunk(4)
    swap(0)
    chunk(5)
    scatter(0, gxx, gxm, 1.0 / (MIDY * COLS))
    swap(1)

    for k in range(CHUNKS - 1):
        landed(fr.at[0], y_recv.at[k])
    landed(fr.at[0, :, 0:EP], y_recv.at[CHUNKS - 1])
    gram(0, 6)
    gram(6, 6)
    gram(12, 5)
    landed(fr.at[0, :, EP:HP], y_recv.at[CHUNKS])
    gram(EP, LP)
    scatter(1, gyy, gym, 1.0 / (RANK * COLS))
    share(0)
    spread_yz(0)
    share(1)
    spread_yz(1)
    lax.fori_loop(0, HP // wide, finish, 0)
    core_store = pltpu.make_async_copy(core_v, core_out, store_sem)
    core_store.start()
    publish(0, gather_yz(0))
    publish(1, gather_yz(1))
    for hop in (0, 1):
        landed(g.at[0, 0:3], hop_send.at[hop])
        landed(g.at[0, 0:3, :, :, 0 : LANES - 128], hop_send.at[hop])
    landed(ft.at[0, 0 : 6 * 2 * IB], fold_sem.at[0])
    landed(ft.at[0, 0 : 7 * HP * 2 * JB], y_send)
    core_store.wait()
    for i in (0, 1):
        landed(full_out.at[i], ag_recv.at[i])
    landed(ft.at[0, 0 : 2 * (7 + 15 + 7) * 24], sum_send)


def unfold(full, core, gx_out, gy_out, core_out):
    left = lax.broadcasted_iota(jnp.int32, (64, 128), 1) < 64
    for i, ref in enumerate((gx_out, gy_out)):
        p0, p1, p2 = full[i, 0:64], full[i, 64:128], full[i, 128:192]
        t0 = full[i, 0:128].T
        t2 = jnp.concatenate([p2, p2], axis=0).T
        q1, q2 = pltpu.roll(p1, 64, 1), pltpu.roll(p2, 64, 1)
        ref[0:64, 0:128] = p0
        ref[0:64, 128:192] = p2[:, :64]
        ref[64:128, 0:128] = jnp.where(left, t0[64:128], q1)
        ref[64:128, 128:192] = q1[:, :64]
        ref[128:192, 0:128] = jnp.where(left, t2[0:64], t0[64:128])
        ref[128:192, 128:192] = q2[:, :64]
    odd = lax.rem(lax.axis_index("my"), 2)
    for p in range(HP):
        v = core[p]
        first, gap = (LATE * odd + p, EP) if p < EP else (EARLY * (1 - odd) + p - EP, LP)
        core_out[first] = v[:RANK, :RANK]
        core_out[first + gap] = pltpu.roll(v, 64, 1)[:RANK, :RANK]


def body(slab, basis_x, basis_y):
    anywhere = pl.BlockSpec(memory_space=pl.ANY)
    vmem = pl.BlockSpec(memory_space=pltpu.VMEM)
    full, core = pl.pallas_call(
        kernel,
        out_shape=(
            jax.ShapeDtypeStruct((2, 192, 128), F32),
            jax.ShapeDtypeStruct((HP, 64, 128), F32),
        ),
        in_specs=[anywhere] * 3,
        out_specs=(anywhere, anywhere),
        scratch_shapes=[
            pltpu.VMEM((JB, IB, COLS), F32),
            pltpu.VMEM((4, 4, IB, LANES), F32),
            pltpu.VMEM((4, 4, IB, LANES), F32),
            pltpu.VMEM((4, 4, IB, LANES), F32),
            pltpu.VMEM((4, 4, IB, LANES), F32),
            pltpu.VMEM((2, 4, 4, IB, LANES), F32),
            pltpu.VMEM((4, 2, IB, 128), F32),
            pltpu.VMEM((4, 2, IB, 128), F32),
            pltpu.VMEM((4, 2, IB, 128), F32),
            pltpu.VMEM((4, 2, IB, 128), F32),
            pltpu.VMEM((2, TILES * 128, 128), F32),
            pltpu.VMEM((CHUNKS, 2, HP, 2 * JB, 128), F32),
            pltpu.VMEM((4, 2, HP, 2 * JB, 128), F32),
            pltpu.VMEM((2, RANK, MIDX), F32),
            pltpu.VMEM((128, MIDX), BF16),
            pltpu.VMEM((128, MIDY), BF16),
            pltpu.VMEM((MIDX, MIDX), F32),
            pltpu.VMEM((MIDX, MIDX), F32),
            pltpu.VMEM((MIDY, MIDY), F32),
            pltpu.VMEM((MIDY, MIDY), F32),
            pltpu.VMEM((2, 192, 128), F32),
            pltpu.VMEM((2, 7, 24, 128), F32),
            pltpu.VMEM((2, 24, 128), F32),
            pltpu.VMEM((2, 16, 24, 128), F32),
            pltpu.VMEM((2, 24, 128), F32),
            pltpu.VMEM((HP, 64, 128), F32),
            pltpu.SemaphoreType.DMA((4,)),
            pltpu.SemaphoreType.DMA((2,)),
            pltpu.SemaphoreType.DMA((3,)),
            pltpu.SemaphoreType.DMA((len(PARTS),)),
            pltpu.SemaphoreType.DMA((len(PARTS),)),
            pltpu.SemaphoreType.DMA,
            pltpu.SemaphoreType.DMA((CHUNKS + 1,)),
            pltpu.SemaphoreType.DMA,
            pltpu.SemaphoreType.DMA,
            pltpu.SemaphoreType.DMA((2,)),
            pltpu.SemaphoreType.DMA((2,)),
            pltpu.SemaphoreType.DMA((2,)),
        ],
        compiler_params=pltpu.CompilerParams(
            collective_id=0, has_side_effects=True, vmem_limit_bytes=58 * 2**20
        ),
    )(jnp.transpose(slab, (1, 0, 2)), basis_x.T, basis_y.T)
    gx, gy, core = pl.pallas_call(
        unfold,
        out_shape=(
            jax.ShapeDtypeStruct((MIDX, MIDX), F32),
            jax.ShapeDtypeStruct((MIDY, MIDY), F32),
            jax.ShapeDtypeStruct((OWN, RANK, RANK), F32),
        ),
        in_specs=[vmem, vmem],
        out_specs=(vmem, vmem, vmem),
    )(full, core)
    return gx, gy, jnp.transpose(core, (1, 2, 0))


def solution(mesh):
    return jax.shard_map(
        body,
        mesh=mesh,
        in_specs=(P("mx", "my", None), P(), P()),
        out_specs=(P(), P(), P(None, None, ("mx", "my"))),
        check_vma=False,
    )
```

```python
import jax
import jax.numpy as jnp
from jax import lax
from jax.experimental import pallas as pl
from jax.experimental.pallas import tpu as pltpu
from jax.sharding import PartitionSpec as P

MESH = pl.DeviceIdType.MESH
F32 = jnp.float32
BF16 = jnp.bfloat16

MIDX = 192
MIDY = 192
RANK = 60
COLS = 6400
JB = 12
IB = 24
OWN = 50
PAIR = 2 * OWN
HP = OWN // 2
CHUNKS = 4
AHEAD = (2, 1, 3, 0)
EARLY, LATE = 34, 16
EP, LP = EARLY // 2, LATE // 2
RUNS = [(k * JB * PAIR + j * PAIR, k, j, 0, PAIR) for k in range(CHUNKS - 1) for j in range(JB)]
FIRST = (CHUNKS - 1) * JB * PAIR
RUNS += [(FIRST + (2 * j + i) * EARLY, CHUNKS - 1, j, i * (PAIR - EARLY), EARLY) for j in range(JB) for i in (0, 1)]
FILLED = FIRST + 2 * JB * EARLY
SECOND = -(-FILLED // 128) * 128
RUNS += [(SECOND + j * 2 * LATE, CHUNKS - 1, j, EARLY, 2 * LATE) for j in range(JB)]
PARTS = (
    ((0, 2), (2, 2)), ((4, 3), (7, 3)), ((10, 5), (15, 5)),
    ((20, 5), (25, 4)), ((29, 3), (32, 3)), ((35, 1), (36, 2)),
)
TILES = 38
LANES = TILES // 2 * 128
FOLDED = 4
STARTS = ((0, 0), (2, 2), (5, 5), (10, 10), (15, 14), (18, 17))

NT = (((1,), (1,)), ((), ()))
NN = (((1,), (0,)), ((), ()))


def split(a):
    hi = a.astype(BF16)
    return hi, (a - hi.astype(F32)).astype(BF16)


def dot(a, b, dims):
    return lax.dot_general(a, b, dims, preferred_element_type=F32)


def kernel(
    slab, bxt, byt, full_out, core_out,
    raw, s1a, s1b, r1a, r1b, g, s1f, r1f, s2f, gf, ft, fs, fr, bases_v, bb, bq, gxx, gxm, gyy, gym,
    part, parts8, sums, parts16, done, core_v,
    load_sem, hop_send, fold_sem, s1_recv, s2_recv, y_send, y_recv, store_sem,
    sum_send, rs_recv, bc_recv, ag_recv,
):
    mx, my = lax.axis_index("mx"), lax.axis_index("my")
    x, zh = lax.rem(mx, 4), mx // 4
    y, zl, core = my // 4, lax.rem(my // 2, 2), lax.rem(my, 2)
    zz = zl * 2 + zh

    def device(px, py, pz, pc):
        return (lax.rem(pz, 2) * 4 + px, py * 4 + (pz // 2) * 2 + pc)

    def step(v, d):
        return lax.rem(v + d, 4)

    barrier = pltpu.get_barrier_semaphore()
    partners = [device(step(x, d), y, zz, core) for d in (1, 2, 3)]
    partners += [device(x, y, step(zz, d), core) for d in (1, 2, 3)]
    partners += [device(x, step(y, d), zz, c) for d in (1, 2, 3) for c in (0, 1)]
    partners += [device(step(x, d), y, zz, 1 - core) for d in range(4)]
    for p in partners:
        pl.semaphore_signal(barrier, inc=1, device_id=p, device_id_type=MESH)


    rows = (pl.ds(0, 3), pl.ds(3, 3), pl.ds(6, 6))
    loads = [pltpu.make_async_copy(slab.at[r], raw.at[r], load_sem.at[n]) for n, r in enumerate(rows)]
    bases = [pltpu.make_async_copy(b, bases_v.at[n], load_sem.at[3]) for n, b in enumerate((bxt, byt))]
    for c in loads + bases:
        c.start()

    def landed(ref, sem):
        pltpu.make_async_copy(ref, ref, sem).wait()

    lane = lax.broadcasted_iota(jnp.int32, (IB, 128), 1)

    def held(t, h):
        return pl.ds(STARTS[t][h] * 128, PARTS[t][h][1] * 128)

    def tiles_sent(t, h):
        return PARTS[t][h][1] - ((t, h) == (FOLDED, 1))

    def lanes(t, h):
        return pl.ds(STARTS[t][h] * 128, tiles_sent(t, h) * 128)

    fold_tile = pl.ds((STARTS[FOLDED][1] + tiles_sent(FOLDED, 1)) * 128, 128)
    half = lane < 64

    def joined(a, b):
        return jnp.where(half, a, pltpu.roll(b, 64, 1))

    def fold(blocks, dst):
        for n in (0, 1):
            dst[n] = joined(blocks[2 * n, :, fold_tile], blocks[2 * n + 1, :, fold_tile])

    def whole(t):
        return pl.ds(0, (tiles_sent(t, 0) + tiles_sent(t, 1)) * 128)

    def pack(t, h, px, pz, dst):
        first, count = PARTS[t][h]
        tiles = [None] * count
        base = {}
        for at, k, j, col, size in RUNS:
            d, w = at % 128, at // 128 - first
            if w >= count or at + size <= first * 128:
                continue
            if k not in base:
                base[k] = PAIR * ((lax.rem(pz, 2) * 4 + px) * 8 + step(y, AHEAD[k]) * 2 + pz // 2)
            off = base[k] + col
            t0 = off // 128
            t1 = jnp.minimum(t0 + 1, COLS // 128 - 1)
            s = off - t0 * 128
            sh = lax.rem(d - s + 128, 128)
            v0 = pltpu.roll(raw[j, :, pl.ds(pl.multiple_of(t0 * 128, 128), 128)], sh, 1)
            v1 = pltpu.roll(raw[j, :, pl.ds(pl.multiple_of(t1 * 128, 128), 128)], sh, 1)
            v = jnp.where(lax.rem(lane - d + 128, 128) < 128 - s, v0, v1)
            if w >= 0:
                tiles[w] = v if tiles[w] is None else jnp.where(lane < d, tiles[w], v)
            if d + size > 128 and w + 1 < count:
                tiles[w + 1] = v
        if first <= FILLED // 128 < first + count:
            w = FILLED // 128 - first
            tiles[w] = jnp.where(lane < FILLED % 128, tiles[w], 0.0)
        for w in range(count):
            lo = (STARTS[t][h] + w) * 128
            dst[:, lo : lo + 128] = tiles[w]

    def pack_a(t, px, dst):
        lax.fori_loop(0, 4, lambda pz, c: (pack(t, 0, px, pz, dst.at[pz]), c)[1], 0)

    def pack_b(t, pz, dst):
        lax.fori_loop(0, 4, lambda px, c: (pack(t, 1, px, pz, dst.at[px]), c)[1], 0)

    def remote(src, dst, ssem, rsem, dev):
        return pltpu.make_async_remote_copy(
            src_ref=src, dst_ref=dst, send_sem=ssem, recv_sem=rsem, device_id=dev, device_id_type=MESH
        )

    def first_copy(t, h, d):
        w = lanes(t, h)
        if h == 0:
            px = step(x, d)
            return remote(s1a.at[px, :, :, w], r1a.at[x, :, :, w], hop_send.at[0], s1_recv.at[t], device(px, y, zz, core))
        pz = step(zz, d)
        return remote(s1b.at[pz, :, :, w], r1b.at[zz, :, :, w], hop_send.at[0], s1_recv.at[t], device(x, y, pz, core))

    def send_a(t, d):
        px = step(x, d)
        pack_a(t, px, s1a.at[px])
        first_copy(t, 0, d).start()

    def send_b(t, d):
        pz = step(zz, d)
        pack_b(t, pz, s1b.at[pz])
        first_copy(t, 1, d).start()
        if t == FOLDED:
            fold(s1b.at[pz], s1f.at[pz])
            remote(s1f.at[pz], r1f.at[zz], fold_sem.at[0], fold_sem.at[1], device(x, y, pz, core)).start()

    def first_hop(t, begun=False):
        def message(n, carry):
            d = 2 - n + 3 * (n // 2)
            send_a(t, d)
            send_b(t, d)
            return carry

        lax.fori_loop(1 if begun else 0, 3, message, 0)
        pack_a(t, x, r1a.at[x])
        pack_b(t, zz, r1b.at[zz])
        if t == FOLDED:
            fold(r1b.at[zz], r1f.at[zz])

    def second_hop(t):
        wa, wb = lanes(t, 0), lanes(t, 1)
        landed(r1a.at[0:3, :, :, whole(t)], s1_recv.at[t])
        for d in (2, 1, 3):
            px, pz = step(x, d), step(zz, d)
            remote(r1a.at[:, pz, :, wa], g.at[0, zz, :, :, wa], hop_send.at[1], s2_recv.at[t], device(x, y, pz, core)).start()
            remote(r1b.at[:, px, :, wb], g.at[1, :, x, :, wb], hop_send.at[1], s2_recv.at[t], device(px, y, zz, core)).start()
        if t == FOLDED:
            landed(r1f.at[0:3], fold_sem.at[1])
            for px in range(4):
                for n in (0, 1):
                    a, b = r1f[2 * n, px // 2], r1f[2 * n + 1, px // 2]
                    s2f[px, n] = joined(a, b) if px % 2 == 0 else jnp.where(half, pltpu.roll(a, 64, 1), b)
            for d in (2, 1, 3):
                px = step(x, d)
                remote(s2f.at[px], gf.at[x], fold_sem.at[0], fold_sem.at[2], device(px, y, zz, core)).start()
            gf[x] = s2f[x]
        pltpu.make_async_copy(r1a.at[:, zz, :, wa], g.at[0, zz, :, :, wa], s2_recv.at[t]).start()
        pltpu.make_async_copy(r1b.at[:, x, :, wb], g.at[1, :, x, :, wb], s2_recv.at[t]).start()

    low = lax.broadcasted_iota(jnp.int32, (JB, 128), 1) < 64

    def project(t):
        both = [(h, v) for h in (0, 1) for v in (0, 1)]
        for group in (both,) if t > 3 else (both[:2], both[2:]):
            blocks = [g[h, v * 2 : v * 2 + 2, :, :, held(t, h)].reshape(MIDX, -1) for h, v in group]
            hi, lo = split(jnp.concatenate(blocks, axis=1))
            gxx[...] += dot(hi, hi, NT)
            gxm[...] += dot(hi, lo, NT)
            f = dot(bb[...], hi, NN)
            f = f[0:64] + (f[64:128] + dot(bb[0:64], lo, NN))
            f = jnp.concatenate([f, f], axis=0)
            at = 0
            for h, v in group:
                first, size = PARTS[t][h][0] * 128, PARTS[t][h][1] * 128
                ft[v, first : first + size, :] = f[:, at : at + size].T
                at += size

    def pair(k, c, row, gap, stride, at, n):
        def pairs(p, carry):
            for v in (0, 1):
                a = ft[v, pl.ds(row + p, JB, stride), :]
                b = ft[v, pl.ds(row + gap + p, JB, stride), :]
                fs[k, c, at + p, v * JB : (v + 1) * JB, :] = jnp.where(low, a, b)
            return carry

        lax.fori_loop(0, n, pairs, 0, unroll=True)

    def spread(k):
        py = step(y, AHEAD[k])
        for c in (0, 1):
            row = k * JB * PAIR + c * (OWN + LATE)
            pair(k, c, row, EP, PAIR, 0, EP)
            pair(k, c, k * JB * PAIR + (OWN if c else EARLY), LP, PAIR, EP, LP)
            remote(fs.at[k, c], fr.at[y, core], y_send, y_recv.at[k], device(x, py, zz, c)).start()

    def swap(part):
        k, c = CHUNKS - 1, 1 - core
        at, n = ((0, EP), (EP, LP))[part]
        w = pl.ds(at, n)

        def collect(i):
            row = SECOND + i * LATE if part else FIRST + i * EARLY
            pair(k, i, row, n, 2 * (LATE if part else EARLY), at, n)

        collect(c)
        remote(fs.at[k, c, w], fr.at[y, core, w], y_send, y_recv.at[k + part], device(x, y, zz, c)).start()
        collect(core)
        pltpu.make_async_copy(fs.at[k, core, w], fr.at[y, core, w], y_recv.at[k + part]).start()

    def chunk(t):
        landed(g.at[0, :, :, :, whole(t)], s2_recv.at[t])
        if t == FOLDED:
            landed(gf.at[0:3], fold_sem.at[2])
            for v in (0, 1):
                for px in range(4):
                    both = gf[px, v]
                    g[1, 2 * v, px, :, fold_tile] = jnp.where(half, both, 0.0)
                    g[1, 2 * v + 1, px, :, fold_tile] = jnp.where(half, pltpu.roll(both, 64, 1), 0.0)
        project(t)

    eights = [(2, 1), (2, 0), (1, 1), (3, 1), (1, 0), (3, 0), (0, 1), (0, 0)]
    sixteens = [(2, 2), (2, 1), (1, 2), (2, 3), (3, 2), (1, 1), (3, 3), (1, 3), (3, 1)]
    sixteens += [(0, 2), (2, 0), (0, 1), (1, 0), (0, 3), (3, 0), (0, 0)]
    left = lax.broadcasted_iota(jnp.int32, (64, 128), 1) < 64

    def own_rows(px, pc):
        return pl.ds(pl.multiple_of((px * 2 + pc) * 24, 24), 24)

    def scatter(i, main, cross, scale):
        m = cross[...]
        main[...] = (main[...] + (m + m.T)) * scale
        part[i, 0:64] = main[0:64, 0:128]
        high = jnp.concatenate([main[64:128, 128:192], jnp.zeros((64, 64), F32)], axis=1)
        part[i, 64:128] = jnp.where(left, pltpu.roll(main[64:128, 0:128], 64, 1), pltpu.roll(high, 64, 1))
        top = jnp.concatenate([main[0:64, 128:192], jnp.zeros((64, 64), F32)], axis=1)
        end = jnp.concatenate([main[128:192, 128:192], jnp.zeros((64, 64), F32)], axis=1)
        part[i, 128:192] = jnp.where(left, top, pltpu.roll(end, 64, 1))
        for d, e in eights:
            if d or e:
                px, pc = step(x, d), lax.rem(core + e, 2)
                remote(part.at[i, own_rows(px, pc)], parts8.at[i, d * 2 + e - 1], sum_send, rs_recv.at[i], device(px, y, zz, pc)).start()

    def share(i):
        landed(parts8.at[i], rs_recv.at[i])
        total = part[i, own_rows(x, core)]
        for n in range(7):
            total += parts8[i, n]
        sums[i] = total

    def spread_yz(i):
        parts16[i, y * 4 + zz] = sums[i]
        for d, e in sixteens:
            if d or e:
                remote(sums.at[i], parts16.at[i, y * 4 + zz], sum_send, bc_recv.at[i], device(x, step(y, d), step(zz, e), core)).start()

    def gather_yz(i):
        landed(parts16.at[i, 0:15], bc_recv.at[i])
        total = parts16[i, 0]
        for n in range(1, 16):
            total += parts16[i, n]
        return total

    def publish(i, total):
        done[i] = total
        mine = full_out.at[i, own_rows(x, core)]
        for d, e in eights:
            if d or e:
                px, pc = step(x, d), lax.rem(core + e, 2)
                remote(done.at[i], mine, sum_send, ag_recv.at[i], device(px, y, zz, pc)).start()
        pltpu.make_async_copy(done.at[i], mine, ag_recv.at[i]).start()

    def columns(at, n):
        parts = []
        for p in range(n):
            rows = []
            for s in range(4):
                a, b = fr[s, 0, at + p], fr[s, 1, at + p]
                rows += [a[:JB], b[:JB], a[JB:], b[JB:]]
            parts.append(jnp.concatenate(rows, axis=0))
        return split(jnp.concatenate(parts, axis=1))

    def gram(at, n):
        hi, lo = columns(at, n)
        gyy[...] += dot(hi, hi, NT)
        gym[...] += dot(hi, lo, NT)

    wide = 5

    def finish(u, carry):
        hi, lo = columns(u * wide, wide)
        c = dot(bq[...], hi, NN)
        c = c[0:64] + (c[64:128] + dot(bq[0:64], lo, NN))
        for p in range(wide):
            core_v[u * wide + p] = c[:, p * 128 : (p + 1) * 128]
        return carry

    loads[0].wait()
    pack_a(0, step(x, 2), s1a.at[step(x, 2)])
    loads[1].wait()
    pack_b(0, step(zz, 2), s1b.at[step(zz, 2)])
    pl.semaphore_wait(barrier, len(partners))
    first_copy(0, 0, 2).start()
    first_copy(0, 1, 2).start()
    first_hop(0, True)
    loads[2].wait()
    first_hop(1)
    first_hop(2)
    landed(bases_v, load_sem.at[3])
    for n, ref in enumerate((bb, bq)):
        hi, lo = split(jnp.concatenate([bases_v[n], jnp.zeros((64 - RANK, MIDX), F32)], axis=0))
        ref[0:64] = hi
        ref[64:128] = lo
    for acc in (gxx, gxm, gyy, gym):
        acc[...] = jnp.zeros_like(acc)
    second_hop(0)
    second_hop(1)
    first_hop(3)
    second_hop(2)
    chunk(0)
    chunk(1)
    spread(0)
    second_hop(3)
    first_hop(4)
    first_hop(5)
    chunk(2)
    spread(1)
    chunk(3)
    spread(2)
    second_hop(4)
    second_hop(5)
    chunk(4)
    swap(0)
    chunk(5)
    scatter(0, gxx, gxm, 1.0 / (MIDY * COLS))
    swap(1)

    for k in range(CHUNKS - 1):
        landed(fr.at[0], y_recv.at[k])
    landed(fr.at[0, :, 0:EP], y_recv.at[CHUNKS - 1])
    gram(0, 6)
    gram(6, 6)
    gram(12, 5)
    landed(fr.at[0, :, EP:HP], y_recv.at[CHUNKS])
    gram(EP, LP)
    scatter(1, gyy, gym, 1.0 / (RANK * COLS))
    share(0)
    spread_yz(0)
    share(1)
    spread_yz(1)
    lax.fori_loop(0, HP // wide, finish, 0)
    core_store = pltpu.make_async_copy(core_v, core_out, store_sem)
    core_store.start()
    publish(0, gather_yz(0))
    publish(1, gather_yz(1))
    for hop in (0, 1):
        landed(g.at[0, 0:3], hop_send.at[hop])
        landed(g.at[0, 0:3, :, :, 0 : LANES - 128], hop_send.at[hop])
    landed(ft.at[0, 0 : 6 * 2 * IB], fold_sem.at[0])
    landed(ft.at[0, 0 : 7 * HP * 2 * JB], y_send)
    core_store.wait()
    for i in (0, 1):
        landed(full_out.at[i], ag_recv.at[i])
    landed(ft.at[0, 0 : 2 * (7 + 15 + 7) * 24], sum_send)


def unfold(full, core, gx_out, gy_out, core_out):
    left = lax.broadcasted_iota(jnp.int32, (64, 128), 1) < 64
    for i, ref in enumerate((gx_out, gy_out)):
        p0, p1, p2 = full[i, 0:64], full[i, 64:128], full[i, 128:192]
        t0 = full[i, 0:128].T
        t2 = jnp.concatenate([p2, p2], axis=0).T
        q1, q2 = pltpu.roll(p1, 64, 1), pltpu.roll(p2, 64, 1)
        ref[0:64, 0:128] = p0
        ref[0:64, 128:192] = p2[:, :64]
        ref[64:128, 0:128] = jnp.where(left, t0[64:128], q1)
        ref[64:128, 128:192] = q1[:, :64]
        ref[128:192, 0:128] = jnp.where(left, t2[0:64], t0[64:128])
        ref[128:192, 128:192] = q2[:, :64]
    odd = lax.rem(lax.axis_index("my"), 2)
    for p in range(HP):
        v = core[p]
        first, gap = (LATE * odd + p, EP) if p < EP else (EARLY * (1 - odd) + p - EP, LP)
        core_out[first] = v[:RANK, :RANK]
        core_out[first + gap] = pltpu.roll(v, 64, 1)[:RANK, :RANK]


def body(slab, basis_x, basis_y):
    anywhere = pl.BlockSpec(memory_space=pl.ANY)
    vmem = pl.BlockSpec(memory_space=pltpu.VMEM)
    full, core = pl.pallas_call(
        kernel,
        out_shape=(
            jax.ShapeDtypeStruct((2, 192, 128), F32),
            jax.ShapeDtypeStruct((HP, 64, 128), F32),
        ),
        in_specs=[anywhere] * 3,
        out_specs=(anywhere, anywhere),
        scratch_shapes=[
            pltpu.VMEM((JB, IB, COLS), F32),
            pltpu.VMEM((4, 4, IB, LANES), F32),
            pltpu.VMEM((4, 4, IB, LANES), F32),
            pltpu.VMEM((4, 4, IB, LANES), F32),
            pltpu.VMEM((4, 4, IB, LANES), F32),
            pltpu.VMEM((2, 4, 4, IB, LANES), F32),
            pltpu.VMEM((4, 2, IB, 128), F32),
            pltpu.VMEM((4, 2, IB, 128), F32),
            pltpu.VMEM((4, 2, IB, 128), F32),
            pltpu.VMEM((4, 2, IB, 128), F32),
            pltpu.VMEM((2, TILES * 128, 128), F32),
            pltpu.VMEM((CHUNKS, 2, HP, 2 * JB, 128), F32),
            pltpu.VMEM((4, 2, HP, 2 * JB, 128), F32),
            pltpu.VMEM((2, RANK, MIDX), F32),
            pltpu.VMEM((128, MIDX), BF16),
            pltpu.VMEM((128, MIDY), BF16),
            pltpu.VMEM((MIDX, MIDX), F32),
            pltpu.VMEM((MIDX, MIDX), F32),
            pltpu.VMEM((MIDY, MIDY), F32),
            pltpu.VMEM((MIDY, MIDY), F32),
            pltpu.VMEM((2, 192, 128), F32),
            pltpu.VMEM((2, 7, 24, 128), F32),
            pltpu.VMEM((2, 24, 128), F32),
            pltpu.VMEM((2, 16, 24, 128), F32),
            pltpu.VMEM((2, 24, 128), F32),
            pltpu.VMEM((HP, 64, 128), F32),
            pltpu.SemaphoreType.DMA((4,)),
            pltpu.SemaphoreType.DMA((2,)),
            pltpu.SemaphoreType.DMA((3,)),
            pltpu.SemaphoreType.DMA((len(PARTS),)),
            pltpu.SemaphoreType.DMA((len(PARTS),)),
            pltpu.SemaphoreType.DMA,
            pltpu.SemaphoreType.DMA((CHUNKS + 1,)),
            pltpu.SemaphoreType.DMA,
            pltpu.SemaphoreType.DMA,
            pltpu.SemaphoreType.DMA((2,)),
            pltpu.SemaphoreType.DMA((2,)),
            pltpu.SemaphoreType.DMA((2,)),
        ],
        compiler_params=pltpu.CompilerParams(
            collective_id=0, has_side_effects=True, vmem_limit_bytes=58 * 2**20
        ),
    )(jnp.transpose(slab, (1, 0, 2)), basis_x.T, basis_y.T)
    gx, gy, core = pl.pallas_call(
        unfold,
        out_shape=(
            jax.ShapeDtypeStruct((MIDX, MIDX), F32),
            jax.ShapeDtypeStruct((MIDY, MIDY), F32),
            jax.ShapeDtypeStruct((OWN, RANK, RANK), F32),
        ),
        in_specs=[vmem, vmem],
        out_specs=(vmem, vmem, vmem),
    )(full, core)
    return gx, gy, jnp.transpose(core, (1, 2, 0))


def solution(mesh):
    return jax.shard_map(
        body,
        mesh=mesh,
        in_specs=(P("mx", "my", None), P(), P()),
        out_specs=(P(), P(), P(None, None, ("mx", "my"))),
        check_vma=False,
    )
```
